32 devices in a mesh: exp: 8 (over y, x, core), hid: 4 (over z).
Axes of the slice: x: 2, y: 2, z: 4, core: 2. Of those that a mesh axis runs over, the one named last changes fastest.
Arguments:
- tokens: bfloat16 [6144, 2048], P(('exp', 'hid')), may hold values from -6 to 6
- segment_ids: int32 [32, 192], P(('exp', 'hid')), may hold values from 0 to 3, never falling along the last dimension, each value on 1 to 96 neighbouring positions
- expert_choice: int32 [6144, 8], P(('exp', 'hid')), may hold values from 0 to 63, all different within a row; in each aligned block of 192 rows (0 to 191, 192 to 383, ...) at most 32 rows name the same one
- w_query: bfloat16 [2048, 2048], P(('exp', 'hid')), may hold values from -0.125 to 0.125
- w_key: bfloat16 [2048, 2048], P(('exp', 'hid')), may hold values from -0.125 to 0.125
- w_value: bfloat16 [2048, 2048], P(('exp', 'hid')), may hold values from -0.125 to 0.125
- w_output: bfloat16 [2048, 2048], P(('exp', 'hid')), may hold values from -0.75 to 0.75
- w_router: bfloat16 [2048, 64], P(('exp', 'hid')), may hold values from -0.0625 to 0.0625
- attn_gain: bfloat16 [2048], P(('exp', 'hid')), may hold values from 0.25 to 1.75
- query_gain: bfloat16 [2048], P(('exp', 'hid')), may hold values from 0.25 to 1.75
- key_gain: bfloat16 [2048], P(('exp', 'hid')), may hold values from 0.25 to 1.75
- ffn_gain: bfloat16 [2048], P(('exp', 'hid')), may hold values from 0.25 to 1.75
- w_gate: bfloat16 [64, 2048, 1024], P('exp', None, 'hid'), may hold values from -0.125 to 0.125
- w_up: bfloat16 [64, 2048, 1024], P('exp', None, 'hid'), may hold values from -0.125 to 0.125
- w_down: bfloat16 [64, 1024, 2048], P('exp', 'hid'), may hold values from -6 to 6
- out_grad: bfloat16 [6144, 2048], P(('exp', 'hid')), may hold values from -6 to 6
Outputs:
- output: bfloat16 [6144, 2048], P(('exp', 'hid'))
- input_grad: float32 [6144, 2048], P(('exp', 'hid'))
- w_query_grad: float32 [2048, 2048], P(('exp', 'hid'))
- w_key_grad: float32 [2048, 2048], P(('exp', 'hid'))
- w_value_grad: float32 [2048, 2048], P(('exp', 'hid'))
- w_output_grad: float32 [2048, 2048], P(('exp', 'hid'))
- w_router_grad: float32 [2048, 64], P(('exp', 'hid'))
- attn_gain_grad: float32 [2048], P(('exp', 'hid'))
- query_gain_grad: float32 [2048], P(('exp', 'hid'))
- key_gain_grad: float32 [2048], P(('exp', 'hid'))
- ffn_gain_grad: float32 [2048], P(('exp', 'hid'))
- w_gate_grad: float32 [64, 2048, 1024], P('exp', None, 'hid')
- w_up_grad: float32 [64, 2048, 1024], P('exp', None, 'hid')
- w_down_grad: float32 [64, 1024, 2048], P('exp', 'hid')
- expert_counts: int32 [32, 64], replicated
The draws below stay inside these ranges and needn't reach their ends.
Inputs may be any that keep to these rules, and one draw needn't show every extreme that they name: `segment_ids`: within a packed row the ids never fall; each id covers 1 to 96 positions, some id exactly that many. `expert_choice`: each row names 8 different experts. Among the 192 rows of one device no expert is named by more than 32 rows, a bound that some block reaches.
All inputs are finite; a program needn't handle non-finite values.
Results may differ from the reference program's by a relative error of at most 0.018.
Values may be sent and summed in bfloat16 or wider, within the bound.
A program may use at most 640 MiB of HBM per device.

```python
import math
import jax
import jax.numpy as jnp
import numpy as np
from jax import lax

D = 2048
HEADS = 16
HEAD_DIM = 128
EXPERTS = 64
TOP = 8
FF = 1024
TOK_DEV = 192
ROWS = 32
TOKENS = 6144
CAP = 32


def steps_of(own_key, shape, pieces, smallest, top_value):
    def one(position, parts):
        heights = jax.random.uniform(jax.random.fold_in(jax.random.fold_in(own_key, 6), position), (parts,), jnp.float32, smallest / len(pieces), top_value / len(pieces))
        return jnp.repeat(jnp.exp(heights), shape[position] // parts).reshape((-1,) + (1,) * (len(shape) - position - 1))

    level = one(*pieces[0])
    for cut in pieces[1:]:
        level = level * one(*cut)
    return level


def length_profile(number_of, total, limit, skew):
    loads = [(1 << 20) // math.isqrt(rank ** skew) + 1 for rank in range(2, number_of + 1)]
    surplus, given = total - limit - (number_of - 1), [1] * (number_of - 1)
    while surplus > 0:
        candidates = [i for i in range(number_of - 1) if given[i] < limit]
        whole, left = sum([loads[i] for i in candidates]), surplus
        for i in candidates:
            more = min(limit - given[i], max(1, left * loads[i] // whole), surplus)
            given[i] = given[i] + more
            surplus = surplus - more
    return np.array([limit] + given)


def uneven(rng, count, total, most, lean):
    if count == 2:
        one = jax.random.randint(rng, (), max(1, total - most), min(most, total - 1) + 1)
        return jnp.stack([one, total - one])
    tallies = jnp.asarray(length_profile(count, total, most, lean), jnp.int32)
    twos = (count - 1) // 2
    source_of, sink = tallies[1:1 + 2 * twos:2], tallies[2:2 + 2 * twos:2]
    margin = jnp.minimum(source_of - 1, most - sink)
    moved = jax.random.randint(jax.random.fold_in(rng, 1), (twos,), 0, 1 << 20) % (margin + 1)
    tallies = tallies.at[1:1 + 2 * twos:2].set(source_of - moved).at[2:2 + 2 * twos:2].set(sink + moved)
    return tallies[jax.random.permutation(jax.random.fold_in(rng, 2), count)]


def routed_block(rng, own, number, rows, amount, top, most, slope):
    sequence = jax.random.permutation(rng, amount)
    crowded, common = portions_of(amount, rows * top, most, slope, True), portions_of(amount, rows * top, most, slope, False)
    places = jnp.arange(amount)

    def named(lengths, rotation):
        used = int((lengths > 0).sum())
        fixed = max(1, used // 4)
        moved = fixed + (places - fixed + rotation * (used - fixed)) % max(1, amount - fixed)
        return jnp.zeros((amount,), jnp.int32).at[sequence[jnp.where(places < fixed, places, moved)]].set(jnp.asarray(lengths, jnp.int32))

    lengths = jnp.where(number % 4 == 0, named(crowded, number // 4), named(common, number - number // 4 - 1))
    mixed = jax.random.permutation(jax.random.fold_in(own, 3), amount)
    giver, taker = mixed[0:amount // 2 * 2:2], mixed[1:amount // 2 * 2:2]
    room = jnp.minimum(lengths[giver] - 1, most - lengths[taker]) // 2
    room = jnp.where((giver == sequence[0]) | (taker == sequence[0]) | (lengths[taker] == 0), 0, jnp.maximum(room, 0))
    moved = jax.random.randint(jax.random.fold_in(own, 4), (amount // 2,), 0, 1 << 20) % (room + 1)
    lengths = lengths.at[giver].add(-moved).at[taker].add(moved)
    labels = jnp.searchsorted(jnp.cumsum(lengths), jnp.arange(rows * top), side="right").astype(jnp.int32)
    listing = labels.reshape(top, rows).T
    listing = listing[jax.random.permutation(jax.random.fold_in(own, 1), rows)]
    rotation = jax.random.randint(jax.random.fold_in(own, 2), (rows, 1), 0, top)
    return jnp.take_along_axis(listing, (jnp.arange(top)[None, :] + rotation) % top, axis=1)


def portions_of(count, total, most, skew, full):
    weights = [(1 << 20) // math.isqrt(standing ** skew) + 1 for standing in range(1, count + 1)]
    largest = most if full else min(most, max(-(-total // count), total * weights[0] // sum(weights)))
    least = 1 if total - largest >= count - 1 else 0
    given, spare = [largest] + [least] * (count - 1), total - largest - least * (count - 1)
    while spare > 0:
        movable = [i for i in range(1, count) if given[i] < largest] or [i for i in range(1, count) if given[i] < most]
        mass, remaining = sum([weights[i] for i in movable]), spare
        for i in movable:
            extra = min(most - given[i], max(1, remaining * weights[i] // mass), spare)
            given[i] = given[i] + extra
            spare = spare - extra
    return np.array(given)


def noise(stream_key, extent, scale, limit, shards=(), kind=jnp.bfloat16):
    values = jax.random.normal(stream_key, extent, jnp.float32) * scale
    if len(shards) > 0:
        values = steps_of(stream_key, extent, shards, -0.22, 0.18) * values
    return jnp.clip(values, min=-limit, max=limit).astype(kind)


def setup_inputs(seed: int = 0) -> dict:
    key_of = jax.random.split(jax.random.key(seed), 17)
    tokens = noise(key_of[0], (TOKENS, D), 1.0, 6.0, ((0, 32),))
    segment_ids = jax.vmap(lambda own: jnp.searchsorted(jnp.cumsum(uneven(own, 4, TOK_DEV, TOK_DEV // 2, 1)), jnp.arange(TOK_DEV), side="right"))(jax.random.split(key_of[1], ROWS)).reshape((ROWS, TOK_DEV)).astype(jnp.int32)
    expert_choice_keys = jax.random.split(jax.random.fold_in(key_of[2], 1), TOKENS // TOK_DEV)
    expert_choice_turns = jax.random.permutation(jax.random.fold_in(key_of[2], 3), TOKENS // TOK_DEV)
    expert_choice = jax.vmap(lambda own, number: routed_block(jax.random.fold_in(key_of[2], 2), own, number, TOK_DEV, EXPERTS, TOP, CAP, 1))(expert_choice_keys, expert_choice_turns).reshape((TOKENS, TOP))
    w_query = noise(key_of[3], (D, D), D ** -0.5, 0.125, ((0, 32),))
    w_key = noise(key_of[4], (D, D), D ** -0.5, 0.125, ((0, 32),))
    w_value = noise(key_of[5], (D, D), D ** -0.5, 0.125, ((0, 32),))
    w_output = noise(key_of[6], (D, D), (D // 32) ** -0.5, 0.75, ((0, 32),))
    w_router = noise(key_of[7], (D, EXPERTS), (4 * D) ** -0.5, 0.0625, ((0, 32),))
    attn_gain = jnp.clip(1.0 + 0.15 * jax.random.normal(key_of[8], (D,), jnp.float32), 0.25, 1.75).astype(jnp.bfloat16)
    query_gain = jnp.clip(1.0 + 0.15 * jax.random.normal(key_of[9], (D,), jnp.float32), 0.25, 1.75).astype(jnp.bfloat16)
    key_gain = jnp.clip(1.0 + 0.15 * jax.random.normal(key_of[10], (D,), jnp.float32), 0.25, 1.75).astype(jnp.bfloat16)
    ffn_gain = jnp.clip(1.0 + 0.15 * jax.random.normal(key_of[11], (D,), jnp.float32), 0.25, 1.75).astype(jnp.bfloat16)
    w_gate = noise(key_of[12], (EXPERTS, D, FF), D ** -0.5, 0.125, ((0, 8), (2, 4)))
    w_up = noise(key_of[13], (EXPERTS, D, FF), D ** -0.5, 0.125, ((0, 8), (2, 4)))
    w_down = noise(key_of[14], (EXPERTS, FF, D), 1 ** -0.5, 6.0, ((0, 8), (1, 4)))
    out_grad = noise(key_of[15], (TOKENS, D), 1.0, 6.0, ((0, 32),))
    return {"tokens": tokens, "segment_ids": segment_ids, "expert_choice": expert_choice, "w_query": w_query, "w_key": w_key, "w_value": w_value, "w_output": w_output, "w_router": w_router, "attn_gain": attn_gain, "query_gain": query_gain, "key_gain": key_gain, "ffn_gain": ffn_gain, "w_gate": w_gate, "w_up": w_up, "w_down": w_down, "out_grad": out_grad}


epsilon = 1e-05
base_freq = 10000.0
masked_value = -1e+30
highest = lax.Precision.HIGHEST

@jax.custom_vjp
def low(v):
    return lax.optimization_barrier(v.astype(jnp.bfloat16)).astype(jnp.float32)

@jax.custom_vjp
def low_back(v):
    return v

def low_keep(v):
    return (low(v), None)

def low_pass(kept, grad):
    return (grad,)

def back_keep(v):
    return (v, None)

def back_low(kept, grad):
    return (low(grad),)
low.defvjp(low_keep, low_pass)
low_back.defvjp(back_keep, back_low)

def matmul(left, right):
    return jnp.dot(left, right, precision=highest, preferred_element_type=jnp.float32)

def normalize(values):
    return values * lax.rsqrt(lax.optimization_barrier(jnp.mean(values * values, axis=-1, keepdims=True)) + epsilon)

def rotary_tables():
    positions = jnp.arange(TOK_DEV).astype(jnp.float32)
    freqs = base_freq ** (-jnp.arange(HEAD_DIM // 2).astype(jnp.float32) * 2.0 / HEAD_DIM)
    angles = positions[:, None] * freqs[None, :]
    return (jnp.cos(angles)[:, None, :], jnp.sin(angles)[:, None, :])

def rotate(values, cosine_table, sine_table):
    half_dim = values.shape[-1] // 2
    first = values[..., :half_dim]
    second = values[..., half_dim:]
    return jnp.concatenate([first * cosine_table - second * sine_table, second * cosine_table + first * sine_table], axis=-1)

def attend_row(step_items):
    query_row, key_row, value_row, segment_row = step_items
    scores = jnp.einsum('qhd,khd->hqk', query_row, key_row, precision=highest) * HEAD_DIM ** (-0.5)
    scores = low_back(scores)
    positions = jnp.arange(TOK_DEV).astype(jnp.int32)
    allowed = (positions[:, None] >= positions[None, :]) & (segment_row[:, None] == segment_row[None, :])
    scores = jnp.where(allowed[None], scores, masked_value)
    attn_probs = jax.nn.softmax(scores, axis=-1)
    return jnp.einsum('hqk,khd->qhd', low(attn_probs), value_row, precision=highest)

def build_slots(expert_choice):
    flat_choice = expert_choice.reshape(ROWS, TOK_DEV * TOP).astype(jnp.int32)
    flat_hot = (flat_choice[:, :, None] == jnp.arange(EXPERTS).astype(jnp.int32)[None, None, :]).astype(jnp.int32)
    slot_ranks = (lax.optimization_barrier(jnp.sum(jnp.cumsum(flat_hot, axis=1, dtype=jnp.int32) * flat_hot, axis=2, dtype=jnp.int32)) - 1).astype(jnp.int32)
    row_index = jnp.broadcast_to(jnp.arange(ROWS).astype(jnp.int32)[:, None], flat_choice.shape)
    assigned = jnp.arange(ROWS * TOK_DEV * TOP).astype(jnp.int32).reshape(ROWS, TOK_DEV * TOP)
    empty_pick = jnp.int32(ROWS * TOK_DEV * TOP)
    slot_map = jnp.full((EXPERTS, ROWS, CAP), empty_pick, jnp.int32).at[flat_choice, row_index, slot_ranks].set(assigned)
    counts = lax.optimization_barrier(jnp.sum(flat_hot, axis=1, dtype=jnp.int32)).astype(jnp.int32)
    return (slot_map.reshape(EXPERTS, ROWS * CAP), counts)

def expert_pass(padded_rows, padded_gates, gate_weight, up_weight, down_weight, slot_picks):
    token_rows = (slot_picks // TOP).astype(jnp.int32)
    expert_in = low_back(padded_rows[token_rows])
    gate_act = low_back(matmul(expert_in, gate_weight))
    up_act = low_back(matmul(expert_in, up_weight))
    hidden = low(jax.nn.silu(gate_act) * up_act)
    produced = low_back(low(matmul(hidden, down_weight)))
    weighted = padded_gates[slot_picks][:, None] * produced
    return jnp.zeros((TOKENS + 1, D), jnp.float32).at[token_rows].add(weighted)[:TOKENS]

def reference(tokens, segment_ids, expert_choice, w_query, w_key, w_value, w_output, w_router, attn_gain, query_gain, key_gain, ffn_gain, w_gate, w_up, w_down, out_grad):
    slot_map, counts = build_slots(expert_choice)
    cosine_table, sine_table = rotary_tables()
    four_shape = (ROWS, TOK_DEV, HEADS, HEAD_DIM)

    def forward(inputs, query_weight, key_weight, value_weight, output_weight, router_weight, gain_attn, gain_query, gain_key, gain_ffn, gate_weight, up_weight, down_weight):
        normed_a = low(normalize(inputs) * gain_attn)
        query_raw = low_back(matmul(normed_a, query_weight))
        key_raw = low_back(matmul(normed_a, key_weight))
        value_low = low_back(low(matmul(normed_a, value_weight)))
        query_low = low(rotate((normalize(query_raw) * gain_query).reshape(four_shape), cosine_table, sine_table))
        key_low = low(rotate((normalize(key_raw) * gain_key).reshape(four_shape), cosine_table, sine_table))
        attended = lax.map(jax.checkpoint(attend_row), (query_low, key_low, value_low.reshape(four_shape), segment_ids))
        attended_low = low_back(low(attended.reshape(TOKENS, D)))
        residual = inputs + low_back(matmul(attended_low, output_weight))
        normed_f = low(normalize(residual) * gain_ffn)
        router_probs = jax.nn.softmax(low_back(matmul(normed_f, router_weight)), axis=-1)
        gate_weights = jnp.take_along_axis(router_probs, expert_choice, axis=1).reshape(TOKENS * TOP)
        padded_gates = jnp.concatenate([gate_weights, jnp.zeros((1,), jnp.float32)])
        padded_rows = jnp.concatenate([normed_f, jnp.zeros((1, D), jnp.float32)], axis=0)
        checked = jax.checkpoint(expert_pass)

        def accumulate(running, step_items):
            gate_one, up_one, down_one, slot_picks = step_items
            return (running + checked(padded_rows, padded_gates, gate_one, up_one, down_one, slot_picks), None)
        mixture, unused = lax.scan(accumulate, jnp.zeros((TOKENS, D), jnp.float32), (gate_weight, up_weight, down_weight, slot_map))
        return residual + mixture
    output, pullback = jax.vjp(forward, tokens.astype(jnp.float32), w_query.astype(jnp.float32), w_key.astype(jnp.float32), w_value.astype(jnp.float32), w_output.astype(jnp.float32), w_router.astype(jnp.float32), attn_gain.astype(jnp.float32), query_gain.astype(jnp.float32), key_gain.astype(jnp.float32), ffn_gain.astype(jnp.float32), w_gate.astype(jnp.float32), w_up.astype(jnp.float32), w_down.astype(jnp.float32))
    gradients = pullback(out_grad.astype(jnp.float32))
    return (output.astype(jnp.bfloat16), gradients[0], gradients[1], gradients[2], gradients[3], gradients[4], gradients[5], gradients[6], gradients[7], gradients[8], gradients[9], gradients[10], gradients[11], gradients[12], counts)
```

```python
import functools
import math

import jax
import jax.numpy as jnp
from jax import lax
from jax.experimental import pallas as pl
from jax.experimental.pallas import tpu as pltpu
from jax.sharding import PartitionSpec as P

MESH = pl.DeviceIdType.MESH


def grid_of(exp, hid):
    plane = exp // 2
    na = 1 << (int(math.log2(plane)) // 2)
    return na, plane // na, hid


class Place:
    def __init__(self, shape):
        self.na, self.nb, self.nz = shape
        e = lax.axis_index("exp")
        self.z = lax.axis_index("hid")
        self.c = e % 2
        self.b = (e // 2) % self.nb
        self.a = e // (2 * self.nb)

    def ident(self, a=None, b=None, c=None, z=None):
        a = self.a if a is None else a
        b = self.b if b is None else b
        c = self.c if c is None else c
        z = self.z if z is None else z
        return ((a * self.nb + b) * 2 + c, z)

    def linear(self, **kw):
        e, z = self.ident(**kw)
        return e * self.nz + z


def xor(value, k):
    out = value
    bit = 1
    while bit <= k:
        if k & bit:
            has = (out // bit) % 2
            out = out + bit - 2 * bit * has
        bit *= 2
    return out


def greet(p):
    barrier = pltpu.get_barrier_semaphore()
    n = 0
    for k in range(1, p.nz):
        pl.semaphore_signal(barrier, inc=1, device_id=p.ident(z=xor(p.z, k)), device_id_type=MESH)
        n += 1
    for k in range(1, p.na):
        pl.semaphore_signal(barrier, inc=1, device_id=p.ident(a=xor(p.a, k)), device_id_type=MESH)
        n += 1
    for k in range(1, p.nb):
        pl.semaphore_signal(barrier, inc=1, device_id=p.ident(b=xor(p.b, k)), device_id_type=MESH)
        n += 1
    pl.semaphore_signal(barrier, inc=1, device_id=p.ident(c=1 - p.c), device_id_type=MESH)
    n += 1
    pl.semaphore_wait(barrier, n)


def ag_count(shape):
    na, nb, nz = shape
    return (nz - 1) + nz * (na - 1) + nz * (nb - 1) + nz * na * (nb - 1) + nz * nb * (na - 1) + na * nb * nz


class Gather:
    def __init__(self, p, x, o, send, recv, local, base=0):
        self.p, self.x, self.o, self.send, self.recv, self.local = p, x, o, send, recv, local
        rows = x.shape[0]
        cut = rows // 32 * 16
        self.halves = ((0, cut), (cut, rows - cut))
        na, nb, nz = p.na, p.nb, p.nz
        i = base
        self.iz = i; i += nz - 1
        self.i1a = i; i += nz * (na - 1)
        self.i1b = i; i += nz * (nb - 1)
        self.i2b = i; i += nz * na * (nb - 1)
        self.i2a = i; i += nz * nb * (na - 1)
        self.isib = i; i += na * nb * nz
        self.end = i

    def copy(self, src, dst, i, target):
        return pltpu.make_async_remote_copy(src_ref=src, dst_ref=dst, send_sem=self.send.at[i], recv_sem=self.recv.at[i], device_id=target, device_id_type=MESH)

    def part(self, d, h):
        s, n = self.halves[h]
        return self.o.at[d, pl.ds(s, n)]

    def src(self, d, h, own):
        s, n = self.halves[h]
        return self.x.at[pl.ds(s, n)] if own else self.o.at[d, pl.ds(s, n)]

    def m_z(self, k):
        p = self.p
        d = p.linear()
        return self.copy(self.x, self.o.at[d], self.iz + k - 1, p.ident(z=xor(p.z, k)))

    def r_z(self, k):
        p = self.p
        d = p.linear(z=xor(p.z, k))
        return self.copy(self.o.at[d], self.o.at[d], self.iz + k - 1, p.ident(z=xor(p.z, k)))

    def m_1(self, axis, k, j):
        p = self.p
        n = p.na if axis == "a" else p.nb
        base = self.i1a if axis == "a" else self.i1b
        h = 0 if axis == "a" else 1
        d = p.linear(z=xor(p.z, k))
        t = p.ident(**{axis: xor(getattr(p, axis), j)})
        return self.copy(self.src(d, h, k == 0), self.part(d, h), base + k * (n - 1) + j - 1, t)

    def r_1(self, axis, k, j):
        p = self.p
        n = p.na if axis == "a" else p.nb
        base = self.i1a if axis == "a" else self.i1b
        h = 0 if axis == "a" else 1
        d = p.linear(z=xor(p.z, k), **{axis: xor(getattr(p, axis), j)})
        return self.copy(self.part(d, h), self.part(d, h), base + k * (n - 1) + j - 1, p.ident(**{axis: xor(getattr(p, axis), j)}))

    def m_2(self, axis, k, i, j):
        p = self.p
        other = "b" if axis == "a" else "a"
        n = p.na if axis == "a" else p.nb
        m = p.nb if axis == "a" else p.na
        base = self.i2a if axis == "a" else self.i2b
        h = 1 if axis == "a" else 0
        d = p.linear(z=xor(p.z, k), **{other: xor(getattr(p, other), i)})
        t = p.ident(**{axis: xor(getattr(p, axis), j)})
        return self.copy(self.src(d, h, k == 0 and i == 0), self.part(d, h), base + (k * m + i) * (n - 1) + j - 1, t)

    def r_2(self, axis, k, i, j):
        p = self.p
        other = "b" if axis == "a" else "a"
        n = p.na if axis == "a" else p.nb
        m = p.nb if axis == "a" else p.na
        base = self.i2a if axis == "a" else self.i2b
        h = 1 if axis == "a" else 0
        d = p.linear(z=xor(p.z, k), **{other: xor(getattr(p, other), i), axis: xor(getattr(p, axis), j)})
        t = p.ident(**{axis: xor(getattr(p, axis), j)})
        return self.copy(self.part(d, h), self.part(d, h), base + (k * m + i) * (n - 1) + j - 1, t)

    def m_s(self, k, i, j):
        p = self.p
        d = p.linear(z=xor(p.z, k), a=xor(p.a, i), b=xor(p.b, j))
        own = k == 0 and i == 0 and j == 0
        return self.copy(self.x if own else self.o.at[d], self.o.at[d], self.isib + (k * p.na + i) * p.nb + j, p.ident(c=1 - p.c))

    def r_s(self, k, i, j):
        p = self.p
        d = p.linear(z=xor(p.z, k), a=xor(p.a, i), b=xor(p.b, j), c=1 - p.c)
        return self.copy(self.o.at[d], self.o.at[d], self.isib + (k * p.na + i) * p.nb + j, p.ident(c=1 - p.c))

    def own(self):
        return pltpu.make_async_copy(self.x, self.o.at[self.p.linear()], self.local)

    def start(self):
        p = self.p
        self.own().start()
        for k in range(1, p.nz):
            self.m_z(k).start()
        self.spread(0)

    def spread(self, k):
        p = self.p
        for j in range(1, p.na):
            self.m_1("a", k, j).start()
        for j in range(1, p.nb):
            self.m_1("b", k, j).start()
        for j in range(1, p.nb):
            self.m_2("b", k, 0, j).start()
        for j in range(1, p.na):
            self.m_2("a", k, 0, j).start()
        self.m_s(k, 0, 0).start()

    def turn(self, k):
        p = self.p
        for i in range(1, p.na):
            self.r_1("a", k, i).wait_recv()
            for j in range(1, p.nb):
                self.m_2("b", k, i, j).start()
        for i in range(1, p.nb):
            self.r_1("b", k, i).wait_recv()
            for j in range(1, p.na):
                self.m_2("a", k, i, j).start()

    def close(self, k):
        p = self.p
        for i in range(p.na):
            for j in range(1, p.nb):
                self.r_2("b", k, i, j).wait_recv()
        for i in range(p.nb):
            for j in range(1, p.na):
                self.r_2("a", k, i, j).wait_recv()
        for i in range(p.na):
            for j in range(p.nb):
                if i or j:
                    self.m_s(k, i, j).start()

    def arrive(self, k):
        self.r_z(k).wait_recv()
        self.spread(k)

    def middle(self):
        p = self.p
        for k in range(1, p.nz):
            self.arrive(k)
            self.turn(k - 1)
        self.turn(p.nz - 1)
        for k in range(p.nz):
            self.close(k)

    def finish(self):
        p = self.p
        self.own().wait()
        for k in range(p.nz):
            for i in range(p.na):
                for j in range(p.nb):
                    self.r_s(k, i, j).wait_recv()
                    self.m_s(k, i, j).wait_send()
        for k in range(1, p.nz):
            self.m_z(k).wait_send()
        for k in range(p.nz):
            for j in range(1, p.na):
                self.m_1("a", k, j).wait_send()
                for i in range(p.nb):
                    self.m_2("a", k, i, j).wait_send()
            for j in range(1, p.nb):
                self.m_1("b", k, j).wait_send()
                for i in range(p.na):
                    self.m_2("b", k, i, j).wait_send()


def gather_kernel(shape, n, *refs):
    xs, os = refs[:n], refs[n:2 * n]
    send, recv, local = refs[2 * n:]
    p = Place(shape)
    greet(p)
    gs, base = [], 0
    for i in range(n):
        g = Gather(p, xs[i], os[i], send, recv, local.at[i], base)
        base = g.end
        gs.append(g)
    for g in gs:
        g.start()
    for k in range(1, p.nz):
        for g in gs:
            g.arrive(k)
            g.turn(k - 1)
    for g in gs:
        g.turn(p.nz - 1)
    for k in range(p.nz):
        for g in gs:
            g.close(k)
    for g in gs:
        g.finish()


def all_gather(shape, xs, collective_id):
    na, nb, nz = shape
    nd = na * nb * nz * 2
    n = len(xs)
    count = ag_count(shape) * n
    any_ = pl.BlockSpec(memory_space=pl.ANY)
    return pl.pallas_call(
        functools.partial(gather_kernel, shape, n),
        out_shape=[jax.ShapeDtypeStruct((nd,) + x.shape, x.dtype) for x in xs],
        in_specs=[any_] * n,
        out_specs=[any_] * n,
        scratch_shapes=[pltpu.SemaphoreType.DMA((count,)), pltpu.SemaphoreType.DMA((count,)), pltpu.SemaphoreType.DMA((n,))],
        compiler_params=pltpu.CompilerParams(collective_id=collective_id, has_side_effects=True),
    )(*xs)

OUTS = 12


def rs_layout(shape, rows):
    na, nb, nz = shape
    cut = rows // 32 * 16
    s0, s1 = cut, rows - cut
    counts = [na * nb * nz, (nb - 1) * na * nz, (na - 1) * nb * nz, (na - 1) * nz, (nb - 1) * nz, 2 * (nz - 1)]
    buffers = [
        (na, nb, nz, rows),
        (nb - 1, na, nz, s0),
        (na - 1, nb, nz, s1),
        (na - 1, nz, s0),
        (nb - 1, nz, s1),
        (nz - 1, rows),
    ]
    return counts, buffers


class Scatter:
    def __init__(self, p, v, out, buffers, send, recv, base=0):
        self.p, self.v, self.out, self.send, self.recv = p, v, out, send, recv
        self.r1, self.r2b, self.r2a, self.r3a, self.r3b, self.r4 = buffers
        rows = v.shape[4]
        cut = rows // 32 * 16
        self.halves = ((0, cut), (cut, rows - cut))
        counts, _ = rs_layout((p.na, p.nb, p.nz), rows)
        self.starts = []
        for n in counts:
            self.starts.append(base)
            base += n
        self.end = base
        self.waited = set()

    def copy(self, src, dst, i, target):
        return pltpu.make_async_remote_copy(src_ref=src, dst_ref=dst, send_sem=self.send.at[i], recv_sem=self.recv.at[i], device_id=target, device_id_type=MESH)

    def block(self, i, j, k, other=False):
        p = self.p
        c = 1 - p.c if other else p.c
        return self.v.at[xor(p.a, i), xor(p.b, j), c, xor(p.z, k)]

    def half(self, ref, h):
        s, n = self.halves[h]
        return ref.at[pl.ds(s, n)]

    def sibling(self, i, j, k):
        p = self.p
        n = self.starts[0] + (i * p.nb + j) * p.nz + k
        return self.copy(self.block(i, j, k, True), self.r1.at[i, j, k], n, p.ident(c=1 - p.c))

    def arrived(self, key, ref, i):
        if key in self.waited:
            return None
        self.waited.add(key)
        p = self.p
        return self.copy(ref, ref, i, p.ident(c=1 - p.c))

    def base_inputs(self, i, j, k, h):
        p = self.p
        n = self.starts[0] + (i * p.nb + j) * p.nz + k
        r = self.r1.at[i, j, k]
        return [(self.half(self.block(i, j, k), h), None), (self.half(r, h), self.arrived((1, i, j, k), r, n))]

    def two(self, h, far, near, k):
        p = self.p
        if h == 0:
            r, n = self.r2b.at[far - 1, near, k], self.starts[1] + ((far - 1) * p.na + near) * p.nz + k
        else:
            r, n = self.r2a.at[far - 1, near, k], self.starts[2] + ((far - 1) * p.nb + near) * p.nz + k
        return r, n

    def three(self, h, far, k):
        p = self.p
        if h == 0:
            return self.r3a.at[far - 1, k], self.starts[3] + (far - 1) * p.nz + k
        return self.r3b.at[far - 1, k], self.starts[4] + (far - 1) * p.nz + k

    def four(self, h, k):
        return self.half(self.r4.at[k - 1], h), self.starts[5] + 2 * (k - 1) + h

    def stage2(self, k):
        p, jobs = self.p, []
        for far, near in [(f, n) for n in range(max(p.na, p.nb)) for f in range(1, max(p.na, p.nb))]:
            if far < p.nb and near < p.na:
                r, n = self.two(0, far, near, k)
                jobs.append((self.base_inputs(near, far, k, 0), (r, n, p.ident(b=xor(p.b, far)))))
            if far < p.na and near < p.nb:
                r, n = self.two(1, far, near, k)
                jobs.append((self.base_inputs(far, near, k, 1), (r, n, p.ident(a=xor(p.a, far)))))
        return jobs

    def with_two(self, h, near, k):
        p = self.p
        i, j = (near, 0) if h == 0 else (0, near)
        got = self.base_inputs(i, j, k, h)
        for far in range(1, p.nb if h == 0 else p.na):
            r, n = self.two(h, far, near, k)
            got.append((r, self.arrived((2, h, far, near, k), r, n)))
        return got

    def stage3(self, k):
        p, jobs = self.p, []
        for near in range(1, max(p.na, p.nb)):
            if near < p.na:
                r, n = self.three(0, near, k)
                jobs.append((self.with_two(0, near, k), (r, n, p.ident(a=xor(p.a, near)))))
            if near < p.nb:
                r, n = self.three(1, near, k)
                jobs.append((self.with_two(1, near, k), (r, n, p.ident(b=xor(p.b, near)))))
        return jobs

    def with_three(self, h, k):
        p = self.p
        got = self.with_two(h, 0, k)
        for far in range(1, p.na if h == 0 else p.nb):
            r, n = self.three(h, far, k)
            got.append((r, self.arrived((3, h, far, k), r, n)))
        return got

    def stage4(self, k):
        p, jobs = self.p, []
        for h in range(2):
            got = self.with_three(h, k)
            if k:
                r, n = self.four(h, k)
                jobs.append((got, (r, n, p.ident(z=xor(p.z, k)))))
            else:
                for far in range(1, p.nz):
                    r, n = self.four(h, far)
                    got.append((r, self.arrived((4, h, far), r, n)))
                jobs.append((got, self.half(self.out, h)))
        return jobs

    def start(self):
        p = self.p
        for k in reversed(range(p.nz)):
            for i in reversed(range(p.na)):
                for j in reversed(range(p.nb)):
                    self.sibling(i, j, k).start()

    def finish(self):
        p = self.p
        for k in range(p.nz):
            for i in range(p.na):
                for j in range(p.nb):
                    self.sibling(i, j, k).wait_send()


class Worker:
    def __init__(self, inbuf, outbuf, finbuf, load, sent, fin, send, recv):
        self.inbuf, self.outbuf, self.finbuf = inbuf, outbuf, finbuf
        self.load, self.fin, self.send, self.recv = load, fin, send, recv
        self.jobs, self.loaded, self.ran = [], 0, 0
        self.out_use = [None] * OUTS
        self.fin_use = [None] * 2
        self.n_out, self.n_fin = 0, 0

    def add(self, jobs):
        self.jobs.extend(jobs)

    def fetch(self, j):
        inputs, _ = self.jobs[j]
        slot = j % 2
        for n, (ref, arrived) in enumerate(inputs):
            if arrived is not None:
                arrived.wait_recv()
            self.loading(j, n).start()

    def loading(self, j, n):
        ref, _ = self.jobs[j][0][n]
        slot = j % 2
        return pltpu.make_async_copy(
            ref, self.inbuf.at[slot, n, pl.ds(0, ref.shape[0])], self.load.at[slot, n]
        )

    def run(self, j):
        inputs, out = self.jobs[j]
        slot = j % 2
        rows = inputs[0][0].shape[0]
        for n in range(len(inputs)):
            self.loading(j, n).wait()
        final = not isinstance(out, tuple)
        if final:
            s = self.n_fin % 2
            self.n_fin += 1
            if self.fin_use[s] is not None:
                self.fin_use[s].wait()
            target = self.finbuf
        else:
            s = self.n_out % OUTS
            self.n_out += 1
            if self.out_use[s] is not None:
                self.out_use[s].wait_send()
            target = self.outbuf
        count = len(inputs)

        def body(t, carry):
            at = pl.ds(pl.multiple_of(t * 16, 16), 16)
            acc = self.inbuf[slot, 0, at].astype(jnp.float32)
            for n in range(1, count):
                acc = acc + self.inbuf[slot, n, at].astype(jnp.float32)
            target[s, at] = acc.astype(target.dtype)
            return carry

        lax.fori_loop(0, rows // 16, body, 0)
        src = target.at[s, pl.ds(0, rows)]
        if final:
            c = pltpu.make_async_copy(src, out, self.fin.at[s])
            self.fin_use[s] = c
        else:
            r, n, where = out
            c = pltpu.make_async_remote_copy(src_ref=src, dst_ref=r, send_sem=self.send.at[n], recv_sem=self.recv.at[n], device_id=where, device_id_type=MESH)
            self.out_use[s] = c
        c.start()

    def drain(self):
        for j in range(self.ran, len(self.jobs)):
            if self.loaded <= j:
                self.fetch(j)
                self.loaded = j + 1
            if j + 1 < len(self.jobs):
                self.fetch(j + 1)
                self.loaded = j + 2
            self.run(j)
            self.ran = j + 1

    def finish(self):
        for c in self.out_use:
            if c is not None:
                c.wait_send()
        for c in self.fin_use:
            if c is not None:
                c.wait()


def scatter_kernel(shape, n, *refs):
    vs, outs = refs[:n], refs[n:2 * n]
    bufs = refs[2 * n:8 * n]
    inbuf, outbuf, finbuf, load, fin, send, recv = refs[8 * n:]
    p = Place(shape)
    greet(p)
    scs, base = [], 0
    for i in range(n):
        s = Scatter(p, vs[i], outs[i], bufs[6 * i:6 * i + 6], send, recv, base)
        base = s.end
        scs.append(s)
    w = Worker(inbuf, outbuf, finbuf, load, None, fin, send, recv)
    steps = [(s, k) for s in scs for k in reversed(range(p.nz))]
    for s in scs:
        s.start()
    for t in range(len(steps) + 2):
        if t < len(steps):
            s, k = steps[t]
            w.add(s.stage2(k))
        if 1 <= t <= len(steps):
            s, k = steps[t - 1]
            w.add(s.stage3(k))
        if 2 <= t:
            s, k = steps[t - 2]
            w.add(s.stage4(k))
    w.drain()
    w.finish()
    for s in scs:
        s.finish()


def reduce_scatter(shape, vs, collective_id):
    na, nb, nz = shape
    n = len(vs)
    any_ = pl.BlockSpec(memory_space=pl.ANY)
    vs = [v.reshape((na, nb, 2, nz) + v.shape[1:]) for v in vs]
    outs, bufs, total = [], [], 0
    rows = max(v.shape[4] for v in vs)
    width = vs[0].shape[5]
    for v in vs:
        counts, buffers = rs_layout(shape, v.shape[4])
        total += sum(counts)
        outs.append(jax.ShapeDtypeStruct(v.shape[4:], jnp.float32))
        bufs += [jax.ShapeDtypeStruct(b + (width,), v.dtype) for b in buffers]
    cut = rows - rows // 32 * 16
    inputs = na + nb + nz - 1
    got = pl.pallas_call(
        functools.partial(scatter_kernel, shape, n),
        out_shape=outs + bufs,
        in_specs=[any_] * n,
        out_specs=[any_] * (7 * n),
        scratch_shapes=[
            pltpu.VMEM((2, inputs, cut, width), jnp.bfloat16),
            pltpu.VMEM((OUTS, cut, width), jnp.bfloat16),
            pltpu.VMEM((2, cut, width), jnp.float32),
            pltpu.SemaphoreType.DMA((2, inputs)),
            pltpu.SemaphoreType.DMA((2,)),
            pltpu.SemaphoreType.DMA((total,)),
            pltpu.SemaphoreType.DMA((total,)),
        ],
        compiler_params=pltpu.CompilerParams(collective_id=collective_id, has_side_effects=True, vmem_limit_bytes=56 << 20),
    )(*vs)
    return got[:n]

HEADS = 16
HEAD_DIM = 128
EXPERTS = 64
TOP = 8
CAP = 32

epsilon = 1e-05
base_freq = 10000.0
masked_value = -1e30
low = jnp.bfloat16
wide = jnp.float32


def normalize(values):
    factor = lax.rsqrt(jnp.mean(values * values, axis=-1, keepdims=True) + epsilon)
    return (values * factor, factor)


def norm_back(grad_normed, unit_values, factor):
    return factor * (
        grad_normed - unit_values * jnp.mean(grad_normed * unit_values, axis=-1, keepdims=True)
    )


def rotary(length, head_width):
    positions = jnp.arange(length, dtype=jnp.float32)
    freqs = base_freq ** (-jnp.arange(head_width // 2, dtype=jnp.float32) * 2.0 / head_width)
    angles = positions[:, None] * freqs[None, :]
    return (jnp.cos(angles)[:, None, :], jnp.sin(angles)[:, None, :])


def rotate(values, cosine_table, sine_table):
    half_dim = values.shape[-1] // 2
    first = values[..., :half_dim]
    second = values[..., half_dim:]
    return jnp.concatenate(
        [first * cosine_table - second * sine_table, second * cosine_table + first * sine_table],
        axis=-1,
    )


def unrotate(grads_in, cosine_table, sine_table):
    half_dim = grads_in.shape[-1] // 2
    first = grads_in[..., :half_dim]
    second = grads_in[..., half_dim:]
    return jnp.concatenate(
        [first * cosine_table + second * sine_table, second * cosine_table - first * sine_table],
        axis=-1,
    )


def dot(left, right, kind=wide):
    return jnp.dot(left, right, preferred_element_type=kind)


def tdot(left, right, kind=wide):
    return lax.dot_general(left, right, (((0,), (0,)), ((), ())), preferred_element_type=kind)


def rdot(left, right):
    return lax.dot_general(left, right, (((1,), (1,)), ((), ())), preferred_element_type=wide)


def ein(form, *values):
    return jnp.einsum(form, *values, preferred_element_type=wide)


def in_parts(step, shape, arrays, axis, collective_id):
    sizes = [a.shape[axis] for a in arrays]
    if min(sizes) >= 32:
        return step(shape, arrays, collective_id)
    whole = step(shape, [jnp.concatenate(arrays, axis=axis)], collective_id)[0]
    ends = [sum(sizes[: i + 1]) for i in range(len(sizes) - 1)]
    return jnp.split(whole, ends, axis=1 - axis)


def experts_part(x_all, g_all, choices, router, w_gate, w_up, w_down):
    rows, length, width = x_all.shape
    local = w_gate.shape[0]
    first = lax.axis_index("exp") * local
    mine = first + jnp.arange(local)
    chosen = jnp.any(choices[:, :, :, None] == mine, axis=2)
    order = jnp.arange(length)
    before = (order[:, None] > order[None, :]).astype(low)
    ranks = ein("ut,rtj->ruj", before, chosen.astype(low)).astype(jnp.int32)
    place = jnp.where(chosen, ranks, -1).transpose(0, 2, 1)
    hot = place[:, :, None, :] == jnp.arange(CAP)[None, None, :, None]
    hot_low = hot.astype(low)
    logits = ein("rtd,de->rte", x_all, router)
    probs = jax.nn.softmax(logits, axis=-1)
    probs = lax.dynamic_slice_in_dim(probs, first, local, 2).transpose(0, 2, 1)
    gates = jnp.sum(jnp.where(hot, probs[:, :, None, :], 0.0), axis=3).transpose(1, 0, 2)
    gates = gates.reshape(local, rows * CAP, 1)
    xs = ein("rjst,rtd->jrsd", hot_low, x_all).astype(low).reshape(local, rows * CAP, width)
    gs = ein("rjst,rtd->jrsd", hot_low, g_all).astype(low).reshape(local, rows * CAP, width)
    gate_act = ein("jnd,jdf->jnf", xs, w_gate)
    up_act = ein("jnd,jdf->jnf", xs, w_up)
    back = ein("jnd,jfd->jnf", gs, w_down)
    sig = jax.nn.sigmoid(gate_act)
    silu = gate_act * sig
    hidden = silu * up_act
    slot_pg = jnp.sum(hidden * back, axis=-1).reshape(local, rows, CAP)
    scaled = (hidden * gates).astype(low)
    grad_hidden = back * gates
    grad_up = (grad_hidden * silu).astype(low)
    grad_gate = (grad_hidden * up_act * sig * (1.0 + gate_act * (1.0 - sig))).astype(low)
    y = ein("jnf,jfd->jnd", scaled, w_down).astype(low)
    dx = (ein("jnf,jdf->jnd", grad_gate, w_gate) + ein("jnf,jdf->jnd", grad_up, w_up)).astype(low)
    y = ein("rjst,jrsd->rtd", hot_low, y.reshape(local, rows, CAP, width)).astype(low)
    dx = ein("rjst,jrsd->rtd", hot_low, dx.reshape(local, rows, CAP, width)).astype(low)
    pg = jnp.sum(jnp.where(hot, slot_pg.transpose(1, 0, 2)[:, :, :, None], 0.0), axis=2)
    pg = pg.transpose(0, 2, 1)
    whole = jnp.zeros((rows, length, EXPERTS), wide)
    pg = lax.dynamic_update_slice_in_dim(whole, pg, first, 2)
    grad_wgate = ein("jnd,jnf->jdf", xs, grad_gate)
    grad_wup = ein("jnd,jnf->jdf", xs, grad_up)
    grad_wdown = ein("jnf,jnd->jfd", scaled, gs)
    return y, dx, pg, grad_wgate, grad_wup, grad_wdown


def on_device(
    shape,
    tokens,
    segment_ids,
    expert_choice,
    w_query,
    w_key,
    w_value,
    w_output,
    w_router,
    attn_gain,
    query_gain,
    key_gain,
    ffn_gain,
    w_gate,
    w_up,
    w_down,
    out_grad,
):
    length, width = tokens.shape
    part = w_query.shape[0]
    devices = width // part

    def rows_of(values):
        flat = values.reshape(-1).astype(low)
        return jnp.pad(flat, (0, -flat.shape[0] % width)).reshape(-1, width)

    small = [w_router, jnp.concatenate([attn_gain, query_gain, key_gain, ffn_gain]), expert_choice]
    small = [rows_of(s) for s in small]
    sizes = [s.shape[0] for s in small]
    small = jnp.concatenate(small)
    small = jnp.pad(small, ((0, 16 - small.shape[0]), (0, 0)))
    gathered = in_parts(
        all_gather, shape, [w_query, w_key, w_value, jnp.concatenate([w_output, small])], 0, 1
    )
    full_query, full_key, full_value = (g.reshape(width, width) for g in gathered[:3])
    full_output = gathered[3][:, :part].reshape(width, width)
    small = gathered[3][:, part:]
    full_router = small[:, : sizes[0]].reshape(devices, -1)[:, : part * EXPERTS]
    full_router = full_router.reshape(width, EXPERTS)
    gains = small[:, sizes[0], : 4 * part].reshape(devices, 4, part).transpose(1, 0, 2)
    gain_attn, gain_query, gain_key, gain_ffn = gains.reshape(4, width).astype(wide)
    choices = small[:, sizes[0] + 1].reshape(devices, -1)[:, : length * TOP]
    choices = choices.reshape(devices, length, TOP).astype(jnp.int32)
    total_counts = jnp.sum(
        (choices.reshape(devices, -1)[:, :, None] == jnp.arange(EXPERTS)).astype(jnp.int32), axis=1
    )

    head_shape = (length, HEADS, HEAD_DIM)
    inputs = tokens.astype(wide)
    unit_attn, factor_attn = normalize(inputs)
    normed_attn = (unit_attn * gain_attn).astype(low)
    query_raw = dot(normed_attn, full_query)
    key_raw = dot(normed_attn, full_key)
    value_low = dot(normed_attn, full_value).astype(low).reshape(head_shape)
    unit_query, factor_query = normalize(query_raw)
    unit_key, factor_key = normalize(key_raw)
    cosine_table, sine_table = rotary(length, HEAD_DIM)
    query_low = rotate((unit_query * gain_query).reshape(head_shape), cosine_table, sine_table)
    query_low = query_low.astype(low)
    key_low = rotate((unit_key * gain_key).reshape(head_shape), cosine_table, sine_table)
    key_low = key_low.astype(low)
    positions = jnp.arange(length)
    segment_row = segment_ids[0]
    allowed = (positions[:, None] >= positions[None, :]) & (
        segment_row[:, None] == segment_row[None, :]
    )
    score_scale = HEAD_DIM ** (-0.5)
    scores = ein("qhd,khd->hqk", query_low, key_low) * score_scale
    scores = jnp.where(allowed[None], scores, masked_value)
    attn_probs = jnp.exp(scores - jnp.max(scores, axis=-1, keepdims=True))
    attn_probs = attn_probs / jnp.sum(attn_probs, axis=-1, keepdims=True)
    probs_low = attn_probs.astype(low)
    attended_low = ein("hqk,khd->qhd", probs_low, value_low).reshape(length, width).astype(low)
    residual = inputs + dot(attended_low, full_output)
    unit_ffn, factor_ffn = normalize(residual)
    normed_ffn = (unit_ffn * gain_ffn).astype(low)
    router_probs = jax.nn.softmax(dot(normed_ffn, full_router), axis=-1)

    x_all, g_all = all_gather(shape, [normed_ffn, out_grad], 2)
    y, dx, pg, grad_wgate, grad_wup, grad_wdown = experts_part(
        x_all, g_all, choices, full_router, w_gate, w_up, w_down
    )
    pg = pg.astype(low).reshape(devices, -1, width)
    pg = jnp.pad(pg, ((0, 0), (0, 16 - pg.shape[1]), (0, 0)))
    dx_sum, mixture = reduce_scatter(shape, [jnp.concatenate([dx, pg], axis=1), y], 3)
    result = (residual + mixture).astype(low)
    prob_grads = dx_sum[length : length + length * EXPERTS // width].reshape(length, EXPERTS)
    expert_input_grad = dx_sum[:length]

    upstream = out_grad.astype(wide)
    logit_grads = router_probs * (
        prob_grads - jnp.sum(router_probs * prob_grads, axis=-1, keepdims=True)
    )
    logit_low = logit_grads.astype(low)
    grad_router = tdot(normed_ffn, logit_low)
    grad_normed_ffn = rdot(logit_low, full_router) + expert_input_grad
    grad_gain_ffn = jnp.sum(grad_normed_ffn * unit_ffn, axis=0)
    residual_grad = upstream + norm_back(grad_normed_ffn * gain_ffn, unit_ffn, factor_ffn)
    residual_low = residual_grad.astype(low)
    grad_woutput = tdot(attended_low, residual_low, low)
    attended_grad = rdot(residual_low, full_output).astype(low).reshape(head_shape)
    value_grad = ein("hqk,qhd->khd", probs_low, attended_grad).astype(low).reshape(length, width)
    prob_grad = ein("qhd,khd->hqk", attended_grad, value_low)
    score_grads = (
        attn_probs * (prob_grad - jnp.sum(attn_probs * prob_grad, axis=-1, keepdims=True))
    ).astype(low)
    query_rot_grad = ein("hqk,khd->qhd", score_grads, key_low) * score_scale
    key_rot_grad = ein("hqk,qhd->khd", score_grads, query_low) * score_scale
    query_normed_grad = unrotate(query_rot_grad, cosine_table, sine_table).reshape(length, width)
    key_normed_grad = unrotate(key_rot_grad, cosine_table, sine_table).reshape(length, width)
    grad_gain_query = jnp.sum(query_normed_grad * unit_query, axis=0)
    grad_gain_key = jnp.sum(key_normed_grad * unit_key, axis=0)
    query_raw_grad = norm_back(query_normed_grad * gain_query, unit_query, factor_query).astype(low)
    key_raw_grad = norm_back(key_normed_grad * gain_key, unit_key, factor_key).astype(low)
    grad_wquery = tdot(normed_attn, query_raw_grad, low)
    grad_wkey = tdot(normed_attn, key_raw_grad, low)
    grad_wvalue = tdot(normed_attn, value_grad, low)
    grad_normed_attn = (
        rdot(query_raw_grad, full_query)
        + rdot(key_raw_grad, full_key)
        + rdot(value_grad, full_value)
    )
    grad_gain_attn = jnp.sum(grad_normed_attn * unit_attn, axis=0)
    input_grad = residual_grad + norm_back(grad_normed_attn * gain_attn, unit_attn, factor_attn)

    def parts_of(values):
        return values.reshape(devices, part, width)

    def block_rows(values):
        values = values.reshape(devices, -1)
        values = jnp.pad(values, ((0, 0), (0, -values.shape[1] % width)))
        return values.reshape(devices, -1, width).astype(low)

    gain_grads = jnp.stack([grad_gain_attn, grad_gain_query, grad_gain_key, grad_gain_ffn])
    gain_grads = gain_grads.reshape(4, devices, part).transpose(1, 0, 2)
    small = jnp.concatenate([block_rows(grad_router), block_rows(gain_grads)], axis=1)
    small = jnp.pad(small, ((0, 0), (0, 16 - small.shape[1]), (0, 0)))
    last = jnp.concatenate([parts_of(grad_woutput), small], axis=1)
    sums = in_parts(
        reduce_scatter,
        shape,
        [parts_of(grad_wquery), parts_of(grad_wkey), parts_of(grad_wvalue), last],
        1,
        4,
    )
    small = sums[3][part:]
    sum_router = small[: sizes[0]].reshape(-1)[: part * EXPERTS].reshape(part, EXPERTS)
    sum_gains = small[sizes[0], : 4 * part].reshape(4, part)
    return (
        result,
        input_grad,
        sums[0],
        sums[1],
        sums[2],
        sums[3][:part],
        sum_router,
        sum_gains[0],
        sum_gains[1],
        sum_gains[2],
        sum_gains[3],
        grad_wgate,
        grad_wup,
        grad_wdown,
        total_counts,
    )


def solution(mesh):
    rows, both = P(("exp", "hid"), None), P(("exp", "hid"))
    shape = grid_of(mesh.shape["exp"], mesh.shape["hid"])
    experts = (P("exp", None, "hid"), P("exp", None, "hid"), P("exp", "hid", None))
    return jax.shard_map(
        functools.partial(on_device, shape),
        mesh=mesh,
        in_specs=(rows,) * 8 + (both,) * 4 + experts + (rows,),
        out_specs=(rows,) * 7 + (both,) * 4 + experts + (P(),),
        check_vma=False,
    )
```

```python
import functools
import math

import jax
import jax.numpy as jnp
from jax import lax
from jax.experimental import pallas as pl
from jax.experimental.pallas import tpu as pltpu
from jax.sharding import PartitionSpec as P

MESH = pl.DeviceIdType.MESH


def grid_of(exp, hid):
    plane = exp // 2
    na = 1 << (int(math.log2(plane)) // 2)
    return na, plane // na, hid


class Place:
    def __init__(self, shape):
        self.na, self.nb, self.nz = shape
        e = lax.axis_index("exp")
        self.z = lax.axis_index("hid")
        self.c = e % 2
        self.b = (e // 2) % self.nb
        self.a = e // (2 * self.nb)

    def ident(self, a=None, b=None, c=None, z=None):
        a = self.a if a is None else a
        b = self.b if b is None else b
        c = self.c if c is None else c
        z = self.z if z is None else z
        return ((a * self.nb + b) * 2 + c, z)

    def linear(self, **kw):
        e, z = self.ident(**kw)
        return e * self.nz + z


def xor(value, k):
    if isinstance(k, int) and k == 0:
        return value
    out = 0
    for bit in (1, 2, 4):
        out = out + ((value // bit + k // bit) % 2) * bit
    return out


def greet(p):
    barrier = pltpu.get_barrier_semaphore()
    n = 0
    for k in range(1, p.nz):
        pl.semaphore_signal(barrier, inc=1, device_id=p.ident(z=xor(p.z, k)), device_id_type=MESH)
        n += 1
    for k in range(1, p.na):
        pl.semaphore_signal(barrier, inc=1, device_id=p.ident(a=xor(p.a, k)), device_id_type=MESH)
        n += 1
    for k in range(1, p.nb):
        pl.semaphore_signal(barrier, inc=1, device_id=p.ident(b=xor(p.b, k)), device_id_type=MESH)
        n += 1
    pl.semaphore_signal(barrier, inc=1, device_id=p.ident(c=1 - p.c), device_id_type=MESH)
    n += 1
    pl.semaphore_wait(barrier, n)


def ag_count(shape):
    na, nb, nz = shape
    return (nz - 1) + nz * (na - 1) + nz * (nb - 1) + nz * na * (nb - 1) + nz * nb * (na - 1) + na * nb * nz


class Gather:
    def __init__(self, p, x, o, send, recv, local, base=0):
        self.p, self.x, self.o, self.send, self.recv, self.local = p, x, o, send, recv, local
        rows = x.shape[0]
        cut = rows // 32 * 16 if rows >= 32 else rows
        self.halves = ((0, cut), (cut, rows - cut))
        na, nb, nz = p.na, p.nb, p.nz
        whole = rows > cut
        self.a1, self.b2 = range(1, na), range(1, nb)
        self.b1, self.a2 = (range(1, nb), range(1, na)) if whole else ((), ())
        i = base
        self.iz = i; i += nz - 1
        self.i1a = i; i += nz * (na - 1)
        self.i1b = i; i += nz * (nb - 1)
        self.i2b = i; i += nz * na * (nb - 1)
        self.i2a = i; i += nz * nb * (na - 1)
        self.isib = i; i += na * nb * nz
        self.end = i

    def copy(self, src, dst, i, target):
        return pltpu.make_async_remote_copy(src_ref=src, dst_ref=dst, send_sem=self.send.at[i], recv_sem=self.recv.at[i], device_id=target, device_id_type=MESH)

    def part(self, d, h):
        s, n = self.halves[h]
        return self.o.at[d, pl.ds(s, n)]

    def src(self, d, h, own):
        s, n = self.halves[h]
        return self.x.at[pl.ds(s, n)] if own else self.o.at[d, pl.ds(s, n)]

    def m_z(self, k):
        p = self.p
        d = p.linear()
        return self.copy(self.x, self.o.at[d], self.iz + k - 1, p.ident(z=xor(p.z, k)))

    def r_z(self, k):
        p = self.p
        d = p.linear(z=xor(p.z, k))
        return self.copy(self.o.at[d], self.o.at[d], self.iz + k - 1, p.ident(z=xor(p.z, k)))

    def m_1(self, axis, k, j):
        p = self.p
        n = p.na if axis == "a" else p.nb
        base = self.i1a if axis == "a" else self.i1b
        h = 0 if axis == "a" else 1
        d = p.linear(z=xor(p.z, k))
        t = p.ident(**{axis: xor(getattr(p, axis), j)})
        return self.copy(self.src(d, h, k == 0), self.part(d, h), base + k * (n - 1) + j - 1, t)

    def r_1(self, axis, k, j):
        p = self.p
        n = p.na if axis == "a" else p.nb
        base = self.i1a if axis == "a" else self.i1b
        h = 0 if axis == "a" else 1
        d = p.linear(z=xor(p.z, k), **{axis: xor(getattr(p, axis), j)})
        return self.copy(self.part(d, h), self.part(d, h), base + k * (n - 1) + j - 1, p.ident(**{axis: xor(getattr(p, axis), j)}))

    def m_2(self, axis, k, i, j):
        p = self.p
        other = "b" if axis == "a" else "a"
        n = p.na if axis == "a" else p.nb
        m = p.nb if axis == "a" else p.na
        base = self.i2a if axis == "a" else self.i2b
        h = 1 if axis == "a" else 0
        d = p.linear(z=xor(p.z, k), **{other: xor(getattr(p, other), i)})
        t = p.ident(**{axis: xor(getattr(p, axis), j)})
        return self.copy(self.src(d, h, k == 0 and i == 0), self.part(d, h), base + (k * m + i) * (n - 1) + j - 1, t)

    def r_2(self, axis, k, i, j):
        p = self.p
        other = "b" if axis == "a" else "a"
        n = p.na if axis == "a" else p.nb
        m = p.nb if axis == "a" else p.na
        base = self.i2a if axis == "a" else self.i2b
        h = 1 if axis == "a" else 0
        d = p.linear(z=xor(p.z, k), **{other: xor(getattr(p, other), i), axis: xor(getattr(p, axis), j)})
        t = p.ident(**{axis: xor(getattr(p, axis), j)})
        return self.copy(self.part(d, h), self.part(d, h), base + (k * m + i) * (n - 1) + j - 1, t)

    def m_s(self, k, i, j):
        p = self.p
        d = p.linear(z=xor(p.z, k), a=xor(p.a, i), b=xor(p.b, j))
        own = k == 0 and i == 0 and j == 0
        return self.copy(self.x if own else self.o.at[d], self.o.at[d], self.isib + (k * p.na + i) * p.nb + j, p.ident(c=1 - p.c))

    def r_s(self, k, i, j):
        p = self.p
        d = p.linear(z=xor(p.z, k), a=xor(p.a, i), b=xor(p.b, j), c=1 - p.c)
        return self.copy(self.o.at[d], self.o.at[d], self.isib + (k * p.na + i) * p.nb + j, p.ident(c=1 - p.c))

    def own(self):
        return pltpu.make_async_copy(self.x, self.o.at[self.p.linear()], self.local)

    def start(self):
        self.begin()
        for k in range(1, self.p.nz):
            self.launch(k)

    def begin(self):
        self.own().start()
        self.spread(0)

    def launch(self, k):
        self.m_z(k).start()

    def spread(self, k):
        p = self.p
        for j in self.a1:
            self.m_1("a", k, j).start()
        for j in self.b1:
            self.m_1("b", k, j).start()
        for j in self.b2:
            self.m_2("b", k, 0, j).start()
        for j in self.a2:
            self.m_2("a", k, 0, j).start()
        self.m_s(k, 0, 0).start()

    def turn(self, k):
        p = self.p
        for i in self.a1:
            self.r_1("a", k, i).wait_recv()
            for j in self.b2:
                self.m_2("b", k, i, j).start()
        for i in self.b1:
            self.r_1("b", k, i).wait_recv()
            for j in self.a2:
                self.m_2("a", k, i, j).start()

    def close(self, k):
        p = self.p
        for i in range(p.na):
            for j in self.b2:
                self.r_2("b", k, i, j).wait_recv()
        for i in range(p.nb):
            for j in self.a2:
                self.r_2("a", k, i, j).wait_recv()
        for i in range(p.na):
            for j in range(p.nb):
                if i or j:
                    self.m_s(k, i, j).start()

    def arrive(self, k):
        self.r_z(k).wait_recv()
        self.spread(k)

    def middle(self):
        p = self.p
        for k in range(1, p.nz):
            self.arrive(k)
            self.turn(k - 1)
        self.turn(p.nz - 1)
        for k in range(p.nz):
            self.close(k)

    def plane(self, k):
        for i in range(self.p.na):
            for j in range(self.p.nb):
                self.r_s(k, i, j).wait_recv()

    def finish(self):
        p = self.p
        for k in range(p.nz):
            for i in range(p.na):
                for j in range(p.nb):
                    self.m_s(k, i, j).wait_send()
        for k in range(1, p.nz):
            self.m_z(k).wait_send()
        for k in range(p.nz):
            for j in self.a1:
                self.m_1("a", k, j).wait_send()
            for j in self.b1:
                self.m_1("b", k, j).wait_send()
            for j in self.a2:
                for i in range(p.nb):
                    self.m_2("a", k, i, j).wait_send()
            for j in self.b2:
                for i in range(p.na):
                    self.m_2("b", k, i, j).wait_send()


def gather_kernel(shape, n, *refs):
    xs, os = refs[:n], refs[n:2 * n]
    send, recv, local = refs[2 * n:]
    p = Place(shape)
    greet(p)
    gs, base = [], 0
    for i in range(n):
        g = Gather(p, xs[i], os[i], send, recv, local.at[i], base)
        base = g.end
        gs.append(g)
    for g in gs:
        g.start()
    for k in range(1, p.nz):
        for g in gs:
            g.arrive(k)
            g.turn(k - 1)
    for g in gs:
        g.turn(p.nz - 1)
    for k in range(p.nz):
        for g in gs:
            g.close(k)
    for g in gs:
        g.own().wait()
        for k in range(p.nz):
            g.plane(k)
        g.finish()


def all_gather(shape, xs, collective_id):
    na, nb, nz = shape
    nd = na * nb * nz * 2
    n = len(xs)
    count = ag_count(shape) * n
    any_ = pl.BlockSpec(memory_space=pl.ANY)
    return pl.pallas_call(
        functools.partial(gather_kernel, shape, n),
        out_shape=[jax.ShapeDtypeStruct((nd,) + x.shape, x.dtype) for x in xs],
        in_specs=[any_] * n,
        out_specs=[any_] * n,
        scratch_shapes=[pltpu.SemaphoreType.DMA((count,)), pltpu.SemaphoreType.DMA((count,)), pltpu.SemaphoreType.DMA((n,))],
        compiler_params=pltpu.CompilerParams(collective_id=collective_id, has_side_effects=True),
    )(*xs)

OUTS = 4


def rs_layout(shape, rows):
    na, nb, nz = shape
    cut = rows // 32 * 16
    s0, s1 = cut, rows - cut
    counts = [na * nb * nz, (nb - 1) * na * nz, (na - 1) * nb * nz, (na - 1) * nz, (nb - 1) * nz, 2 * (nz - 1)]
    buffers = [
        (na, nb, nz, rows),
        (nb - 1, na, nz, s0),
        (na - 1, nb, nz, s1),
        (na - 1, nz, s0),
        (nb - 1, nz, s1),
        (nz - 1, rows),
    ]
    return counts, buffers


class Scatter:
    def __init__(self, p, v, out, buffers, send, recv, base=0, rows=None):
        self.p, self.v, self.out, self.send, self.recv = p, v, out, send, recv
        self.r1, self.r2b, self.r2a, self.r3a, self.r3b, self.r4 = buffers
        rows = out.shape[0] if rows is None else rows
        cut = rows // 32 * 16
        self.rows = rows
        self.halves = ((0, cut), (cut, rows - cut))
        counts, _ = rs_layout((p.na, p.nb, p.nz), rows)
        self.starts = []
        for n in counts:
            self.starts.append(base)
            base += n
        self.end = base
        self.waited = set()

    def copy(self, src, dst, i, target):
        return pltpu.make_async_remote_copy(src_ref=src, dst_ref=dst, send_sem=self.send.at[i], recv_sem=self.recv.at[i], device_id=target, device_id_type=MESH)

    def block(self, i, j, k, other=False):
        p = self.p
        if len(self.v.shape) == 5:
            return self.v.at[i, j, k]
        if len(self.v.shape) == 3:
            d = p.linear(a=xor(p.a, i), b=xor(p.b, j), z=xor(p.z, k))
            return self.v.at[d, pl.ds(0, self.rows)]
        c = 1 - p.c if other else p.c
        return self.v.at[xor(p.a, i), xor(p.b, j), c, xor(p.z, k)]

    def half(self, ref, h):
        s, n = self.halves[h]
        return ref.at[pl.ds(s, n)]

    def sibling(self, i, j, k):
        p = self.p
        n = self.starts[0] + (i * p.nb + j) * p.nz + k
        return self.copy(self.block(i, j, k, True), self.r1.at[i, j, k], n, p.ident(c=1 - p.c))

    def arrived(self, key, ref, i):
        if key in self.waited:
            return None
        self.waited.add(key)
        p = self.p
        return self.copy(ref, ref, i, p.ident(c=1 - p.c))

    def base_inputs(self, i, j, k, h):
        p = self.p
        n = self.starts[0] + (i * p.nb + j) * p.nz + k
        r = self.r1.at[i, j, k]
        return [(self.half(self.block(i, j, k), h), None), (self.half(r, h), self.arrived((1, i, j, k), r, n))]

    def two(self, h, far, near, k):
        p = self.p
        if h == 0:
            r, n = self.r2b.at[far - 1, near, k], self.starts[1] + ((far - 1) * p.na + near) * p.nz + k
        else:
            r, n = self.r2a.at[far - 1, near, k], self.starts[2] + ((far - 1) * p.nb + near) * p.nz + k
        return r, n

    def three(self, h, far, k):
        p = self.p
        if h == 0:
            return self.r3a.at[far - 1, k], self.starts[3] + (far - 1) * p.nz + k
        return self.r3b.at[far - 1, k], self.starts[4] + (far - 1) * p.nz + k

    def four(self, h, k):
        return self.half(self.r4.at[k - 1], h), self.starts[5] + 2 * (k - 1) + h

    def stage2(self, k):
        p, jobs = self.p, []
        for far, near in [(f, n) for n in range(max(p.na, p.nb)) for f in range(1, max(p.na, p.nb))]:
            if far < p.nb and near < p.na:
                r, n = self.two(0, far, near, k)
                own = self.half(self.r1.at[near, far, k], 0)
                jobs.append((self.base_inputs(near, far, k, 0), (own, r, n, p.ident(b=xor(p.b, far)))))
            if far < p.na and near < p.nb:
                r, n = self.two(1, far, near, k)
                own = self.half(self.r1.at[far, near, k], 1)
                jobs.append((self.base_inputs(far, near, k, 1), (own, r, n, p.ident(a=xor(p.a, far)))))
        return jobs

    def with_two(self, h, near, k):
        p = self.p
        i, j = (near, 0) if h == 0 else (0, near)
        got = self.base_inputs(i, j, k, h)
        for far in range(1, p.nb if h == 0 else p.na):
            r, n = self.two(h, far, near, k)
            got.append((r, self.arrived((2, h, far, near, k), r, n)))
        return got

    def stage3(self, k):
        p, jobs = self.p, []
        for near in range(1, max(p.na, p.nb)):
            if near < p.na:
                r, n = self.three(0, near, k)
                own = self.half(self.r1.at[near, 0, k], 0)
                jobs.append((self.with_two(0, near, k), (own, r, n, p.ident(a=xor(p.a, near)))))
            if near < p.nb:
                r, n = self.three(1, near, k)
                own = self.half(self.r1.at[0, near, k], 1)
                jobs.append((self.with_two(1, near, k), (own, r, n, p.ident(b=xor(p.b, near)))))
        return jobs

    def with_three(self, h, k):
        p = self.p
        got = self.with_two(h, 0, k)
        for far in range(1, p.na if h == 0 else p.nb):
            r, n = self.three(h, far, k)
            got.append((r, self.arrived((3, h, far, k), r, n)))
        return got

    def stage4(self, k, last):
        p, jobs = self.p, []
        if last != (k == 0):
            return jobs
        for h in range(2):
            got = self.with_three(h, k)
            if k:
                r, n = self.four(h, k)
                own = self.half(self.r1.at[0, 0, k], h)
                jobs.append((got, (own, r, n, p.ident(z=xor(p.z, k)))))
            else:
                for far in range(1, p.nz):
                    r, n = self.four(h, far)
                    got.append((r, self.arrived((4, h, far), r, n)))
                jobs.append((got, self.half(self.out, h)))
        return jobs

    def start(self):
        p = self.p
        for k in reversed(range(p.nz)):
            for i in reversed(range(p.na)):
                for j in reversed(range(p.nb)):
                    self.sibling(i, j, k).start()

    def finish(self):
        p = self.p
        for k in range(p.nz):
            for i in range(p.na):
                for j in range(p.nb):
                    self.sibling(i, j, k).wait_send()


class Worker:
    def __init__(self, ins, outbuf, finbuf, load, put, fin, send, recv):
        self.ins, self.outbuf, self.finbuf = ins, outbuf, finbuf
        self.load, self.put, self.fin, self.send, self.recv = load, put, fin, send, recv
        self.room = outbuf.shape[1]
        self.jobs, self.loaded, self.ran = [], 0, 0
        self.puts, self.n_out = [], 0
        self.sends = []

    def add(self, jobs):
        self.jobs.extend(jobs)

    def place(self, j, n, rows):
        return self.ins[j % 2].at[pl.ds(n * self.room, rows)]

    def loading(self, j, n):
        ref, _ = self.jobs[j][0][n]
        return pltpu.make_async_copy(ref, self.place(j, n, ref.shape[0]), self.load.at[j % 2, n])

    def fetch(self, j):
        inputs, _ = self.jobs[j]
        for n, (ref, arrived) in enumerate(inputs):
            if arrived is not None:
                if n > 1:
                    self.forward(0)
                arrived.wait_recv()
            self.loading(j, n).start()
        self.loaded = j + 1

    def forward(self, left):
        while len(self.puts) > left:
            put, (own, r, n, where) = self.puts.pop(0)
            put.wait()
            c = pltpu.make_async_remote_copy(
                src_ref=own,
                dst_ref=r,
                send_sem=self.send.at[n],
                recv_sem=self.recv.at[n],
                device_id=where,
                device_id_type=MESH,
            )
            c.start()
            self.sends.append(c)

    def run(self, j):
        inputs, out = self.jobs[j]
        rows = inputs[0][0].shape[0]
        for n in range(len(inputs)):
            self.loading(j, n).wait()
        final = not isinstance(out, tuple)
        if final:
            target = self.finbuf
        else:
            self.forward(OUTS - 1)
            s = self.n_out % OUTS
            self.n_out += 1
            target = self.outbuf.at[s]
        source, count, room = self.ins[j % 2], len(inputs), self.room

        def body(t, carry):
            acc = source[pl.ds(pl.multiple_of(t * 16, 16), 16)].astype(jnp.float32)
            for n in range(1, count):
                at = pl.ds(pl.multiple_of(n * room + t * 16, 16), 16)
                acc = acc + source[at].astype(jnp.float32)
            target[pl.ds(pl.multiple_of(t * 16, 16), 16)] = acc.astype(target.dtype)
            return carry

        lax.fori_loop(0, rows // 16, body, 0)
        if final:
            c = pltpu.make_async_copy(target.at[pl.ds(0, rows)], out, self.fin.at[0])
            c.start()
            c.wait()
        else:
            c = pltpu.make_async_copy(target.at[pl.ds(0, rows)], out[0], self.put.at[s])
            c.start()
            self.puts.append((c, out))
            self.forward(1)

    def drain(self):
        for j in range(self.ran, len(self.jobs)):
            if self.loaded <= j:
                self.fetch(j)
            if j + 1 < len(self.jobs):
                self.fetch(j + 1)
            self.run(j)
            self.ran = j + 1
        self.forward(0)

    def finish(self):
        for c in self.sends:
            c.wait_send()


def scatter_kernel(shape, n, *refs):
    vs, outs = refs[:n], refs[n:2 * n]
    bufs = refs[2 * n:8 * n]
    inbuf, outbuf, finbuf, load, put, fin, send, recv = refs[8 * n:]
    p = Place(shape)
    greet(p)
    scs, base = [], 0
    for i in range(n):
        s = Scatter(p, vs[i], outs[i], bufs[6 * i:6 * i + 6], send, recv, base)
        base = s.end
        scs.append(s)
    w = Worker((inbuf.at[0], inbuf.at[1]), outbuf, finbuf, load, put, fin, send, recv)
    steps = [(s, k) for s in scs for k in reversed(range(p.nz))]
    for s in scs:
        s.start()
    for t in range(len(steps) + 2):
        if t < len(steps):
            s, k = steps[t]
            w.add(s.stage2(k))
        if 1 <= t <= len(steps):
            s, k = steps[t - 1]
            w.add(s.stage3(k))
        if 2 <= t:
            s, k = steps[t - 2]
            w.add(s.stage4(k, k == 0))
    w.drain()
    w.finish()
    for s in scs:
        s.finish()


def reduce_scatter(shape, vs, collective_id):
    na, nb, nz = shape
    n = len(vs)
    any_ = pl.BlockSpec(memory_space=pl.ANY)
    vs = [v.reshape((na, nb, 2, nz) + v.shape[1:]) for v in vs]
    outs, bufs, total = [], [], 0
    rows = max(v.shape[4] for v in vs)
    width = vs[0].shape[5]
    for v in vs:
        counts, buffers = rs_layout(shape, v.shape[4])
        total += sum(counts)
        outs.append(jax.ShapeDtypeStruct(v.shape[4:], jnp.float32))
        bufs += [jax.ShapeDtypeStruct(b + (width,), v.dtype) for b in buffers]
    cut = rows - rows // 32 * 16
    inputs = na + nb + nz - 1
    got = pl.pallas_call(
        functools.partial(scatter_kernel, shape, n),
        out_shape=outs + bufs,
        in_specs=[any_] * n,
        out_specs=[any_] * (7 * n),
        scratch_shapes=[
            pltpu.VMEM((2, inputs * cut, width), jnp.bfloat16),
            pltpu.VMEM((OUTS, cut, width), jnp.bfloat16),
            pltpu.VMEM((cut, width), jnp.float32),
            pltpu.SemaphoreType.DMA((2, inputs)),
            pltpu.SemaphoreType.DMA((OUTS,)),
            pltpu.SemaphoreType.DMA((1,)),
            pltpu.SemaphoreType.DMA((total,)),
            pltpu.SemaphoreType.DMA((total,)),
        ],
        compiler_params=pltpu.CompilerParams(collective_id=collective_id, has_side_effects=True, vmem_limit_bytes=56 << 20),
    )(*vs)
    return got[:n]

CHUNK = 512
CAP = 32


def experts_kernel(shape, local, *refs):
    na, nb, nz = shape
    x, small, _, place, choice_t, wg_hbm, wu_hbm, wd_hbm = refs[:8]
    dx_sum, y_part, y_r1, xs_out, gs_out, hs_out, gu_out = refs[8:15]
    x_all, small_all, dx_part = refs[15:18]
    dx_bufs = refs[18:24]
    (wg, wu, wd, xs, gs, xin, gin, pin, sin, cin, ybuf, dbuf, gate, score, hkeep, gkeep, inbuf, outbuf, finbuf) = refs[24:43]
    (wsem, insem, savesem, keepsem, ownsem, outsem, load, put, fin, ag_send, ag_recv, ag_local, rs_send, rs_recv) = refs[43:]
    g_all = y_part
    p = Place(shape)
    length, width = x.shape
    planes = na * nb * 2
    slots = CAP
    many = planes * slots
    first = lax.axis_index("exp") * local
    greet(p)
    weights = [pltpu.make_async_copy(a, b, wsem.at[n]) for n, (a, b) in enumerate(((wg_hbm, wg), (wu_hbm, wu), (wd_hbm, wd)))]
    for w in weights:
        w.start()
    ga = Gather(p, x, x_all, ag_send, ag_recv, ag_local.at[0])
    gb = Gather(p, small, small_all, ag_send, ag_recv, ag_local.at[1], ga.end)
    both = (gb, ga)
    sd = Scatter(p, dx_part, dx_sum, dx_bufs, rs_send, rs_recv)
    sy = Scatter(p, y_part, None, (y_r1,) + (None,) * 5, rs_send, rs_recv, sd.end, length)
    work = Worker((inbuf.at[0], inbuf.at[1]), outbuf, finbuf, load, put, fin, rs_send, rs_recv)
    order = [*range(1, nz), 0]

    def step(name, k):
        for g in both:
            getattr(g, name)(k)

    for g in both:
        g.begin()
        g.launch(1)
    step("turn", 0)
    step("arrive", 1)
    for k in range(2, nz):
        for g in both:
            g.launch(k)
    step("close", 0)
    step("turn", 1)
    step("close", 1)
    for g in both:
        g.own().wait()

    def device(r, k):
        return r * nz + xor(p.z, k)

    def spots(s):
        at = pin[s]
        slot = lax.broadcasted_iota(jnp.int32, (slots, length), 0)
        rows = [jnp.where(at[e : e + 1] == slot, 1.0, 0.0) for e in range(local)]
        return rows, jnp.concatenate(rows, axis=0).astype(jnp.bfloat16)

    def dispatch(k):
        def loads(r, s):
            d = device(r, k)
            pairs = (
                (x_all.at[d], xin),
                (g_all.at[d, pl.ds(0, length)], gin),
                (place.at[d], pin),
                (small_all.at[d], sin),
                (choice_t.at[d], cin),
            )
            return [pltpu.make_async_copy(a, b.at[s], insem.at[s, n]) for n, (a, b) in enumerate(pairs)]

        def item(r, s):
            for c in loads(r, s):
                c.wait()
            masks, spot = spots(s)
            for n in range(0, width, CHUNK):
                for source, target in ((xin, xs), (gin, gs)):
                    rows = jnp.dot(spot, source[s, :, n : n + CHUNK], preferred_element_type=jnp.float32).astype(jnp.bfloat16)
                    for e in range(local):
                        at = pl.ds(pl.multiple_of(e * many + r * slots, slots), slots)
                        target[at, n : n + CHUNK] = rows[e * slots : (e + 1) * slots]
            chosen = cin[s]
            gates = sin[s].astype(jnp.float32)
            gates = gates[0:8, 0:length] + gates[8:16, 0:length]
            for e in range(local):
                weight = jnp.sum(jnp.where(chosen == first + e, gates, 0.0), axis=0, keepdims=True)
                value = jnp.sum(masks[e] * weight, axis=1, keepdims=True)
                gate[e, pl.ds(pl.multiple_of(r * slots, slots), slots)] = jnp.broadcast_to(value, (slots, 128))

        for c in loads(0, 0):
            c.start()

        def body(t, carry):
            for c in loads(2 * t + 1, 1):
                c.start()
            item(2 * t, 0)

            @pl.when(t < planes // 2 - 1)
            def _():
                for c in loads(2 * t + 2, 0):
                    c.start()

            item(2 * t + 1, 1)
            return carry

        lax.fori_loop(0, planes // 2, body, 0)

    def saves(k, e):
        at = pl.ds(pl.multiple_of(e * many, many), many)
        return [pltpu.make_async_copy(a.at[at], b.at[e, k], savesem.at[n, e]) for n, (a, b) in enumerate(((xs, xs_out), (gs, gs_out)))]

    def keeps(k, e, s):
        pairs = ((hkeep, hs_out), (gkeep, gu_out))
        return [pltpu.make_async_copy(a.at[s], b.at[e, k], keepsem.at[s, n]) for n, (a, b) in enumerate(pairs)]

    def expert(k, e, s):
        at = pl.ds(pl.multiple_of(e * many, many), many)
        rows = xs[at]
        gate_act = jnp.dot(rows, wg[e], preferred_element_type=jnp.float32)
        up_act = jnp.dot(rows, wu[e], preferred_element_type=jnp.float32)
        back = lax.dot_general(gs[at], wd[e], (((1,), (1,)), ((), ())), preferred_element_type=jnp.float32)
        weight = gate[e][:, 0:1]
        sig = jax.nn.sigmoid(gate_act)
        silu = gate_act * sig
        hidden = silu * up_act
        score[e] = jnp.broadcast_to(jnp.sum(hidden * back, axis=1, keepdims=True), (many, 128))
        grad = back * weight
        hs = (hidden * weight).astype(jnp.bfloat16)
        gu = (grad * silu).astype(jnp.bfloat16)
        gg = (grad * up_act * sig * (1.0 + gate_act * (1.0 - sig))).astype(jnp.bfloat16)
        hkeep[s] = hs
        gkeep[s] = jnp.concatenate([gg, gu], axis=1)
        for c in keeps(k, e, s):
            c.start()
        for c in saves(k, e):
            c.wait()
        for n in range(0, width, CHUNK):
            y = jnp.dot(hs, wd[e, :, n : n + CHUNK], preferred_element_type=jnp.float32)
            gs[at, n : n + CHUNK] = y.astype(jnp.bfloat16)
            form = (((1,), (1,)), ((), ()))
            dx = lax.dot_general(gg, wg[e, n : n + CHUNK], form, preferred_element_type=jnp.float32)
            dx = dx + lax.dot_general(gu, wu[e, n : n + CHUNK], form, preferred_element_type=jnp.float32)
            xs[at, n : n + CHUNK] = dx.astype(jnp.bfloat16)

    def experts(k, start, stop):
        def body(t, carry):
            for s in range(2):
                e = 2 * t + s

                @pl.when(e >= 2)
                def _():
                    for c in keeps(k, e - 2, s):
                        c.wait()

                expert(k, e, s)
            return carry

        lax.fori_loop(start // 2, stop // 2, body, 0)

    def combine(k):
        def at_offset(t, s):
            i, j = t // nb, t % nb
            c = p.c if s else 1 - p.c
            return i, j, (xor(p.a, i) * nb + xor(p.b, j)) * 2 + c

        def loads(t, s):
            r = at_offset(t, s)[2]
            d = device(r, k)
            return pltpu.make_async_copy(place.at[d], pin.at[s], insem.at[s, 0])

        def stores(t, s):
            i, j, _ = at_offset(t, s)
            got = []
            for n, (buf, sc) in enumerate(((ybuf, sy), (dbuf, sd))):
                if s:
                    got.append(pltpu.make_async_copy(buf.at[s], sc.block(i, j, k), outsem.at[n]))
                else:
                    m = sc.starts[0] + (i * nb + j) * nz + k
                    got.append(sc.copy(buf.at[s], sc.r1.at[i, j, k], m, p.ident(c=1 - p.c)))
            return got

        def finish(t, s):
            for c in stores(t, s):
                if s:
                    c.wait()
                else:
                    c.wait_send()

        def item(t, s):
            r = at_offset(t, s)[2]
            loads(t, s).wait()

            @pl.when(t > 0)
            def _():
                finish(t - 1, s)

            masks, spot = spots(s)
            form = (((0,), (0,)), ((), ()))
            for n in range(0, width, CHUNK):
                for source, target in ((gs, ybuf), (xs, dbuf)):
                    rows = [source[pl.ds(pl.multiple_of(e * many + r * slots, slots), slots), n : n + CHUNK] for e in range(local)]
                    rows = jnp.concatenate(rows, axis=0)
                    total = lax.dot_general(spot, rows, form, preferred_element_type=jnp.float32)
                    target[s, 0:length, n : n + CHUNK] = total.astype(jnp.bfloat16)
            row = lax.broadcasted_iota(jnp.int32, (8, length), 0)
            table = jnp.zeros((8, length), jnp.float32)
            for e in range(local):
                value = score[e, pl.ds(pl.multiple_of(r * slots, slots), slots)][:, 0:1]
                line = jnp.sum(masks[e] * value, axis=0, keepdims=True)
                table = jnp.where(row == (first + e) % 8, line, table)
            table = jnp.concatenate([table, jnp.zeros((8, length), jnp.float32)], axis=0)
            table = jnp.concatenate([table, jnp.zeros((16, 256 - length), jnp.float32)], axis=1)
            dbuf[s, length : length + 16] = jnp.zeros((16, width), jnp.bfloat16)
            dbuf[s, length : length + 16, pl.ds(pl.multiple_of(first // 8 * 256, 256), 256)] = table.astype(jnp.bfloat16)
            for c in stores(t, s):
                c.start()

        loads(0, 0).start()

        def body(t, carry):
            loads(t, 1).start()
            item(t, 0)

            @pl.when(t < na * nb - 1)
            def _():
                loads(t + 1, 0).start()

            item(t, 1)
            return carry

        lax.fori_loop(0, na * nb, body, 0)
        for s in range(2):
            finish(na * nb - 1, s)

    def add(jobs):
        work.add(jobs)
        work.drain()

    for t, k in enumerate(order):
        after = order[t + 1] if t + 1 < nz else 0
        for g in both:
            g.plane(k)
        dispatch(k)
        for e in range(local):
            for c in saves(k, e):
                c.start()
        if after:
            step("arrive", after)
        if t == 0:
            for w in weights:
                w.wait()
        half = local // 4 * 2
        if half:
            experts(k, 0, half)
        if after:
            step("turn", after)
        if t:
            add(sd.stage3(order[t - 1]))
        experts(k, half, local)
        for s in range(2):
            for c in keeps(k, local - 2 + s, s):
                c.wait()
        if after:
            step("close", after)
        if t:
            add(sd.stage4(order[t - 1], False))
        combine(k)
        add(sd.stage2(k))
    for k in range(nz):
        for i in range(na):
            for j in range(nb):
                r, n = y_r1.at[i, j, k], sy.starts[0] + (i * nb + j) * nz + k
                sy.copy(r, r, n, p.ident(c=1 - p.c)).wait_recv()
    add(sd.stage3(0))
    add(sd.stage4(0, True))
    work.finish()
    for g in both:
        g.finish()


def run_experts(shape, x, small, g_all, place, choice_t, wg, wu, wd, collective_id):
    na, nb, nz = shape
    local, width, hidden = wg.shape
    length = x.shape[0]
    planes = na * nb * 2
    many = planes * CAP
    tall = length + 16
    low, wide = jnp.bfloat16, jnp.float32
    any_ = pl.BlockSpec(memory_space=pl.ANY)
    sds = jax.ShapeDtypeStruct
    outs = [sds((tall, width), wide), sds(g_all.shape, low), sds((na, nb, nz, length, width), low)]
    outs += [sds((local, nz, many, width), low)] * 2 + [sds((local, nz, many, n * hidden), low) for n in (1, 2)]
    outs += [sds((g_all.shape[0],) + x.shape, low), sds((g_all.shape[0],) + small.shape, low)]
    outs += [sds((na, nb, nz, tall, width), low)]
    counts, buffers = rs_layout(shape, tall)
    total = sum(counts) + rs_layout(shape, length)[0][0]
    outs += [sds(b + (width,), low) for b in buffers]
    messages = 2 * ag_count(shape)
    room = tall - tall // 32 * 16
    inputs = na + nb + nz - 1
    dma = pltpu.SemaphoreType.DMA
    got = pl.pallas_call(
        functools.partial(experts_kernel, shape, local),
        out_shape=outs,
        in_specs=[any_] * 8,
        out_specs=[any_] * len(outs),
        input_output_aliases={2: 1},
        scratch_shapes=[
            pltpu.VMEM((local, width, hidden), low),
            pltpu.VMEM((local, width, hidden), low),
            pltpu.VMEM((local, hidden, width), low),
            pltpu.VMEM((local * many, width), low),
            pltpu.VMEM((local * many, width), low),
            pltpu.VMEM((2, length, width), low),
            pltpu.VMEM((2, length, width), low),
            pltpu.VMEM((2,) + place.shape[1:], jnp.int32),
            pltpu.VMEM((2,) + small.shape, low),
            pltpu.VMEM((2,) + choice_t.shape[1:], jnp.int32),
            pltpu.VMEM((2, length, width), low),
            pltpu.VMEM((2, tall, width), low),
            pltpu.VMEM((local, many, 128), wide),
            pltpu.VMEM((local, many, 128), wide),
            pltpu.VMEM((2, many, hidden), low),
            pltpu.VMEM((2, many, 2 * hidden), low),
            pltpu.VMEM((2, inputs * room, width), low),
            pltpu.VMEM((OUTS, room, width), low),
            pltpu.VMEM((room, width), wide),
            dma((3,)),
            dma((2, 5)),
            dma((2, local)),
            dma((2, 2)),
            dma((2,)),
            dma((2,)),
            dma((2, inputs)),
            dma((OUTS,)),
            dma((1,)),
            dma((messages,)),
            dma((messages,)),
            dma((2,)),
            dma((total,)),
            dma((total,)),
        ],
        compiler_params=pltpu.CompilerParams(
            collective_id=collective_id, has_side_effects=True, vmem_limit_bytes=63 << 20
        ),
    )(x, small, g_all, place, choice_t, wg, wu, wd)
    return got[:7]


def last_kernel(shape, part, *refs):
    na, nb, nz = shape
    y_part, _, normed_t, attended_t, dq, dk, dv, dres, small, xs, gs, hs, gu = refs[:13]
    y_sum, w_sum, dwg, dwu, dwd, y_r1, w_part = refs[13:20]
    y_bufs, w_bufs = refs[20:25], refs[25:31]
    wbuf, xin, gin, hin, uin, og, ou, od, accg, accd, inbuf, outbuf, finbuf = refs[31:44]
    tsem, outsem, insem, savesem, load, put, fin, send, recv = refs[44:]
    p = Place(shape)
    greet(p)
    length, width = y_sum.shape
    rows = 4 * part
    sy = Scatter(p, y_part, y_sum, (y_r1,) + tuple(y_bufs), send, recv)
    sy.waited = {(1, i, j, k) for i in range(na) for j in range(nb) for k in range(nz)}
    sw = Scatter(p, w_part, w_sum, w_bufs, send, recv, sy.end)
    work = Worker((inbuf.at[0], inbuf.at[1]), outbuf, finbuf, load, put, fin, send, recv)
    local, chunks = xs.shape[:2]
    hidden = hs.shape[3]
    order = [*range(1, nz), 0]

    def add(jobs):
        work.add(jobs)
        work.drain()

    def products():
        def where(t, s):
            i, j = t // nb, t % nb
            c = p.c if s else 1 - p.c
            return i, j, (xor(p.a, i) * nb + xor(p.b, j)) * 2 + c

        def stores(t, s):
            i, j, _ = where(t, s)
            got = []
            for k in range(nz):
                src = wbuf.at[s, xor(p.z, k)]
                if s:
                    got.append(pltpu.make_async_copy(src, sw.block(i, j, k), outsem.at[k]))
                else:
                    n = sw.starts[0] + (i * nb + j) * nz + k
                    got.append(sw.copy(src, sw.r1.at[i, j, k], n, p.ident(c=1 - p.c)))
            return got

        def finish(t, s):
            for c in stores(t, s):
                if s:
                    c.wait()
                else:
                    c.wait_send()

        def tail(t, s, z):
            r = where(t, s)[2]
            return pltpu.make_async_copy(small.at[r * nz + z], wbuf.at[s, z, pl.ds(rows, 16)], tsem.at[s, z])

        def body(t, carry):
            for s in range(2):

                @pl.when(t > 0)
                def _():
                    finish(t - 1, s)

                for z in range(nz):
                    tail(t, s, z).start()
                r = where(t, s)[2]
                at = pl.ds(pl.multiple_of(r * nz * part, nz * part), nz * part)
                for m, (left, right) in enumerate(((normed_t, dq), (normed_t, dk), (normed_t, dv), (attended_t, dres))):
                    for n in range(0, width, 512):
                        got = jnp.dot(left[at], right[:, n : n + 512], preferred_element_type=jnp.float32).astype(jnp.bfloat16)
                        for z in range(nz):
                            wbuf[s, z, m * part : (m + 1) * part, n : n + 512] = got[z * part : (z + 1) * part]
                for z in range(nz):
                    tail(t, s, z).wait()
                for c in stores(t, s):
                    c.start()
            return carry

        lax.fori_loop(0, na * nb, body, 0)
        for s in range(2):
            finish(na * nb - 1, s)

    pieces = [(e, c) for e in range(local) for c in range(chunks)]

    def loads(n):
        e, c = pieces[n]
        pairs = ((xs, xin), (gs, gin), (hs, hin), (gu, uin))
        return [pltpu.make_async_copy(a.at[e, c], b.at[n % 2], insem.at[n % 2, m]) for m, (a, b) in enumerate(pairs)]

    def saves(e):
        s = e % 2
        pairs = ((og, dwg), (ou, dwu), (od, dwd))
        return [pltpu.make_async_copy(a.at[s], b.at[e], savesem.at[s, m]) for m, (a, b) in enumerate(pairs)]

    def piece(n):
        e, c = pieces[n]
        s, o = n % 2, e % 2
        if n + 1 < len(pieces):
            for d in loads(n + 1):
                d.start()
        for d in loads(n):
            d.wait()
        if c == 0 and e >= 2:
            for d in saves(e - 2):
                d.wait()
        form = (((0,), (0,)), ((), ()))

        def columns(t, carry):
            at = pl.ds(pl.multiple_of(t * 512, 512), 512)
            g = lax.dot_general(xin[s, :, at], uin[s], form, preferred_element_type=jnp.float32)
            d = lax.dot_general(hin[s], gin[s, :, at], form, preferred_element_type=jnp.float32)
            if c:
                g = g + accg[at]
                d = d + accd[:, at]
            if c + 1 < chunks:
                accg[at] = g
                accd[:, at] = d
            else:
                og[o, at] = g[:, :hidden].astype(jnp.bfloat16)
                ou[o, at] = g[:, hidden:].astype(jnp.bfloat16)
                od[o, :, at] = d.astype(jnp.bfloat16)
            return carry

        lax.fori_loop(0, width // 512, columns, 0)
        if c + 1 == chunks:
            for d in saves(e):
                d.start()

    for d in loads(0):
        d.start()
    steps = [(s, k) for s in (sy, sw) for k in order]
    done, count = 0, len(steps) + 1
    for t in range(count + 1):
        if t < len(steps):
            s, k = steps[t]
            add(s.stage2(k))
        if t == 0:
            products()
        else:
            until = len(pieces) * t // (count - 1) if t < count - 1 else len(pieces)
            while done < until:
                piece(done)
                done += 1
        if 1 <= t <= len(steps):
            s, k = steps[t - 1]
            add(s.stage3(k))
        if 2 <= t:
            s, k = steps[t - 2]
            add(s.stage4(k, False))
    for s in (sy, sw):
        add(s.stage4(0, True))
    work.finish()
    for e in range(max(0, local - 2), local):
        for d in saves(e):
            d.wait()


def run_last(shape, y_part, y_r1, normed_t, attended_t, dq, dk, dv, dres, small, xs, gs, hs, gu, collective_id):
    na, nb, nz = shape
    width, length = normed_t.shape
    part = width // small.shape[0]
    tall = 4 * part + 16
    low, wide = jnp.bfloat16, jnp.float32
    local, hidden = xs.shape[0], hs.shape[3]
    total_slots = xs.shape[1] * xs.shape[2]
    deep = min(1024, total_slots)
    xs, gs, hs, gu = (a.reshape(local, total_slots // deep, deep, a.shape[3]) for a in (xs, gs, hs, gu))
    any_, vmem = pl.BlockSpec(memory_space=pl.ANY), pl.BlockSpec(memory_space=pltpu.VMEM)
    sds = jax.ShapeDtypeStruct
    outs = [sds((length, width), wide), sds((tall, width), wide)]
    outs += [sds((local, width, hidden), low)] * 2 + [sds((local, hidden, width), low)]
    outs += [sds(y_r1.shape, low), sds((na, nb, nz, tall, width), low)]
    y_counts, y_buffers = rs_layout(shape, length)
    w_counts, w_buffers = rs_layout(shape, tall)
    total = sum(y_counts) + sum(w_counts)
    outs += [sds(b + (width,), low) for b in y_buffers[1:] + w_buffers]
    room = max(tall - tall // 32 * 16, length - length // 32 * 16)
    inputs = na + nb + nz - 1
    dma = pltpu.SemaphoreType.DMA
    several = 1 if total_slots > deep else 0
    got = pl.pallas_call(
        functools.partial(last_kernel, shape, part),
        out_shape=outs,
        in_specs=[any_] * 2 + [vmem] * 6 + [any_] * 5,
        out_specs=[any_] * len(outs),
        input_output_aliases={1: 5},
        scratch_shapes=[
            pltpu.VMEM((2, nz, tall, width), low),
            pltpu.VMEM((2, deep, width), low),
            pltpu.VMEM((2, deep, width), low),
            pltpu.VMEM((2, deep, hidden), low),
            pltpu.VMEM((2, deep, 2 * hidden), low),
            pltpu.VMEM((2, width, hidden), low),
            pltpu.VMEM((2, width, hidden), low),
            pltpu.VMEM((2, hidden, width), low),
            pltpu.VMEM((width if several else 8, 2 * hidden), wide),
            pltpu.VMEM((hidden if several else 8, width), wide),
            pltpu.VMEM((2, inputs * room, width), low),
            pltpu.VMEM((OUTS, room, width), low),
            pltpu.VMEM((room, width), wide),
            dma((2, nz)),
            dma((nz,)),
            dma((2, 4)),
            dma((2, 3)),
            dma((2, inputs)),
            dma((OUTS,)),
            dma((1,)),
            dma((total,)),
            dma((total,)),
        ],
        compiler_params=pltpu.CompilerParams(
            collective_id=collective_id, has_side_effects=True, vmem_limit_bytes=63 << 20
        ),
    )(y_part, y_r1, normed_t, attended_t, dq, dk, dv, dres, small, xs, gs, hs, gu)
    return got[:5]

HEADS = 16
HEAD_DIM = 128
EXPERTS = 64
TOP = 8
CAP = 32

epsilon = 1e-05
base_freq = 10000.0
masked_value = -1e30
low = jnp.bfloat16
wide = jnp.float32


def normalize(values):
    factor = lax.rsqrt(jnp.mean(values * values, axis=-1, keepdims=True) + epsilon)
    return (values * factor, factor)


def norm_back(grad_normed, unit_values, factor):
    return factor * (
        grad_normed - unit_values * jnp.mean(grad_normed * unit_values, axis=-1, keepdims=True)
    )


def rotary(length, head_width):
    positions = jnp.arange(length, dtype=jnp.float32)
    freqs = base_freq ** (-jnp.arange(head_width // 2, dtype=jnp.float32) * 2.0 / head_width)
    angles = positions[:, None] * freqs[None, :]
    return (jnp.cos(angles)[:, None, :], jnp.sin(angles)[:, None, :])


def rotate(values, cosine_table, sine_table):
    half_dim = values.shape[-1] // 2
    first = values[..., :half_dim]
    second = values[..., half_dim:]
    return jnp.concatenate(
        [first * cosine_table - second * sine_table, second * cosine_table + first * sine_table],
        axis=-1,
    )


def unrotate(grads_in, cosine_table, sine_table):
    half_dim = grads_in.shape[-1] // 2
    first = grads_in[..., :half_dim]
    second = grads_in[..., half_dim:]
    return jnp.concatenate(
        [first * cosine_table + second * sine_table, second * cosine_table - first * sine_table],
        axis=-1,
    )


def dot(left, right, kind=wide):
    return jnp.dot(left, right, preferred_element_type=kind)


def tdot(left, right, kind=wide):
    return lax.dot_general(left, right, (((0,), (0,)), ((), ())), preferred_element_type=kind)


def rdot(left, right):
    return lax.dot_general(left, right, (((1,), (1,)), ((), ())), preferred_element_type=wide)


def ein(form, *values):
    return jnp.einsum(form, *values, preferred_element_type=wide)


def gather_all(shape, weights, rows, collective_id):
    part = weights[0].shape[0]
    if part >= 32:
        *full, rows = all_gather(shape, weights + [rows], collective_id)
    else:
        full, rows = all_gather(shape, [jnp.concatenate(weights), rows], collective_id)
        full = [full[:, i * part : (i + 1) * part] for i in range(len(weights))]
    return [w.reshape(-1, w.shape[2]) for w in full], rows


def slot_table(choices, local):
    length = choices.shape[2]
    mine = lax.axis_index("exp") * local + jnp.arange(local)
    chosen = jnp.any(choices[:, None] == mine[:, None, None], axis=2)
    order = jnp.arange(length)
    before = (order[:, None] < order[None, :]).astype(low)
    ranks = ein("rjt,tu->rju", chosen.astype(low), before).astype(jnp.int32)
    return jnp.where(chosen, ranks, -1)


def on_device(
    shape,
    tokens,
    segment_ids,
    expert_choice,
    w_query,
    w_key,
    w_value,
    w_output,
    w_router,
    attn_gain,
    query_gain,
    key_gain,
    ffn_gain,
    w_gate,
    w_up,
    w_down,
    out_grad,
):
    length, width = tokens.shape
    part = w_query.shape[0]
    devices = width // part

    def rows_of(values):
        flat = values.reshape(-1).astype(low)
        return jnp.pad(flat, (0, -flat.shape[0] % width)).reshape(-1, width)

    small = [w_router, jnp.concatenate([attn_gain, query_gain, key_gain, ffn_gain]), expert_choice.T]
    small = [rows_of(s) for s in small]
    sizes = [s.shape[0] for s in small]
    small = jnp.concatenate(small)
    small = jnp.pad(small, ((0, 16 - small.shape[0]), (0, 0)))
    weights, g_all = gather_all(
        shape, [w_query, w_key, w_value, w_output], jnp.concatenate([out_grad, small]), 1
    )
    full_query, full_key, full_value, full_output = weights
    small = g_all[:, length:]
    full_router = small[:, : sizes[0]].reshape(devices, -1)[:, : part * EXPERTS]
    full_router = full_router.reshape(width, EXPERTS)
    gains = small[:, sizes[0], : 4 * part].reshape(devices, 4, part).transpose(1, 0, 2)
    gain_attn, gain_query, gain_key, gain_ffn = gains.reshape(4, width).astype(wide)
    choices = small[:, sizes[0] + 1].reshape(devices, -1)[:, : length * TOP]
    choices = choices.reshape(devices, TOP, length).astype(jnp.int32)
    total_counts = jnp.sum(
        (choices.reshape(devices, -1)[:, None, :] == jnp.arange(EXPERTS)[:, None]).astype(jnp.int32),
        axis=2,
    )

    head_shape = (length, HEADS, HEAD_DIM)
    inputs = tokens.astype(wide)
    unit_attn, factor_attn = normalize(inputs)
    normed_attn = (unit_attn * gain_attn).astype(low)
    query_raw = dot(normed_attn, full_query)
    key_raw = dot(normed_attn, full_key)
    value_low = dot(normed_attn, full_value).astype(low).reshape(head_shape)
    unit_query, factor_query = normalize(query_raw)
    unit_key, factor_key = normalize(key_raw)
    cosine_table, sine_table = rotary(length, HEAD_DIM)
    query_low = rotate((unit_query * gain_query).reshape(head_shape), cosine_table, sine_table)
    query_low = query_low.astype(low)
    key_low = rotate((unit_key * gain_key).reshape(head_shape), cosine_table, sine_table)
    key_low = key_low.astype(low)
    positions = jnp.arange(length)
    segment_row = segment_ids[0]
    allowed = (positions[:, None] >= positions[None, :]) & (
        segment_row[:, None] == segment_row[None, :]
    )
    score_scale = HEAD_DIM ** (-0.5)
    scores = ein("qhd,khd->hqk", query_low, key_low) * score_scale
    scores = jnp.where(allowed[None], scores, masked_value)
    attn_probs = jnp.exp(scores - jnp.max(scores, axis=-1, keepdims=True))
    attn_probs = attn_probs / jnp.sum(attn_probs, axis=-1, keepdims=True)
    probs_low = attn_probs.astype(low)
    attended_low = ein("hqk,khd->qhd", probs_low, value_low).reshape(length, width).astype(low)
    residual = inputs + dot(attended_low, full_output)
    unit_ffn, factor_ffn = normalize(residual)
    normed_ffn = (unit_ffn * gain_ffn).astype(low)
    router_probs = jax.nn.softmax(dot(normed_ffn, full_router), axis=-1)

    chosen = expert_choice[:, :, None] == jnp.arange(EXPERTS)
    gates = jnp.sum(jnp.where(chosen, router_probs[:, None, :], 0.0), axis=-1).T
    upper = lax.reduce_precision(gates, 8, 7)
    gates = jnp.concatenate([upper, gates - upper]).astype(low)
    gates = jnp.pad(gates, ((0, 0), (0, -length % 256)))
    dx_sum, y_part, y_sibling, xs, gs, hs, gu = run_experts(
        shape,
        normed_ffn,
        gates,
        g_all,
        slot_table(choices, w_gate.shape[0]),
        choices,
        w_gate,
        w_up,
        w_down,
        2,
    )
    table = dx_sum[length : length + 8].reshape(8, 8, -1)[:, :, :length]
    prob_grads = table.transpose(2, 1, 0).reshape(length, EXPERTS)
    expert_input_grad = dx_sum[:length]

    upstream = out_grad.astype(wide)
    logit_grads = router_probs * (
        prob_grads - jnp.sum(router_probs * prob_grads, axis=-1, keepdims=True)
    )
    logit_low = logit_grads.astype(low)
    grad_router = tdot(normed_ffn, logit_low)
    grad_normed_ffn = rdot(logit_low, full_router) + expert_input_grad
    grad_gain_ffn = jnp.sum(grad_normed_ffn * unit_ffn, axis=0)
    residual_grad = upstream + norm_back(grad_normed_ffn * gain_ffn, unit_ffn, factor_ffn)
    residual_low = residual_grad.astype(low)
    attended_grad = rdot(residual_low, full_output).astype(low).reshape(head_shape)
    value_grad = ein("hqk,qhd->khd", probs_low, attended_grad).astype(low).reshape(length, width)
    prob_grad = ein("qhd,khd->hqk", attended_grad, value_low)
    score_grads = (
        attn_probs * (prob_grad - jnp.sum(attn_probs * prob_grad, axis=-1, keepdims=True))
    ).astype(low)
    query_rot_grad = ein("hqk,khd->qhd", score_grads, key_low) * score_scale
    key_rot_grad = ein("hqk,qhd->khd", score_grads, query_low) * score_scale
    query_normed_grad = unrotate(query_rot_grad, cosine_table, sine_table).reshape(length, width)
    key_normed_grad = unrotate(key_rot_grad, cosine_table, sine_table).reshape(length, width)
    grad_gain_query = jnp.sum(query_normed_grad * unit_query, axis=0)
    grad_gain_key = jnp.sum(key_normed_grad * unit_key, axis=0)
    query_raw_grad = norm_back(query_normed_grad * gain_query, unit_query, factor_query).astype(low)
    key_raw_grad = norm_back(key_normed_grad * gain_key, unit_key, factor_key).astype(low)
    grad_normed_attn = (
        rdot(query_raw_grad, full_query)
        + rdot(key_raw_grad, full_key)
        + rdot(value_grad, full_value)
    )
    grad_gain_attn = jnp.sum(grad_normed_attn * unit_attn, axis=0)
    input_grad = residual_grad + norm_back(grad_normed_attn * gain_attn, unit_attn, factor_attn)

    def block_rows(values):
        values = values.reshape(devices, -1)
        values = jnp.pad(values, ((0, 0), (0, -values.shape[1] % width)))
        return values.reshape(devices, -1, width).astype(low)

    gain_grads = jnp.stack([grad_gain_attn, grad_gain_query, grad_gain_key, grad_gain_ffn])
    gain_grads = gain_grads.reshape(4, devices, part).transpose(1, 0, 2)
    small = jnp.concatenate([block_rows(grad_router), block_rows(gain_grads)], axis=1)
    small = jnp.pad(small, ((0, 0), (0, 16 - small.shape[1]), (0, 0)))
    mixture, sums, grad_wgate, grad_wup, grad_wdown = run_last(
        shape,
        y_part,
        y_sibling,
        normed_attn.T,
        attended_low.T,
        query_raw_grad,
        key_raw_grad,
        value_grad,
        residual_low,
        small,
        xs,
        gs,
        hs,
        gu,
        3,
    )
    result = (residual + mixture).astype(low)
    small = sums[4 * part :]
    sums = sums[: 4 * part].reshape(4, part, width)
    sum_router = small[: sizes[0]].reshape(-1)[: part * EXPERTS].reshape(part, EXPERTS)
    sum_gains = small[sizes[0], : 4 * part].reshape(4, part)
    return (
        result,
        input_grad,
        sums[0],
        sums[1],
        sums[2],
        sums[3],
        sum_router,
        sum_gains[0],
        sum_gains[1],
        sum_gains[2],
        sum_gains[3],
        grad_wgate.astype(wide),
        grad_wup.astype(wide),
        grad_wdown.astype(wide),
        total_counts,
    )


def solution(mesh):
    rows, both = P(("exp", "hid"), None), P(("exp", "hid"))
    shape = grid_of(mesh.shape["exp"], mesh.shape["hid"])
    experts = (P("exp", None, "hid"), P("exp", None, "hid"), P("exp", "hid", None))
    return jax.shard_map(
        functools.partial(on_device, shape),
        mesh=mesh,
        in_specs=(rows,) * 8 + (both,) * 4 + experts + (rows,),
        out_specs=(rows,) * 7 + (both,) * 4 + experts + (P(),),
        check_vma=False,
    )
```

```python
import functools
import math

import jax
import jax.numpy as jnp
from jax import lax
from jax.experimental import pallas as pl
from jax.experimental.pallas import tpu as pltpu
from jax.sharding import PartitionSpec as P

MESH = pl.DeviceIdType.MESH


def grid_of(exp, hid):
    plane = exp // 2
    na = 1 << (int(math.log2(plane)) // 2)
    return na, plane // na, hid


class Place:
    def __init__(self, shape):
        na, nb, nz = self.na, self.nb, self.nz = shape
        e = lax.axis_index("exp")
        self.z = lax.axis_index("hid")
        self.c = lax.rem(e, 2)
        self.b = lax.rem(lax.div(e, 2), nb)
        self.a = lax.div(e, 2 * nb)
        self.zs = [xor(self.z, k) for k in range(nz)]
        aa = [xor(self.a, i) for i in range(na)]
        bb = [xor(self.b, j) for j in range(nb)]
        cc = [self.c, 1 - self.c]
        self.exp = [[[(x * nb + y) * 2 + w for w in cc] for y in bb] for x in aa]
        self.lines = [[[[w * nz + z for z in self.zs] for w in v] for v in u] for u in self.exp]

    def to(self, i=0, j=0, k=0, s=0):
        return (self.exp[i][j][s], self.zs[k])

    def line(self, i=0, j=0, k=0, s=0):
        return self.lines[i][j][s][k]


def xor(value, k):
    out = value
    for bit in (1, 2, 4):
        if k & bit:
            out = out + bit - 2 * bit * lax.rem(lax.div(value, bit), 2)
    return out


def xor_two(value, other, size):
    out, bit = 0, 1
    while bit < size:
        out = out + lax.rem(lax.div(value, bit) + lax.div(other, bit), 2) * bit
        bit *= 2
    return out


def greet(p):
    barrier = pltpu.get_barrier_semaphore()
    others = [p.to(k=k) for k in range(1, p.nz)] + [p.to(i=i) for i in range(1, p.na)]
    others += [p.to(j=j) for j in range(1, p.nb)] + [p.to(s=1)]
    for other in others:
        pl.semaphore_signal(barrier, inc=1, device_id=other, device_id_type=MESH)
    pl.semaphore_wait(barrier, len(others))


def ag_count(shape):
    na, nb, nz = shape
    return (nz - 1) + nz * (na - 1) + nz * (nb - 1) + nz * na * (nb - 1) + nz * nb * (na - 1) + na * nb * nz


class Gather:
    def __init__(self, p, x, o, send, recv, local, base=0):
        self.p, self.x, self.o, self.send, self.recv, self.local = p, x, o, send, recv, local
        rows = x.shape[0]
        cut = rows // 32 * 16 if rows >= 32 else rows
        self.halves = ((0, cut), (cut, rows - cut))
        na, nb, nz = p.na, p.nb, p.nz
        whole = rows > cut
        self.a1, self.b2 = range(1, na), range(1, nb)
        self.b1, self.a2 = (range(1, nb), range(1, na)) if whole else ((), ())
        i = base
        self.iz = i; i += nz - 1
        self.i1a = i; i += nz * (na - 1)
        self.i1b = i; i += nz * (nb - 1)
        self.i2b = i; i += nz * na * (nb - 1)
        self.i2a = i; i += nz * nb * (na - 1)
        self.isib = i; i += na * nb * nz
        self.end = i

    def copy(self, src, dst, i, target):
        return pltpu.make_async_remote_copy(src_ref=src, dst_ref=dst, send_sem=self.send.at[i], recv_sem=self.recv.at[i], device_id=target, device_id_type=MESH)

    def part(self, d, h):
        s, n = self.halves[h]
        return self.o.at[d, pl.ds(s, n)]

    def src(self, d, h, own):
        s, n = self.halves[h]
        return self.x.at[pl.ds(s, n)] if own else self.o.at[d, pl.ds(s, n)]

    def m_z(self, k):
        p = self.p
        return self.copy(self.x, self.o.at[p.line()], self.iz + k - 1, p.to(k=k))

    def r_z(self, k):
        p = self.p
        o = self.o.at[p.line(k=k)]
        return self.copy(o, o, self.iz + k - 1, p.to(k=k))

    def m_1(self, axis, k, j):
        p = self.p
        n, base, h, t = (p.na, self.i1a, 0, p.to(i=j)) if axis == "a" else (p.nb, self.i1b, 1, p.to(j=j))
        d = p.line(k=k)
        return self.copy(self.src(d, h, k == 0), self.part(d, h), base + k * (n - 1) + j - 1, t)

    def r_1(self, axis, k, j):
        p = self.p
        if axis == "a":
            n, base, h, t, d = p.na, self.i1a, 0, p.to(i=j), p.line(i=j, k=k)
        else:
            n, base, h, t, d = p.nb, self.i1b, 1, p.to(j=j), p.line(j=j, k=k)
        return self.copy(self.part(d, h), self.part(d, h), base + k * (n - 1) + j - 1, t)

    def m_2(self, axis, k, i, j):
        p = self.p
        if axis == "a":
            n, m, base, h, t, d = p.na, p.nb, self.i2a, 1, p.to(i=j), p.line(j=i, k=k)
        else:
            n, m, base, h, t, d = p.nb, p.na, self.i2b, 0, p.to(j=j), p.line(i=i, k=k)
        return self.copy(self.src(d, h, k == 0 and i == 0), self.part(d, h), base + (k * m + i) * (n - 1) + j - 1, t)

    def r_2(self, axis, k, i, j):
        p = self.p
        if axis == "a":
            n, m, base, h, t, d = p.na, p.nb, self.i2a, 1, p.to(i=j), p.line(i=j, j=i, k=k)
        else:
            n, m, base, h, t, d = p.nb, p.na, self.i2b, 0, p.to(j=j), p.line(i=i, j=j, k=k)
        return self.copy(self.part(d, h), self.part(d, h), base + (k * m + i) * (n - 1) + j - 1, t)

    def m_s(self, k, i, j):
        p = self.p
        d = p.line(i=i, j=j, k=k)
        own = k == 0 and i == 0 and j == 0
        return self.copy(self.x if own else self.o.at[d], self.o.at[d], self.isib + (k * p.na + i) * p.nb + j, p.to(s=1))

    def r_s(self, k, i, j):
        p = self.p
        d = p.line(i=i, j=j, k=k, s=1)
        return self.copy(self.o.at[d], self.o.at[d], self.isib + (k * p.na + i) * p.nb + j, p.to(s=1))

    def own(self):
        return pltpu.make_async_copy(self.x, self.o.at[self.p.line()], self.local)

    def start(self):
        self.begin()
        for k in range(1, self.p.nz):
            self.launch(k)

    def begin(self):
        self.own().start()
        self.spread(0)

    def launch(self, k):
        self.m_z(k).start()

    def spread(self, k):
        p = self.p
        for j in self.a1:
            self.m_1("a", k, j).start()
        for j in self.b1:
            self.m_1("b", k, j).start()
        for j in self.b2:
            self.m_2("b", k, 0, j).start()
        for j in self.a2:
            self.m_2("a", k, 0, j).start()
        self.m_s(k, 0, 0).start()

    def turn(self, k):
        p = self.p
        for i in self.a1:
            self.r_1("a", k, i).wait_recv()
            for j in self.b2:
                self.m_2("b", k, i, j).start()
        for i in self.b1:
            self.r_1("b", k, i).wait_recv()
            for j in self.a2:
                self.m_2("a", k, i, j).start()

    def close(self, k):
        p = self.p
        for i in range(p.na):
            for j in self.b2:
                self.r_2("b", k, i, j).wait_recv()
        for i in range(p.nb):
            for j in self.a2:
                self.r_2("a", k, i, j).wait_recv()
        for i in range(p.na):
            for j in range(p.nb):
                if i or j:
                    self.m_s(k, i, j).start()

    def arrive(self, k):
        self.r_z(k).wait_recv()
        self.spread(k)

    def middle(self):
        p = self.p
        for k in range(1, p.nz):
            self.arrive(k)
            self.turn(k - 1)
        self.turn(p.nz - 1)
        for k in range(p.nz):
            self.close(k)

    def plane(self, k):
        for i in range(self.p.na):
            for j in range(self.p.nb):
                self.r_s(k, i, j).wait_recv()

    def finish(self):
        p = self.p
        for k in range(p.nz):
            for i in range(p.na):
                for j in range(p.nb):
                    self.m_s(k, i, j).wait_send()
        for k in range(1, p.nz):
            self.m_z(k).wait_send()
        for k in range(p.nz):
            for j in self.a1:
                self.m_1("a", k, j).wait_send()
            for j in self.b1:
                self.m_1("b", k, j).wait_send()
            for j in self.a2:
                for i in range(p.nb):
                    self.m_2("a", k, i, j).wait_send()
            for j in self.b2:
                for i in range(p.na):
                    self.m_2("b", k, i, j).wait_send()

OUTS = 4


def rs_layout(shape, rows):
    na, nb, nz = shape
    cut = rows // 32 * 16
    s0, s1 = cut, rows - cut
    counts = [na * nb * nz, (nb - 1) * na * nz, (na - 1) * nb * nz, (na - 1) * nz, (nb - 1) * nz, 2 * (nz - 1)]
    buffers = [
        (na, nb, nz, rows),
        (nb - 1, na, nz, s0),
        (na - 1, nb, nz, s1),
        (na - 1, nz, s0),
        (nb - 1, nz, s1),
        (nz - 1, rows),
    ]
    return counts, buffers


class Scatter:
    def __init__(self, p, v, out, buffers, send, recv, base=0, rows=None):
        self.p, self.v, self.out, self.send, self.recv = p, v, out, send, recv
        self.r1, self.r2b, self.r2a, self.r3a, self.r3b, self.r4 = buffers
        rows = out.shape[0] if rows is None else rows
        cut = rows // 32 * 16
        self.rows = rows
        self.halves = ((0, cut), (cut, rows - cut))
        counts, _ = rs_layout((p.na, p.nb, p.nz), rows)
        self.starts = []
        for n in counts:
            self.starts.append(base)
            base += n
        self.end = base
        self.waited = set()

    def copy(self, src, dst, i, target):
        return pltpu.make_async_remote_copy(src_ref=src, dst_ref=dst, send_sem=self.send.at[i], recv_sem=self.recv.at[i], device_id=target, device_id_type=MESH)

    def block(self, i, j, k, s=0):
        p = self.p
        if len(self.v.shape) == 5:
            return self.v.at[i, j, k]
        return self.v.at[p.line(i, j, k, s), pl.ds(0, self.rows)]

    def half(self, ref, h):
        s, n = self.halves[h]
        return ref.at[pl.ds(s, n)]

    def sibling(self, i, j, k):
        p = self.p
        n = self.starts[0] + (i * p.nb + j) * p.nz + k
        return self.copy(self.block(i, j, k, 1), self.r1.at[i, j, k], n, p.to(s=1))

    def arrived(self, key, ref, i):
        if key in self.waited:
            return None
        self.waited.add(key)
        p = self.p
        return self.copy(ref, ref, i, p.to(s=1))

    def base_inputs(self, i, j, k, h):
        p = self.p
        n = self.starts[0] + (i * p.nb + j) * p.nz + k
        r = self.r1.at[i, j, k]
        return [(self.half(self.block(i, j, k), h), None), (self.half(r, h), self.arrived((1, i, j, k), r, n))]

    def two(self, h, far, near, k):
        p = self.p
        if h == 0:
            r, n = self.r2b.at[far - 1, near, k], self.starts[1] + ((far - 1) * p.na + near) * p.nz + k
        else:
            r, n = self.r2a.at[far - 1, near, k], self.starts[2] + ((far - 1) * p.nb + near) * p.nz + k
        return r, n

    def three(self, h, far, k):
        p = self.p
        if h == 0:
            return self.r3a.at[far - 1, k], self.starts[3] + (far - 1) * p.nz + k
        return self.r3b.at[far - 1, k], self.starts[4] + (far - 1) * p.nz + k

    def four(self, h, k):
        return self.half(self.r4.at[k - 1], h), self.starts[5] + 2 * (k - 1) + h

    def stage2(self, k):
        p, jobs = self.p, []
        for far, near in [(f, n) for n in range(max(p.na, p.nb)) for f in range(1, max(p.na, p.nb))]:
            if far < p.nb and near < p.na:
                r, n = self.two(0, far, near, k)
                own = self.half(self.r1.at[near, far, k], 0)
                jobs.append((self.base_inputs(near, far, k, 0), (own, r, n, p.to(j=far))))
            if far < p.na and near < p.nb:
                r, n = self.two(1, far, near, k)
                own = self.half(self.r1.at[far, near, k], 1)
                jobs.append((self.base_inputs(far, near, k, 1), (own, r, n, p.to(i=far))))
        return jobs

    def with_two(self, h, near, k):
        p = self.p
        i, j = (near, 0) if h == 0 else (0, near)
        got = self.base_inputs(i, j, k, h)
        for far in range(1, p.nb if h == 0 else p.na):
            r, n = self.two(h, far, near, k)
            got.append((r, self.arrived((2, h, far, near, k), r, n)))
        return got

    def stage3(self, k):
        p, jobs = self.p, []
        for near in range(1, max(p.na, p.nb)):
            if near < p.na:
                r, n = self.three(0, near, k)
                own = self.half(self.r1.at[near, 0, k], 0)
                jobs.append((self.with_two(0, near, k), (own, r, n, p.to(i=near))))
            if near < p.nb:
                r, n = self.three(1, near, k)
                own = self.half(self.r1.at[0, near, k], 1)
                jobs.append((self.with_two(1, near, k), (own, r, n, p.to(j=near))))
        return jobs

    def with_three(self, h, k):
        p = self.p
        got = self.with_two(h, 0, k)
        for far in range(1, p.na if h == 0 else p.nb):
            r, n = self.three(h, far, k)
            got.append((r, self.arrived((3, h, far, k), r, n)))
        return got

    def stage4(self, k, last):
        p, jobs = self.p, []
        if last != (k == 0):
            return jobs
        for h in range(2):
            got = self.with_three(h, k)
            if k:
                r, n = self.four(h, k)
                own = self.half(self.r1.at[0, 0, k], h)
                jobs.append((got, (own, r, n, p.to(k=k))))
            else:
                for far in range(1, p.nz):
                    r, n = self.four(h, far)
                    got.append((r, self.arrived((4, h, far), r, n)))
                jobs.append((got, self.half(self.out, h)))
        return jobs

    def start(self, k):
        p = self.p
        for i in reversed(range(p.na)):
            for j in reversed(range(p.nb)):
                self.sibling(i, j, k).start()

    def finish(self, k):
        p = self.p
        for i in range(p.na):
            for j in range(p.nb):
                self.sibling(i, j, k).wait_send()


class Worker:
    def __init__(self, ins, outbuf, finbuf, load, put, fin, send, recv):
        self.ins, self.outbuf, self.finbuf = ins, outbuf, finbuf
        self.load, self.put, self.fin, self.send, self.recv = load, put, fin, send, recv
        self.room = outbuf.shape[1]
        self.jobs, self.loaded, self.ran = [], 0, 0
        self.puts, self.n_out = [], 0
        self.sends = []

    def add(self, jobs):
        self.jobs.extend(jobs)

    def place(self, j, n, rows):
        return self.ins[j % 2].at[pl.ds(n * self.room, rows)]

    def loading(self, j, n):
        ref, _ = self.jobs[j][0][n]
        return pltpu.make_async_copy(ref, self.place(j, n, ref.shape[0]), self.load.at[j % 2, n])

    def fetch(self, j):
        inputs, _ = self.jobs[j]
        for n, (ref, arrived) in enumerate(inputs):
            if arrived is not None:
                if n > 1:
                    self.forward(0)
                arrived.wait_recv()
            self.loading(j, n).start()
        self.loaded = j + 1

    def forward(self, left):
        while len(self.puts) > left:
            put, out = self.puts.pop(0)
            put.wait()
            self.sending(out).start()
            self.sends.append(out)

    def sending(self, out):
        own, r, n, where = out
        return pltpu.make_async_remote_copy(
            src_ref=own,
            dst_ref=r,
            send_sem=self.send.at[n],
            recv_sem=self.recv.at[n],
            device_id=where,
            device_id_type=MESH,
        )

    def run(self, j):
        inputs, out = self.jobs[j]
        rows = inputs[0][0].shape[0]
        for n in range(len(inputs)):
            self.loading(j, n).wait()
        final = not isinstance(out, tuple)
        if final:
            target = self.finbuf
        else:
            self.forward(OUTS - 1)
            s = self.n_out % OUTS
            self.n_out += 1
            target = self.outbuf.at[s]
        source, count, room = self.ins[j % 2], len(inputs), self.room

        def body(t, carry):
            acc = source[pl.ds(pl.multiple_of(t * 16, 16), 16)].astype(jnp.float32)
            for n in range(1, count):
                at = pl.ds(pl.multiple_of(n * room + t * 16, 16), 16)
                acc = acc + source[at].astype(jnp.float32)
            target[pl.ds(pl.multiple_of(t * 16, 16), 16)] = acc.astype(target.dtype)
            return carry

        lax.fori_loop(0, rows // 16, body, 0)
        if final:
            c = pltpu.make_async_copy(target.at[pl.ds(0, rows)], out, self.fin.at[0])
            c.start()
            c.wait()
        else:
            c = pltpu.make_async_copy(target.at[pl.ds(0, rows)], out[0], self.put.at[s])
            c.start()
            self.puts.append((c, out))
            self.forward(1)

    def drain(self):
        for j in range(self.ran, len(self.jobs)):
            if self.loaded <= j:
                self.fetch(j)
            if j + 1 < len(self.jobs):
                self.fetch(j + 1)
            self.run(j)
            self.ran = j + 1
        self.forward(0)

    def finish(self):
        for out in self.sends:
            self.sending(out).wait_send()

CHUNK = 512
CAP = 32
ORDER = True


def experts_kernel(shape, local, *refs):
    na, nb, nz = shape
    x, small, _, place, choice_t, wg_hbm, wu_hbm, wd_hbm = refs[:8]
    dx_sum, y_part, xs_out, gs_out, hs_out, gu_out = refs[8:14]
    x_all, small_all, dx_part = refs[14:17]
    dx_bufs = refs[17:23]
    (wg, wu, wd, xs, gs, xin, gin, pin, sin, cin, ybuf, dbuf, gate, score, hkeep, gkeep, inbuf, outbuf, finbuf) = refs[23:42]
    (wsem, insem, savesem, keepsem, ownsem, outsem, load, put, fin, ag_send, ag_recv, ag_local, rs_send, rs_recv) = refs[42:]
    g_all = y_part
    p = Place(shape)
    length, width = x.shape
    planes = na * nb * 2
    slots = CAP
    many = planes * slots
    first = lax.axis_index("exp") * local
    greet(p)
    weights = [pltpu.make_async_copy(a, b, wsem.at[n]) for n, (a, b) in enumerate(((wg_hbm, wg), (wu_hbm, wu), (wd_hbm, wd)))]
    for w in weights:
        w.start()
    ga = Gather(p, x, x_all, ag_send, ag_recv, ag_local.at[0])
    gb = Gather(p, small, small_all, ag_send, ag_recv, ag_local.at[1], ga.end)
    both = (gb, ga)
    sd = Scatter(p, dx_part, dx_sum, dx_bufs, rs_send, rs_recv)
    work = Worker((inbuf.at[0], inbuf.at[1]), outbuf, finbuf, load, put, fin, rs_send, rs_recv)
    far = [*range(1, nz)]
    order = [*far, 0] if ORDER else [0, *far]
    hooks = {}
    if ORDER:
        early = [("turn", 0), ("arrive", far[0]), ("close", 0), ("turn", far[0]), ("close", far[0])]
        for t, k in enumerate(far[1:]):
            hooks[t, 0], hooks[t, 1], hooks[t, 2] = [("arrive", k)], [("turn", k)], [("close", k)]
    else:
        early = [("turn", 0), ("arrive", far[0]), ("close", 0)]
        for t, k in enumerate(far):
            hooks[t, 0], hooks[t, 2] = [("turn", k)], [("close", k)]
            if t + 1 < len(far):
                hooks[t, 3 if t == 0 else 1] = [("arrive", far[t + 1])]

    def step(name, k):
        for g in both:
            getattr(g, name)(k)

    for g in both:
        g.begin()
        g.launch(far[0])
    for k in far[1:]:
        for g in both:
            g.launch(k)
    for h in early:
        step(*h)
    for g in both:
        g.own().wait()

    def device(r, k):
        return r * nz + p.zs[k]

    def spots(s):
        at = pin[s]
        slot = lax.broadcasted_iota(jnp.int32, (slots, length), 0)
        rows = [jnp.where(at[e : e + 1] == slot, 1.0, 0.0) for e in range(local)]
        return rows, jnp.concatenate(rows, axis=0).astype(jnp.bfloat16)

    def dispatch(k):
        def loads(r, s):
            d = device(r, k)
            pairs = (
                (x_all.at[d], xin),
                (g_all.at[d, pl.ds(0, length)], gin),
                (place.at[d], pin),
                (small_all.at[d], sin),
                (choice_t.at[d], cin),
            )
            return [pltpu.make_async_copy(a, b.at[s], insem.at[s, n]) for n, (a, b) in enumerate(pairs)]

        def item(r, s):
            for c in loads(r, s):
                c.wait()
            masks, spot = spots(s)
            for n in range(0, width, CHUNK):
                for source, target in ((xin, xs), (gin, gs)):
                    rows = jnp.dot(spot, source[s, :, n : n + CHUNK], preferred_element_type=jnp.float32).astype(jnp.bfloat16)
                    for e in range(local):
                        at = pl.ds(pl.multiple_of(e * many + r * slots, slots), slots)
                        target[at, n : n + CHUNK] = rows[e * slots : (e + 1) * slots]
            chosen = cin[s]
            gates = sin[s].astype(jnp.float32)
            gates = gates[0:8, 0:length] + gates[8:16, 0:length]
            for e in range(local):
                weight = jnp.sum(jnp.where(chosen == first + e, gates, 0.0), axis=0, keepdims=True)
                value = jnp.sum(masks[e] * weight, axis=1, keepdims=True)
                gate[e, pl.ds(pl.multiple_of(r * slots, slots), slots)] = jnp.broadcast_to(value, (slots, 128))

        for c in loads(0, 0):
            c.start()

        def body(t, carry):
            for c in loads(2 * t + 1, 1):
                c.start()
            item(2 * t, 0)

            @pl.when(t < planes // 2 - 1)
            def _():
                for c in loads(2 * t + 2, 0):
                    c.start()

            item(2 * t + 1, 1)
            return carry

        lax.fori_loop(0, planes // 2, body, 0)

    def saves(k, e):
        at = pl.ds(pl.multiple_of(e * many, many), many)
        return [pltpu.make_async_copy(a.at[at], b.at[e, k], savesem.at[n, e]) for n, (a, b) in enumerate(((xs, xs_out), (gs, gs_out)))]

    def keeps(k, e, s):
        pairs = ((hkeep, hs_out), (gkeep, gu_out))
        return [pltpu.make_async_copy(a.at[s], b.at[e, k], keepsem.at[s, n]) for n, (a, b) in enumerate(pairs)]

    def expert(k, e, s):
        at = pl.ds(pl.multiple_of(e * many, many), many)
        rows = xs[at]
        gate_act = jnp.dot(rows, wg[e], preferred_element_type=jnp.float32)
        up_act = jnp.dot(rows, wu[e], preferred_element_type=jnp.float32)
        back = lax.dot_general(gs[at], wd[e], (((1,), (1,)), ((), ())), preferred_element_type=jnp.float32)
        weight = gate[e][:, 0:1]
        sig = jax.nn.sigmoid(gate_act)
        silu = gate_act * sig
        hidden = silu * up_act
        score[e] = jnp.broadcast_to(jnp.sum(hidden * back, axis=1, keepdims=True), (many, 128))
        grad = back * weight
        hs = (hidden * weight).astype(jnp.bfloat16)
        gu = (grad * silu).astype(jnp.bfloat16)
        gg = (grad * up_act * sig * (1.0 + gate_act * (1.0 - sig))).astype(jnp.bfloat16)
        hkeep[s] = hs
        gkeep[s] = jnp.concatenate([gg, gu], axis=1)
        for c in keeps(k, e, s):
            c.start()
        for c in saves(k, e):
            c.wait()
        for n in range(0, width, CHUNK):
            y = jnp.dot(hs, wd[e, :, n : n + CHUNK], preferred_element_type=jnp.float32)
            gs[at, n : n + CHUNK] = y.astype(jnp.bfloat16)
            form = (((1,), (1,)), ((), ()))
            dx = lax.dot_general(gg, wg[e, n : n + CHUNK], form, preferred_element_type=jnp.float32)
            dx = dx + lax.dot_general(gu, wu[e, n : n + CHUNK], form, preferred_element_type=jnp.float32)
            xs[at, n : n + CHUNK] = dx.astype(jnp.bfloat16)

    def experts(k, start, stop):
        def body(t, carry):
            for s in range(2):
                e = 2 * t + s

                @pl.when(e >= 2)
                def _():
                    for c in keeps(k, e - 2, s):
                        c.wait()

                expert(k, e, s)
            return carry

        lax.fori_loop(start // 2, stop // 2, body, 0)

    def combine(k):
        def at_offset(t, s):
            t = jnp.int32(t)
            i, j = lax.div(t, nb), lax.rem(t, nb)
            c = p.c if s else 1 - p.c
            return i, j, (xor_two(p.a, i, na) * nb + xor_two(p.b, j, nb)) * 2 + c

        def loads(t, s):
            r = at_offset(t, s)[2]
            d = device(r, k)
            return pltpu.make_async_copy(place.at[d], pin.at[s], insem.at[s, 0])

        def store_y(t, s):
            r = at_offset(t, s)[2]
            out = y_part.at[device(r, k), pl.ds(0, length)]
            return pltpu.make_async_copy(ybuf.at[s], out, ownsem.at[s])

        def store_dx(t, s):
            t = jnp.int32(t)
            i, j, _ = at_offset(t, s)
            if s:
                return pltpu.make_async_copy(dbuf.at[2], sd.block(i, j, k), outsem.at[0])
            n = sd.starts[0] + t * nz + k
            return sd.copy(dbuf.at[lax.rem(t, 2)], sd.r1.at[i, j, k], n, p.to(s=1))

        def item(t, s):
            r = at_offset(t, s)[2]
            loads(t, s).wait()

            @pl.when(t > 0)
            def _():
                store_y(t - 1, s).wait()
                if s:
                    store_dx(t - 1, s).wait()

            if not s:

                @pl.when(t > 1)
                def _():
                    store_dx(t - 2, s).wait_send()

            d = 2 if s else lax.rem(t, 2)
            masks, _ = spots(s)
            spot = jnp.concatenate(masks, axis=0).T.astype(jnp.bfloat16)
            for source, out in ((gs, ybuf.at[s]), (xs, dbuf.at[d])):
                for n in range(0, width, CHUNK):
                    rows = [
                        source[pl.ds(pl.multiple_of(e * many + r * slots, slots), slots), n : n + CHUNK]
                        for e in range(local)
                    ]
                    rows = jnp.concatenate(rows, axis=0)
                    total = jnp.dot(spot, rows, preferred_element_type=jnp.float32)
                    out[0:length, n : n + CHUNK] = total.astype(jnp.bfloat16)
            row = lax.broadcasted_iota(jnp.int32, (8, length), 0)
            table = jnp.zeros((8, length), jnp.float32)
            for e in range(local):
                value = score[e, pl.ds(pl.multiple_of(r * slots, slots), slots)][:, 0:1]
                line = jnp.sum(masks[e] * value, axis=0, keepdims=True)
                table = jnp.where(row == (first + e) % 8, line, table)
            table = jnp.concatenate([table, jnp.zeros((8, length), jnp.float32)], axis=0)
            table = jnp.concatenate([table, jnp.zeros((16, 256 - length), jnp.float32)], axis=1)
            dbuf[d, length : length + 16] = jnp.zeros((16, width), jnp.bfloat16)
            at = pl.ds(pl.multiple_of(first // 8 * 256, 256), 256)
            dbuf[d, length : length + 16, at] = table.astype(jnp.bfloat16)
            store_y(t, s).start()
            store_dx(t, s).start()

        loads(0, 0).start()

        def body(t, carry):
            loads(t, 1).start()
            item(t, 0)

            @pl.when(t < na * nb - 1)
            def _():
                loads(t + 1, 0).start()

            item(t, 1)
            return carry

        lax.fori_loop(0, na * nb, body, 0)
        last = na * nb - 1
        for s in range(2):
            store_y(last, s).wait()
        store_dx(last, 1).wait()
        for t in range(max(0, last - 1), last + 1):
            store_dx(t, 0).wait_send()

    def add(jobs):
        work.add(jobs)
        work.drain()

    for t, k in enumerate(order):
        for g in both:
            g.plane(k)
        dispatch(k)
        for e in range(local):
            for c in saves(k, e):
                c.start()
        for h in hooks.get((t, 0), []):
            step(*h)
        if t == 0:
            for w in weights:
                w.wait()
        half = local // 4 * 2
        if half:
            experts(k, 0, half)
        for h in hooks.get((t, 1), []):
            step(*h)
        if t:
            add(sd.stage3(order[t - 1]))
        experts(k, half, local)
        for s in range(2):
            for c in keeps(k, local - 2 + s, s):
                c.wait()
        for h in hooks.get((t, 2), []):
            step(*h)
        combine(k)
        add((sd.stage4(order[t - 1], False) if t else []) + sd.stage2(k))
        for h in hooks.get((t, 3), []):
            step(*h)
    add(sd.stage3(order[-1]))
    add(sd.stage4(order[-1], False))
    add(sd.stage4(0, True))
    work.finish()
    for g in both:
        g.finish()


def run_experts(shape, x, small, g_all, place, choice_t, wg, wu, wd, collective_id):
    na, nb, nz = shape
    local, width, hidden = wg.shape
    length = x.shape[0]
    planes = na * nb * 2
    many = planes * CAP
    tall = length + 16
    low, wide = jnp.bfloat16, jnp.float32
    any_ = pl.BlockSpec(memory_space=pl.ANY)
    sds = jax.ShapeDtypeStruct
    outs = [sds((tall, width), wide), sds(g_all.shape, low)]
    outs += [sds((local, nz, many, width), low)] * 2 + [sds((local, nz, many, n * hidden), low) for n in (1, 2)]
    outs += [sds((g_all.shape[0],) + x.shape, low), sds((g_all.shape[0],) + small.shape, low)]
    outs += [sds((na, nb, nz, tall, width), low)]
    counts, buffers = rs_layout(shape, tall)
    total = sum(counts)
    outs += [sds(b + (width,), low) for b in buffers]
    messages = 2 * ag_count(shape)
    room = tall - tall // 32 * 16
    inputs = na + nb + nz - 1
    dma = pltpu.SemaphoreType.DMA
    got = pl.pallas_call(
        functools.partial(experts_kernel, shape, local),
        out_shape=outs,
        in_specs=[any_] * 8,
        out_specs=[any_] * len(outs),
        input_output_aliases={2: 1},
        scratch_shapes=[
            pltpu.VMEM((local, width, hidden), low),
            pltpu.VMEM((local, width, hidden), low),
            pltpu.VMEM((local, hidden, width), low),
            pltpu.VMEM((local * many, width), low),
            pltpu.VMEM((local * many, width), low),
            pltpu.VMEM((2, length, width), low),
            pltpu.VMEM((2, length, width), low),
            pltpu.VMEM((2,) + place.shape[1:], jnp.int32),
            pltpu.VMEM((2,) + small.shape, low),
            pltpu.VMEM((2,) + choice_t.shape[1:], jnp.int32),
            pltpu.VMEM((2, length, width), low),
            pltpu.VMEM((3, tall, width), low),
            pltpu.VMEM((local, many, 128), wide),
            pltpu.VMEM((local, many, 128), wide),
            pltpu.VMEM((2, many, hidden), low),
            pltpu.VMEM((2, many, 2 * hidden), low),
            pltpu.VMEM((2, inputs * room, width), low),
            pltpu.VMEM((OUTS, room, width), low),
            pltpu.VMEM((room, width), wide),
            dma((3,)),
            dma((2, 5)),
            dma((2, local)),
            dma((2, 2)),
            dma((2,)),
            dma((2,)),
            dma((2, inputs)),
            dma((OUTS,)),
            dma((1,)),
            dma((messages,)),
            dma((messages,)),
            dma((2,)),
            dma((total,)),
            dma((total,)),
        ],
        compiler_params=pltpu.CompilerParams(
            collective_id=collective_id, has_side_effects=True, vmem_limit_bytes=63 << 20
        ),
    )(x, small, g_all, place, choice_t, wg, wu, wd)
    return got[:6]

HEADS = 16
HEAD_DIM = 128
EXPERTS = 64
epsilon = 1e-05
masked_value = -1e30
low = jnp.bfloat16
wide = jnp.float32
ROWS_OUT = (((1,), (1,)), ((), ()))


def factor_of(values):
    return lax.rsqrt(jnp.mean(values * values, axis=-1, keepdims=True) + epsilon)


def swapped(v):
    half = v.shape[1] // 2
    return jnp.concatenate([v[:, half:], v[:, :half]], axis=1)


def front_kernel(shape, *refs):
    na, nb, nz = shape
    tokens, allowed, cosine, sine, choice = refs[:5]
    shards = refs[5:12]
    alls = refs[12:19]
    normed_f, normed_ft, normed_at, attended_t, gates, residual, q_raw, k_raw, q_low, k_low, v_low, probs, router_p, gains = refs[19:33]
    wq, wk, wv, wo, router, smalls, normed, attended, wsem, send, recv, local = refs[33:]
    p = Place(shape)
    length, width = tokens.shape
    greet(p)
    gs, base = [], 0
    for i in range(7):
        g = Gather(p, shards[i], alls[i], send, recv, local.at[i], base)
        base = g.end
        gs.append(g)
    weights, late = gs[:6], gs[6]

    def begin(g):
        g.begin()
        for k in range(1, nz):
            g.launch(k)

    for g in weights:
        begin(g)
    for k in range(1, nz):
        for g in weights:
            g.arrive(k)
            g.turn(k - 1)
    for g in weights:
        g.turn(nz - 1)
    begin(late)
    for k in range(nz):
        for g in weights:
            g.close(k)
    copies = []
    for n, (g, target) in enumerate(zip(weights, (smalls, router, wq, wk, wv, wo))):
        g.own().wait()
        for k in range(nz):
            g.plane(k)
        c = pltpu.make_async_copy(alls[n], target, wsem.at[n])
        c.start()
        copies.append(c)

    copies[0].wait()
    devices = smalls.shape[0]

    def total(d, carry):
        gains[...] += smalls[d].astype(wide)
        return carry

    gains[...] = jnp.zeros((16, width), wide)
    lax.fori_loop(0, devices, total, 0)
    x = tokens[...].astype(wide)
    scaled = x * factor_of(x) * gains[0:1]
    normed[...] = scaled.astype(low)

    def transposed(source, target):
        def body(n, carry):
            at = pl.ds(pl.multiple_of(n * 256, 256), 256)
            target[at] = source[:, at].astype(wide).T.astype(low)
            return carry

        lax.fori_loop(0, width // 256, body, 0)

    def product(left, right, out, more=None):
        def body(n, carry):
            at = pl.ds(pl.multiple_of(n * 512, 512), 512)
            got = jnp.dot(left[...], right[:, :, at].reshape(width, 512), preferred_element_type=wide)
            if more is not None:
                got = got + more[:, at].astype(wide)
            out[:, at] = got.astype(out.dtype)
            return carry

        lax.fori_loop(0, width // 512, body, 0)

    copies[2].wait()
    product(normed, wq, q_raw)
    copies[3].wait()
    product(normed, wk, k_raw)
    copies[4].wait()
    product(normed, wv, v_low)
    late.turn(0)
    transposed(normed, normed_at)
    factor_q = factor_of(q_raw[...])
    factor_k = factor_of(k_raw[...])

    def head(h, carry):
        at = pl.ds(pl.multiple_of(h * HEAD_DIM, HEAD_DIM), HEAD_DIM)

        def turned(raw, factor, gain):
            v = raw[:, at] * factor * gain[:, at]
            return (v * cosine[...] + swapped(v) * sine[...]).astype(low)

        q = turned(q_raw, factor_q, gains.at[1:2])
        k = turned(k_raw, factor_k, gains.at[2:3])
        q_low[:, at] = q
        k_low[:, at] = k
        scores = lax.dot_general(q, k, ROWS_OUT, preferred_element_type=wide) * HEAD_DIM ** (-0.5)
        scores = jnp.where(allowed[...] > 0.0, scores, masked_value)
        e = jnp.exp(scores - jnp.max(scores, axis=-1, keepdims=True))
        e = e / jnp.sum(e, axis=-1, keepdims=True)
        probs[h] = e
        out = jnp.dot(e.astype(low), v_low[:, at], preferred_element_type=wide)
        attended[:, at] = out.astype(low)
        return carry

    lax.fori_loop(0, HEADS, head, 0)
    late.arrive(1)
    copies[5].wait()
    product(attended, wo, residual, tokens)
    late.turn(1)
    r = residual[...]
    normed_f[...] = (r * factor_of(r) * gains[3:4]).astype(low)
    copies[1].wait()
    logits = jnp.dot(normed_f[...], router[...].reshape(width, 128), preferred_element_type=wide)
    logits = logits.T[0:EXPERTS]
    e = jnp.exp(logits - jnp.max(logits, axis=0, keepdims=True))
    chances = e / jnp.sum(e, axis=0, keepdims=True)
    router_p[...] = chances
    expert = lax.broadcasted_iota(jnp.int32, (EXPERTS, length), 0)
    rows = [
        jnp.sum(jnp.where(expert == choice[n : n + 1], chances, 0.0), axis=0, keepdims=True)
        for n in range(choice.shape[0])
    ]
    rows = jnp.concatenate(rows, axis=0)
    upper = rows.astype(low).astype(wide)
    rows = jnp.concatenate([upper, rows - upper], axis=0)
    rows = jnp.concatenate([rows, jnp.zeros((16, gates.shape[1] - length), wide)], axis=1)
    gates[...] = rows.astype(low)
    late.close(0)
    transposed(attended, attended_t)
    transposed(normed_f, normed_ft)
    for k in range(2, nz):
        late.arrive(k)
        late.close(k - 1)
        late.turn(k)
    late.close(nz - 1)
    late.own().wait()
    for k in range(nz):
        late.plane(k)
    for g in gs:
        g.finish()


def run_front(shape, tokens, allowed, cosine, sine, choice, shards, collective_id):
    na, nb, nz = shape
    length, width = tokens.shape
    devices = na * nb * nz * 2
    any_, vmem = pl.BlockSpec(memory_space=pl.ANY), pl.BlockSpec(memory_space=pltpu.VMEM)
    sds = jax.ShapeDtypeStruct
    alls = [sds((devices,) + s.shape, low) for s in shards]
    row, tall = (length, width), (width, length)
    outs = [sds(row, low), sds(tall, low), sds(tall, low), sds(tall, low)]
    outs += [sds((16, -length % 256 + length), low), sds(row, wide), sds(row, wide), sds(row, wide)]
    outs += [sds(row, low), sds(row, low), sds(row, low), sds((HEADS, length, length), wide)]
    outs += [sds((EXPERTS, length), wide), sds((16, width), wide)]
    count = ag_count(shape) * len(shards)
    got = pl.pallas_call(
        functools.partial(front_kernel, shape),
        out_shape=alls + outs,
        in_specs=[vmem] * 5 + [any_] * 7,
        out_specs=[any_] * 7 + [vmem] * len(outs),
        scratch_shapes=[pltpu.VMEM(alls[n].shape, low) for n in (2, 3, 4, 5, 1, 0)]
        + [
            pltpu.VMEM(row, low),
            pltpu.VMEM(row, low),
            pltpu.SemaphoreType.DMA((6,)),
            pltpu.SemaphoreType.DMA((count,)),
            pltpu.SemaphoreType.DMA((count,)),
            pltpu.SemaphoreType.DMA((7,)),
        ],
        compiler_params=pltpu.CompilerParams(
            collective_id=collective_id, has_side_effects=True, vmem_limit_bytes=63 << 20
        ),
    )(tokens, allowed, cosine, sine, choice, *shards)
    return got[:7], got[7:]


FIRST = (((0,), (0,)), ((), ()))


def last_kernel(shape, part, *refs):
    na, nb, nz = shape
    tokens, out_grad, residual, q_raw, k_raw, q_low, k_low, v_low = refs[:8]
    normed_at, attended_t, normed_ft, router, gains, router_p, dx_in, cosine, sine = refs[8:17]
    y_part, probs, wq, wk, wv, wo, xs, gs, hs, gu = refs[17:27]
    y_sum, w_sum, input_grad, dwg, dwu, dwd, w_part = refs[27:34]
    y_bufs, w_bufs = refs[34:40], refs[40:46]
    flat, xin, gin, hin, uin, outbuf, finbuf, grads = refs[46:54]
    wsem, psem, isem, outsem, insem, savesem, load, put, fin, send, recv = refs[54:]
    p = Place(shape)
    greet(p)
    length, width = y_sum.shape
    rows = 4 * part
    tall = rows + 16
    sy = Scatter(p, y_part, y_sum, y_bufs, send, recv)
    sw = Scatter(p, w_part, w_sum, w_bufs, send, recv, sy.end)
    half = flat.shape[0] // 2
    ins = (flat.at[pl.ds(0, half)], flat.at[pl.ds(half, half)])
    work = Worker(ins, outbuf, finbuf, load, put, fin, send, recv)
    local, chunks = xs.shape[:2]
    hidden = hs.shape[3]
    order = [*range(1, nz), 0]

    def weight(source, target, n):
        return pltpu.make_async_copy(source, target, wsem.at[n])

    def back_product(left, matrix, out, kind):
        def body(n, carry):
            at = pl.ds(pl.multiple_of(n * 512, 512), 512)
            part_of = matrix[lax.div(n, 2), pl.ds(pl.multiple_of(lax.rem(n, 2) * 512, 512), 512)]
            got = lax.dot_general(left[...], part_of, ROWS_OUT, preferred_element_type=wide)
            if kind == "add":
                got = got + out[:, at]
            out[:, at] = got.astype(out.dtype)
            return carry

        lax.fori_loop(0, width // 512, body, 0)

    def norm_back(grad, unit, factor, gain):
        m = grad * gain
        return factor * (m - unit * jnp.mean(m * unit, axis=-1, keepdims=True))

    pieces = [(e, c) for e in range(local) for c in range(chunks)]

    def loads(n):
        e, c = pieces[n]
        pairs = ((xs, xin), (gs, gin), (hs, hin), (gu, uin))
        return [pltpu.make_async_copy(a.at[e, c], b.at[n % 2], insem.at[n % 2, m]) for m, (a, b) in enumerate(pairs)]

    def early(work_a, res_grad, k_grad, res_low, att_grad, dq, dk, dv, llow, pin):
        def back_ffn():
            weight(wo, xin, 0).start()
            weight(wv, gin, 1).start()
            wide_table = dx_in[length : length + 8]
            table = [wide_table[:, n * 256 : n * 256 + length] for n in range(EXPERTS // 8)]
            table = jnp.concatenate(table, axis=0)
            chances = router_p[...]
            grad = chances * (table - jnp.sum(chances * table, axis=0, keepdims=True))
            grad = jnp.concatenate([grad, jnp.zeros((128 - EXPERTS, length), wide)], axis=0)
            llow[...] = grad.T.astype(low)
            for n in range(0, width, 512):
                got = lax.dot_general(
                    llow[...], router[n : n + 512], ROWS_OUT, preferred_element_type=wide
                )
                work_a[:, n : n + 512] = got + dx_in[0:length, n : n + 512]
            factor = factor_of(residual[...])
            unit = residual[...] * factor
            grad = work_a[...]
            grads[3:4] = jnp.sum(grad * unit, axis=0, keepdims=True)
            got = out_grad[...].astype(wide) + norm_back(grad, unit, factor, gains[3:4])
            res_grad[...] = got
            res_low[...] = got.astype(low)
            weight(wo, xin, 0).wait()
            back_product(res_low, xin, att_grad, "set")
            weight(wq, xin, 0).start()

        def back_heads():
            def prob(h, s):
                return pltpu.make_async_copy(probs.at[h], pin.at[s], psem.at[s])

            prob(0, 0).start()

            def one(h, s):
                @pl.when(h + 1 < HEADS)
                def _():
                    prob(h + 1, 1 - s).start()

                prob(h, s).wait()
                at = pl.ds(pl.multiple_of(h * HEAD_DIM, HEAD_DIM), HEAD_DIM)
                grad, q, k, v = att_grad[:, at], q_low[:, at], k_low[:, at], v_low[:, at]
                chances = pin[s]
                got = lax.dot_general(chances.astype(low), grad, FIRST, preferred_element_type=wide)
                dv[:, at] = got.astype(low)
                inner = lax.dot_general(grad, v, ROWS_OUT, preferred_element_type=wide)
                inner = chances * (inner - jnp.sum(chances * inner, axis=-1, keepdims=True))
                inner = inner.astype(low)
                scale = HEAD_DIM ** (-0.5)

                def turned_back(x):
                    return x * cosine[...] - swapped(x) * sine[...]

                got = jnp.dot(inner, k, preferred_element_type=wide) * scale
                work_a[:, at] = turned_back(got)
                got = lax.dot_general(inner, q, FIRST, preferred_element_type=wide) * scale
                k_grad[:, at] = turned_back(got)

            def body(t, carry):
                one(2 * t, 0)
                one(2 * t + 1, 1)
                return carry

            lax.fori_loop(0, HEADS // 2, body, 0)

        def back_inputs():
            for raw, grad, out, n in ((q_raw, work_a, dq, 1), (k_raw, k_grad, dk, 2)):
                factor = factor_of(raw[...])
                unit = raw[...] * factor
                grads[n : n + 1] = jnp.sum(grad[...] * unit, axis=0, keepdims=True)
                out[...] = norm_back(grad[...], unit, factor, gains[n : n + 1]).astype(low)
            weight(wv, gin, 1).wait()
            back_product(dv, gin, work_a, "set")
            weight(wk, gin, 1).start()
            weight(wq, xin, 0).wait()
            back_product(dq, xin, work_a, "add")
            weight(wk, gin, 1).wait()
            back_product(dk, gin, work_a, "add")
            x = tokens[...].astype(wide)
            factor = factor_of(x)
            unit = x * factor
            grad = work_a[...]
            grads[0:1] = jnp.sum(grad * unit, axis=0, keepdims=True)
            res_grad[...] = res_grad[...] + norm_back(grad, unit, factor, gains[0:1])
            c = pltpu.make_async_copy(res_grad, input_grad, isem.at[0])
            c.start()
            c.wait()
            for d in loads(0):
                d.start()

        def products():
            def start_of(s, z):
                return (s * nz + z) * tall

            def where(t, s):
                t = jnp.int32(t)
                i, j = lax.div(t, nb), lax.rem(t, nb)
                c = p.c if s else 1 - p.c
                return i, j, (xor_two(p.a, i, na) * nb + xor_two(p.b, j, nb)) * 2 + c

            def stores(t, s):
                i, j, _ = where(t, s)
                got = []
                for k in range(nz):
                    src = flat.at[pl.ds(pl.multiple_of(start_of(s, p.zs[k]), 16), tall)]
                    if s:
                        got.append(pltpu.make_async_copy(src, sw.block(i, j, k), outsem.at[k]))
                    else:
                        n = sw.starts[0] + t * nz + k
                        got.append(sw.copy(src, sw.r1.at[i, j, k], n, p.to(s=1)))
                return got

            def finish(t, s):
                for c in stores(t, s):
                    if s:
                        c.wait()
                    else:
                        c.wait_send()

            pairs = ((normed_at, dq), (normed_at, dk), (normed_at, dv), (attended_t, res_low))
            groups = part // 16

            def body(t, carry):
                for s in range(2):

                    @pl.when(t > 0)
                    def _():
                        finish(t - 1, s)

                    r = where(t, s)[2]
                    at = pl.ds(pl.multiple_of(r * nz * part, nz * part), nz * part)
                    for m, (left, right) in enumerate(pairs):
                        for n in range(0, width, 512):
                            got = jnp.dot(left[at], right[:, n : n + 512], preferred_element_type=wide)
                            got = got.astype(low)
                            for z in range(nz):
                                to = start_of(s, z) + m * part
                                flat[to : to + part, n : n + 512] = got[z * part : (z + 1) * part]
                    got = jnp.dot(normed_ft[at], llow[...], preferred_element_type=wide).astype(low)
                    for z in range(nz):
                        to = start_of(s, z) + rows
                        lanes = pl.ds(pl.multiple_of((r * nz + z) * part // 128 * 128, 128), 128)
                        gain = jnp.concatenate([grads[:, lanes], jnp.zeros((8, 128), wide)], axis=0)
                        flat[to : to + 16] = jnp.zeros((16, width), low)
                        for n in range(groups):
                            piece = got[z * part + n * 16 : z * part + (n + 1) * 16]
                            flat[to : to + 16, n * 128 : (n + 1) * 128] = piece
                        flat[to : to + 16, groups * 128 : (groups + 1) * 128] = gain.astype(low)
                    for c in stores(t, s):
                        c.start()
                return carry

            lax.fori_loop(0, na * nb, body, 0)
            for s in range(2):
                finish(na * nb - 1, s)

        steps_of = (back_ffn, back_heads, back_inputs, products)
        for kind, what in plan[:cut]:
            if kind == "add":
                add(what)
            else:
                steps_of[what]()

    def late(og, ou, od, accg, accd):
        def saves(e):
            s = e % og.shape[0]
            pairs = ((og, dwg), (ou, dwu), (od, dwd))
            return [pltpu.make_async_copy(a.at[s], b.at[e], savesem.at[s, m]) for m, (a, b) in enumerate(pairs)]

        def piece(n):
            e, c = pieces[n]
            s, o = n % 2, e % og.shape[0]
            if n + 1 < len(pieces):
                for d in loads(n + 1):
                    d.start()
            for d in loads(n):
                d.wait()
            if c == 0 and e >= og.shape[0]:
                for d in saves(e - og.shape[0]):
                    d.wait()
            form = (((0,), (0,)), ((), ()))

            def columns(t, carry):
                at = pl.ds(pl.multiple_of(t * 512, 512), 512)
                g = lax.dot_general(xin[s, :, at], uin[s], form, preferred_element_type=jnp.float32)
                d = lax.dot_general(hin[s], gin[s, :, at], form, preferred_element_type=jnp.float32)
                if c:
                    g = g + accg[at]
                    d = d + accd[:, at]
                if c + 1 < chunks:
                    accg[at] = g
                    accd[:, at] = d
                else:
                    og[o, at] = g[:, :hidden].astype(jnp.bfloat16)
                    ou[o, at] = g[:, hidden:].astype(jnp.bfloat16)
                    od[o, :, at] = d.astype(jnp.bfloat16)
                return carry

            lax.fori_loop(0, width // 512, columns, 0)
            if c + 1 == chunks:
                for d in saves(e):
                    d.start()

        for kind, what in plan[cut:]:
            if kind == "add":
                add(what)
            else:
                piece(what)
        for e in range(max(0, local - og.shape[0]), local):
            for d in saves(e):
                d.wait()

    def add(jobs):
        work.add(jobs)
        work.drain()

    grads[...] = jnp.zeros((8, width), wide)
    for k in order:
        sy.start(k)
    steps = [(s, k) for s in (sy, sw) for k in order]
    slow = 4
    plan, done, count, cut = [], 0, len(steps), 0
    for t in range(count + 2):
        if t < count:
            s, k = steps[t]
            plan.append(("add", s.stage2(k)))
        if t < slow:
            plan.append(("first", t))
            cut = len(plan)
        else:
            until = len(pieces) * (t - slow + 1) // (count - slow) if t < count else len(pieces)
            while done < until:
                plan.append(("piece", done))
                done += 1
        if 1 <= t <= count:
            s, k = steps[t - 1]
            plan.append(("add", s.stage3(k)))
        if 2 <= t:
            s, k = steps[t - 2]
            plan.append(("add", s.stage4(k, False)))
        if t == nz + 2:
            plan.append(("add", sy.stage4(0, True)))
    plan.append(("add", sw.stage4(0, True)))
    row, vmem = (length, width), pltpu.VMEM
    pl.run_scoped(
        early,
        *[vmem(row, wide)] * 3,
        *[vmem(row, low)] * 5,
        vmem((length, 128), low),
        vmem((2,) + probs.shape[1:], wide),
    )
    several = chunks > 1
    slots = 1 if several else 2
    pl.run_scoped(
        late,
        vmem((slots, width, hidden), low),
        vmem((slots, width, hidden), low),
        vmem((slots, hidden, width), low),
        vmem((width if several else 8, 2 * hidden), wide),
        vmem((hidden if several else 8, width), wide),
    )
    work.finish()
    for k in order:
        sy.finish(k)


def run_last(shape, part, vmem_in, any_in, collective_id):
    na, nb, nz = shape
    length, width = vmem_in[0].shape
    y_part, probs, wq, wk, wv, wo, xs, gs, hs, gu = any_in
    tall = 4 * part + 16
    local, hidden = xs.shape[0], hs.shape[3]
    total_slots = xs.shape[1] * xs.shape[2]
    deep = width // 2
    xs, gs, hs, gu = (a.reshape(local, total_slots // deep, deep, a.shape[3]) for a in (xs, gs, hs, gu))
    wq, wk, wv, wo = (a.reshape(2, deep, width) for a in (wq, wk, wv, wo))
    any_, vmem = pl.BlockSpec(memory_space=pl.ANY), pl.BlockSpec(memory_space=pltpu.VMEM)
    sds = jax.ShapeDtypeStruct
    outs = [sds((length, width), wide), sds((tall, width), wide), sds((length, width), wide)]
    outs += [sds((local, width, hidden), low)] * 2 + [sds((local, hidden, width), low)]
    outs += [sds((na, nb, nz, tall, width), low)]
    y_counts, y_buffers = rs_layout(shape, length)
    w_counts, w_buffers = rs_layout(shape, tall)
    total = sum(y_counts) + sum(w_counts)
    outs += [sds(b + (width,), low) for b in y_buffers + w_buffers]
    room = max(tall - tall // 32 * 16, length - length // 32 * 16)
    inputs = na + nb + nz - 1
    dma = pltpu.SemaphoreType.DMA
    got = pl.pallas_call(
        functools.partial(last_kernel, shape, part),
        out_shape=outs,
        in_specs=[vmem] * len(vmem_in) + [any_] * len(any_in),
        out_specs=[any_] * len(outs),
        scratch_shapes=[
            pltpu.VMEM((2 * max(nz * tall, inputs * room), width), low),
            pltpu.VMEM((2, deep, width), low),
            pltpu.VMEM((2, deep, width), low),
            pltpu.VMEM((2, deep, hidden), low),
            pltpu.VMEM((2, deep, 2 * hidden), low),
            pltpu.VMEM((OUTS, room, width), low),
            pltpu.VMEM((room, width), wide),
            pltpu.VMEM((8, width), wide),
            dma((2,)),
            dma((2,)),
            dma((1,)),
            dma((nz,)),
            dma((2, 4)),
            dma((2, 3)),
            dma((2, inputs)),
            dma((OUTS,)),
            dma((1,)),
            dma((total,)),
            dma((total,)),
        ],
        compiler_params=pltpu.CompilerParams(
            collective_id=collective_id, has_side_effects=True, vmem_limit_bytes=63 << 20
        ),
    )(*vmem_in, y_part, probs, wq, wk, wv, wo, xs, gs, hs, gu)
    return got[:6]

TOP = 8

base_freq = 10000.0


def rotary(length, head_width):
    positions = jnp.arange(length, dtype=jnp.float32)
    freqs = base_freq ** (-jnp.arange(head_width // 2, dtype=jnp.float32) * 2.0 / head_width)
    angles = positions[:, None] * freqs[None, :]
    return (jnp.cos(angles), jnp.sin(angles))


def ein(form, *values):
    return jnp.einsum(form, *values, preferred_element_type=wide)


def slot_table(choices, local):
    length = choices.shape[2]
    mine = lax.axis_index("exp") * local + jnp.arange(local)
    chosen = jnp.any(choices[:, None] == mine[:, None, None], axis=2)
    order = jnp.arange(length)
    before = (order[:, None] < order[None, :]).astype(low)
    ranks = ein("rjt,tu->rju", chosen.astype(low), before).astype(jnp.int32)
    return jnp.where(chosen, ranks, -1)


def on_device(
    shape,
    tokens,
    segment_ids,
    expert_choice,
    w_query,
    w_key,
    w_value,
    w_output,
    w_router,
    attn_gain,
    query_gain,
    key_gain,
    ffn_gain,
    w_gate,
    w_up,
    w_down,
    out_grad,
):
    length, width = tokens.shape
    part = w_query.shape[0]
    devices = width // part

    place = (lax.axis_index("exp") * lax.axis_size("hid") + lax.axis_index("hid")) * part
    small = jnp.stack([attn_gain, query_gain, key_gain, ffn_gain])
    small = lax.dynamic_update_slice(jnp.zeros((16, width), low), small, (0, place))
    listing = expert_choice.T
    flat = listing.reshape(1, -1).astype(low)
    small = lax.dynamic_update_slice(small, flat, (4, 0))
    router = jnp.pad(w_router, ((0, 0), (0, 128 - EXPERTS)))
    positions = jnp.arange(length)
    segment_row = segment_ids[0]
    allowed = (positions[:, None] >= positions[None, :]) & (
        segment_row[:, None] == segment_row[None, :]
    )
    cosine, sine = rotary(length, HEAD_DIM)
    shards = [small, router, w_query, w_key, w_value, w_output, out_grad]
    alls, saved = run_front(
        shape,
        tokens,
        allowed.astype(wide),
        jnp.concatenate([cosine, cosine], axis=1),
        jnp.concatenate([-sine, sine], axis=1),
        listing,
        shards,
        1,
    )
    small_all, router_all, query_all, key_all, value_all, output_all, g_all = alls
    normed_ffn, normed_ft, normed_at, attended_t, gates = saved[:5]
    residual, query_raw, key_raw, query_low, key_low, value_low, attn_probs, router_pt, gains = saved[5:]
    choices = small_all[:, 4, : length * TOP].reshape(devices, TOP, length).astype(jnp.int32)
    total_counts = jnp.sum(
        (choices.reshape(devices, -1)[:, None, :] == jnp.arange(EXPERTS)[:, None]).astype(jnp.int32),
        axis=2,
    )
    dx_sum, y_part, xs, gs, hs, gu = run_experts(
        shape,
        normed_ffn,
        gates,
        g_all,
        slot_table(choices, w_gate.shape[0]),
        choices,
        w_gate,
        w_up,
        w_down,
        2,
    )
    vmem_in = [
        tokens,
        out_grad,
        residual,
        query_raw,
        key_raw,
        query_low,
        key_low,
        value_low,
        normed_at,
        attended_t,
        normed_ft,
        router_all.reshape(width, -1),
        gains,
        router_pt,
        dx_sum,
        jnp.concatenate([cosine, cosine], axis=1),
        jnp.concatenate([-sine, sine], axis=1),
    ]
    any_in = [y_part, attn_probs, query_all, key_all, value_all, output_all, xs, gs, hs, gu]
    mixture, sums, input_grad, grad_wgate, grad_wup, grad_wdown = run_last(
        shape, part, vmem_in, any_in, 3
    )
    result = (residual + mixture).astype(low)
    small = sums[4 * part :]
    sums = sums[: 4 * part].reshape(4, part, width)
    lanes = part // 16 * 128
    sum_router = small[:, :lanes].reshape(16, -1, 128)[:, :, :EXPERTS].transpose(1, 0, 2)
    sum_router = sum_router.reshape(part, EXPERTS)
    sum_gains = lax.dynamic_slice(small, (0, lanes + place % 128), (4, part))
    return (
        result,
        input_grad,
        sums[0],
        sums[1],
        sums[2],
        sums[3],
        sum_router,
        sum_gains[0],
        sum_gains[1],
        sum_gains[2],
        sum_gains[3],
        grad_wgate.astype(wide),
        grad_wup.astype(wide),
        grad_wdown.astype(wide),
        total_counts,
    )


def solution(mesh):
    rows, both = P(("exp", "hid"), None), P(("exp", "hid"))
    shape = grid_of(mesh.shape["exp"], mesh.shape["hid"])
    experts = (P("exp", None, "hid"), P("exp", None, "hid"), P("exp", "hid", None))
    return jax.shard_map(
        functools.partial(on_device, shape),
        mesh=mesh,
        in_specs=(rows,) * 8 + (both,) * 4 + experts + (rows,),
        out_specs=(rows,) * 7 + (both,) * 4 + experts + (P(),),
        check_vma=False,
    )
```

```python
import functools
import math

import jax
import jax.numpy as jnp
from jax import lax
from jax.experimental import pallas as pl
from jax.experimental.pallas import tpu as pltpu
from jax.sharding import PartitionSpec as P

MESH = pl.DeviceIdType.MESH


def grid_of(exp, hid):
    plane = exp // 2
    na = 1 << (int(math.log2(plane)) // 2)
    return na, plane // na, hid


class Place:
    def __init__(self, shape):
        na, nb, nz = self.na, self.nb, self.nz = shape
        e = lax.axis_index("exp")
        self.z = lax.axis_index("hid")
        self.c = lax.rem(e, 2)
        self.b = lax.rem(lax.div(e, 2), nb)
        self.a = lax.div(e, 2 * nb)
        self.zs = [xor(self.z, k) for k in range(nz)]
        aa = [xor(self.a, i) for i in range(na)]
        bb = [xor(self.b, j) for j in range(nb)]
        cc = [self.c, 1 - self.c]
        self.exp = [[[(x * nb + y) * 2 + w for w in cc] for y in bb] for x in aa]
        self.lines = [[[[w * nz + z for z in self.zs] for w in v] for v in u] for u in self.exp]

    def to(self, i=0, j=0, k=0, s=0):
        return (self.exp[i][j][s], self.zs[k])

    def line(self, i=0, j=0, k=0, s=0):
        return self.lines[i][j][s][k]


def xor(value, k):
    out = value
    for bit in (1, 2, 4):
        if k & bit:
            out = out + bit - 2 * bit * lax.rem(lax.div(value, bit), 2)
    return out


def xor_two(value, other, size):
    out, bit = 0, 1
    while bit < size:
        out = out + lax.rem(lax.div(value, bit) + lax.div(other, bit), 2) * bit
        bit *= 2
    return out


def greet(p):
    barrier = pltpu.get_barrier_semaphore()
    others = [p.to(k=k) for k in range(1, p.nz)] + [p.to(i=i) for i in range(1, p.na)]
    others += [p.to(j=j) for j in range(1, p.nb)] + [p.to(s=1)]
    for other in others:
        pl.semaphore_signal(barrier, inc=1, device_id=other, device_id_type=MESH)
    pl.semaphore_wait(barrier, len(others))


def ag_count(shape):
    na, nb, nz = shape
    return (nz - 1) + nz * (na - 1) + nz * (nb - 1) + nz * na * (nb - 1) + nz * nb * (na - 1) + na * nb * nz


class Gather:
    def __init__(self, p, x, o, send, recv, local, base=0):
        self.p, self.x, self.o, self.send, self.recv, self.local = p, x, o, send, recv, local
        self.settled = set()
        rows = x.shape[0]
        cut = rows // 32 * 16 if rows >= 32 else rows
        self.halves = ((0, cut), (cut, rows - cut))
        na, nb, nz = p.na, p.nb, p.nz
        whole = rows > cut
        self.a1, self.b2 = range(1, na), range(1, nb)
        self.b1, self.a2 = (range(1, nb), range(1, na)) if whole else ((), ())
        i = base
        self.iz = i; i += nz - 1
        self.i1a = i; i += nz * (na - 1)
        self.i1b = i; i += nz * (nb - 1)
        self.i2b = i; i += nz * na * (nb - 1)
        self.i2a = i; i += nz * nb * (na - 1)
        self.isib = i; i += na * nb * nz
        self.end = i

    def copy(self, src, dst, i, target):
        return pltpu.make_async_remote_copy(src_ref=src, dst_ref=dst, send_sem=self.send.at[i], recv_sem=self.recv.at[i], device_id=target, device_id_type=MESH)

    def part(self, d, h):
        s, n = self.halves[h]
        return self.o.at[d, pl.ds(s, n)]

    def src(self, d, h, own):
        s, n = self.halves[h]
        return self.x.at[pl.ds(s, n)] if own else self.o.at[d, pl.ds(s, n)]

    def m_z(self, k):
        p = self.p
        return self.copy(self.x, self.o.at[p.line()], self.iz + k - 1, p.to(k=k))

    def r_z(self, k):
        p = self.p
        o = self.o.at[p.line(k=k)]
        return self.copy(o, o, self.iz + k - 1, p.to(k=k))

    def m_1(self, axis, k, j):
        p = self.p
        n, base, h, t = (p.na, self.i1a, 0, p.to(i=j)) if axis == "a" else (p.nb, self.i1b, 1, p.to(j=j))
        d = p.line(k=k)
        return self.copy(self.src(d, h, k == 0), self.part(d, h), base + k * (n - 1) + j - 1, t)

    def r_1(self, axis, k, j):
        p = self.p
        if axis == "a":
            n, base, h, t, d = p.na, self.i1a, 0, p.to(i=j), p.line(i=j, k=k)
        else:
            n, base, h, t, d = p.nb, self.i1b, 1, p.to(j=j), p.line(j=j, k=k)
        return self.copy(self.part(d, h), self.part(d, h), base + k * (n - 1) + j - 1, t)

    def m_2(self, axis, k, i, j):
        p = self.p
        if axis == "a":
            n, m, base, h, t, d = p.na, p.nb, self.i2a, 1, p.to(i=j), p.line(j=i, k=k)
        else:
            n, m, base, h, t, d = p.nb, p.na, self.i2b, 0, p.to(j=j), p.line(i=i, k=k)
        return self.copy(self.src(d, h, k == 0 and i == 0), self.part(d, h), base + (k * m + i) * (n - 1) + j - 1, t)

    def r_2(self, axis, k, i, j):
        p = self.p
        if axis == "a":
            n, m, base, h, t, d = p.na, p.nb, self.i2a, 1, p.to(i=j), p.line(i=j, j=i, k=k)
        else:
            n, m, base, h, t, d = p.nb, p.na, self.i2b, 0, p.to(j=j), p.line(i=i, j=j, k=k)
        return self.copy(self.part(d, h), self.part(d, h), base + (k * m + i) * (n - 1) + j - 1, t)

    def m_s(self, k, i, j):
        p = self.p
        d = p.line(i=i, j=j, k=k)
        own = k == 0 and i == 0 and j == 0
        return self.copy(self.x if own else self.o.at[d], self.o.at[d], self.isib + (k * p.na + i) * p.nb + j, p.to(s=1))

    def r_s(self, k, i, j):
        p = self.p
        d = p.line(i=i, j=j, k=k, s=1)
        return self.copy(self.o.at[d], self.o.at[d], self.isib + (k * p.na + i) * p.nb + j, p.to(s=1))

    def own(self):
        return pltpu.make_async_copy(self.x, self.o.at[self.p.line()], self.local)

    def begin(self):
        self.own().start()
        self.spread(0)

    def launch(self, k):
        self.m_z(k).start()

    def spread(self, k):
        p = self.p
        for j in self.a1:
            self.m_1("a", k, j).start()
        for j in self.b1:
            self.m_1("b", k, j).start()
        for j in self.b2:
            self.m_2("b", k, 0, j).start()
        for j in self.a2:
            self.m_2("a", k, 0, j).start()
        self.m_s(k, 0, 0).start()

    def turn(self, k):
        p = self.p
        for i in self.a1:
            self.r_1("a", k, i).wait_recv()
            for j in self.b2:
                self.m_2("b", k, i, j).start()
        for i in self.b1:
            self.r_1("b", k, i).wait_recv()
            for j in self.a2:
                self.m_2("a", k, i, j).start()

    def close(self, k):
        p = self.p
        for i in range(p.na):
            for j in self.b2:
                self.r_2("b", k, i, j).wait_recv()
        for i in range(p.nb):
            for j in self.a2:
                self.r_2("a", k, i, j).wait_recv()
        for i in range(p.na):
            for j in range(p.nb):
                if i or j:
                    self.m_s(k, i, j).start()

    def receive(self, k):
        self.r_z(k).wait_recv()

    def arrive(self, k):
        self.receive(k)
        self.spread(k)

    def plane(self, k):
        for i in range(self.p.na):
            for j in range(self.p.nb):
                self.r_s(k, i, j).wait_recv()

    def settle(self, k):
        p = self.p
        self.settled.add(k)
        for i in range(p.na):
            for j in range(p.nb):
                self.m_s(k, i, j).wait_send()
        for j in self.a1:
            self.m_1("a", k, j).wait_send()
        for j in self.b1:
            self.m_1("b", k, j).wait_send()
        for j in self.a2:
            for i in range(p.nb):
                self.m_2("a", k, i, j).wait_send()
        for j in self.b2:
            for i in range(p.na):
                self.m_2("b", k, i, j).wait_send()

    def finish(self, planes, far):
        for k in planes:
            if k not in self.settled:
                self.settle(k)
        for k in far:
            self.m_z(k).wait_send()

OUTS = 4


def rs_layout(shape, rows):
    na, nb, nz = shape
    cut = rows // 32 * 16
    s0, s1 = cut, rows - cut
    counts = [na * nb * nz, (nb - 1) * na * nz, (na - 1) * nb * nz, (na - 1) * nz, (nb - 1) * nz, 2 * (nz - 1)]
    buffers = [
        (na, nb, nz, rows),
        (nb - 1, na, nz, s0),
        (na - 1, nb, nz, s1),
        (na - 1, nz, s0),
        (nb - 1, nz, s1),
        (nz - 1, rows),
    ]
    return counts, buffers


class Scatter:
    def __init__(self, p, v, out, buffers, send, recv, base=0, rows=None):
        self.p, self.v, self.out, self.send, self.recv = p, v, out, send, recv
        self.r1, self.r2b, self.r2a, self.r3a, self.r3b, self.r4 = buffers
        rows = out.shape[0] if rows is None else rows
        cut = rows // 32 * 16
        self.rows = rows
        self.halves = ((0, cut), (cut, rows - cut))
        counts, _ = rs_layout((p.na, p.nb, p.nz), rows)
        self.starts = []
        for n in counts:
            self.starts.append(base)
            base += n
        self.end = base
        self.waited = set()

    def copy(self, src, dst, i, target):
        return pltpu.make_async_remote_copy(src_ref=src, dst_ref=dst, send_sem=self.send.at[i], recv_sem=self.recv.at[i], device_id=target, device_id_type=MESH)

    def block(self, i, j, k, s=0):
        p = self.p
        if len(self.v.shape) == 5:
            return self.v.at[i, j, k]
        return self.v.at[p.line(i, j, k, s), pl.ds(0, self.rows)]

    def half(self, ref, h):
        s, n = self.halves[h]
        return ref.at[pl.ds(s, n)]

    def sibling(self, i, j, k):
        p = self.p
        n = self.starts[0] + (i * p.nb + j) * p.nz + k
        return self.copy(self.block(i, j, k, 1), self.r1.at[i, j, k], n, p.to(s=1))

    def arrived(self, key, ref, i):
        if key in self.waited:
            return None
        self.waited.add(key)
        p = self.p
        return self.copy(ref, ref, i, p.to(s=1))

    def base_inputs(self, i, j, k, h):
        p = self.p
        n = self.starts[0] + (i * p.nb + j) * p.nz + k
        r = self.r1.at[i, j, k]
        return [(self.half(self.block(i, j, k), h), None), (self.half(r, h), self.arrived((1, i, j, k), r, n))]

    def two(self, h, far, near, k):
        p = self.p
        if h == 0:
            r, n = self.r2b.at[far - 1, near, k], self.starts[1] + ((far - 1) * p.na + near) * p.nz + k
        else:
            r, n = self.r2a.at[far - 1, near, k], self.starts[2] + ((far - 1) * p.nb + near) * p.nz + k
        return r, n

    def three(self, h, far, k):
        p = self.p
        if h == 0:
            return self.r3a.at[far - 1, k], self.starts[3] + (far - 1) * p.nz + k
        return self.r3b.at[far - 1, k], self.starts[4] + (far - 1) * p.nz + k

    def four(self, h, k):
        return self.half(self.r4.at[k - 1], h), self.starts[5] + 2 * (k - 1) + h

    def stage2(self, k):
        p, jobs = self.p, []
        for far, near in [(f, n) for n in range(max(p.na, p.nb)) for f in range(1, max(p.na, p.nb))]:
            if far < p.nb and near < p.na:
                r, n = self.two(0, far, near, k)
                own = self.half(self.r1.at[near, far, k], 0)
                jobs.append((self.base_inputs(near, far, k, 0), (own, r, n, p.to(j=far))))
            if far < p.na and near < p.nb:
                r, n = self.two(1, far, near, k)
                own = self.half(self.r1.at[far, near, k], 1)
                jobs.append((self.base_inputs(far, near, k, 1), (own, r, n, p.to(i=far))))
        return jobs

    def with_two(self, h, near, k):
        p = self.p
        i, j = (near, 0) if h == 0 else (0, near)
        got = self.base_inputs(i, j, k, h)
        for far in range(1, p.nb if h == 0 else p.na):
            r, n = self.two(h, far, near, k)
            got.append((r, self.arrived((2, h, far, near, k), r, n)))
        return got

    def stage3(self, k):
        p, jobs = self.p, []
        for near in range(1, max(p.na, p.nb)):
            if near < p.na:
                r, n = self.three(0, near, k)
                own = self.half(self.r1.at[near, 0, k], 0)
                jobs.append((self.with_two(0, near, k), (own, r, n, p.to(i=near))))
            if near < p.nb:
                r, n = self.three(1, near, k)
                own = self.half(self.r1.at[0, near, k], 1)
                jobs.append((self.with_two(1, near, k), (own, r, n, p.to(j=near))))
        return jobs

    def with_three(self, h, k):
        p = self.p
        got = self.with_two(h, 0, k)
        for far in range(1, p.na if h == 0 else p.nb):
            r, n = self.three(h, far, k)
            got.append((r, self.arrived((3, h, far, k), r, n)))
        return got

    def stage4(self, k, last):
        p, jobs = self.p, []
        if last != (k == 0):
            return jobs
        for h in range(2):
            got = self.with_three(h, k)
            if k:
                r, n = self.four(h, k)
                own = self.half(self.r1.at[0, 0, k], h)
                jobs.append((got, (own, r, n, p.to(k=k))))
            else:
                for far in range(1, p.nz):
                    r, n = self.four(h, far)
                    got.append((r, self.arrived((4, h, far), r, n)))
                jobs.append((got, self.half(self.out, h)))
        return jobs

    def start(self, k):
        p = self.p
        for i in reversed(range(p.na)):
            for j in reversed(range(p.nb)):
                self.sibling(i, j, k).start()

    def finish(self, k):
        p = self.p
        for i in range(p.na):
            for j in range(p.nb):
                self.sibling(i, j, k).wait_send()


class Worker:
    def __init__(self, ins, outbuf, finbuf, load, put, fin, send, recv):
        self.ins, self.outbuf, self.finbuf = ins, outbuf, finbuf
        self.load, self.put, self.fin, self.send, self.recv = load, put, fin, send, recv
        self.room = outbuf.shape[1]
        self.jobs, self.loaded, self.ran = [], 0, 0
        self.puts, self.n_out = [], 0
        self.sends = []

    def add(self, jobs):
        self.jobs.extend(jobs)

    def place(self, j, n, rows):
        return self.ins[j % 2].at[pl.ds(n * self.room, rows)]

    def loading(self, j, n):
        ref, _ = self.jobs[j][0][n]
        return pltpu.make_async_copy(ref, self.place(j, n, ref.shape[0]), self.load.at[j % 2, n])

    def fetch(self, j):
        inputs, _ = self.jobs[j]
        for n, (ref, arrived) in enumerate(inputs):
            if arrived is not None:
                if n > 1:
                    self.forward(0)
                arrived.wait_recv()
            self.loading(j, n).start()
        self.loaded = j + 1

    def forward(self, left):
        while len(self.puts) > left:
            put, out = self.puts.pop(0)
            put.wait()
            self.sending(out).start()
            self.sends.append(out)

    def sending(self, out):
        own, r, n, where = out
        return pltpu.make_async_remote_copy(
            src_ref=own,
            dst_ref=r,
            send_sem=self.send.at[n],
            recv_sem=self.recv.at[n],
            device_id=where,
            device_id_type=MESH,
        )

    def run(self, j):
        inputs, out = self.jobs[j]
        rows = inputs[0][0].shape[0]
        for n in range(len(inputs)):
            self.loading(j, n).wait()
        final = not isinstance(out, tuple)
        if final:
            target = self.finbuf
        else:
            self.forward(OUTS - 1)
            s = self.n_out % OUTS
            self.n_out += 1
            target = self.outbuf.at[s]
        source, count, room = self.ins[j % 2], len(inputs), self.room

        def body(t, carry):
            acc = source[pl.ds(pl.multiple_of(t * 16, 16), 16)].astype(jnp.float32)
            for n in range(1, count):
                at = pl.ds(pl.multiple_of(n * room + t * 16, 16), 16)
                acc = acc + source[at].astype(jnp.float32)
            target[pl.ds(pl.multiple_of(t * 16, 16), 16)] = acc.astype(target.dtype)
            return carry

        lax.fori_loop(0, rows // 16, body, 0)
        if final:
            c = pltpu.make_async_copy(target.at[pl.ds(0, rows)], out, self.fin.at[0])
            c.start()
            c.wait()
        else:
            c = pltpu.make_async_copy(target.at[pl.ds(0, rows)], out[0], self.put.at[s])
            c.start()
            self.puts.append((c, out))
            self.forward(1)

    def drain(self):
        for j in range(self.ran, len(self.jobs)):
            if self.loaded <= j:
                self.fetch(j)
            if j + 1 < len(self.jobs):
                self.fetch(j + 1)
            self.run(j)
            self.ran = j + 1
        self.forward(0)

    def finish(self):
        for out in self.sends:
            self.sending(out).wait_send()

CHUNK = 512
CAP = 32


def experts_kernel(shape, local, *refs):
    na, nb, nz = shape
    x, small, grad, _, place, choice_t, wg_hbm, wu_hbm, wd_hbm = refs[:9]
    dx_sum, y_part, xs_out, gs_out, hs_out, gu_out = refs[9:15]
    x_all, small_all, dx_part = refs[15:18]
    dx_bufs = refs[18:24]
    (wg, wu, wd, xs, gs, xin, gin, pin, sin, cin, ybuf, dbuf, gate, score, hkeep, gkeep, inbuf, outbuf, finbuf) = refs[24:43]
    (wsem, insem, savesem, keepsem, ownsem, outsem, load, put, fin, ag_send, ag_recv, ag_local, rs_send, rs_recv) = refs[43:]
    g_all = y_part
    p = Place(shape)
    length, width = x.shape
    planes = na * nb * 2
    slots = CAP
    many = planes * slots
    first = lax.axis_index("exp") * local
    greet(p)
    weights = [pltpu.make_async_copy(a, b, wsem.at[n]) for n, (a, b) in enumerate(((wg_hbm, wg), (wu_hbm, wu), (wd_hbm, wd)))]
    for w in weights:
        w.start()
    ga = Gather(p, x, x_all, ag_send, ag_recv, ag_local.at[0])
    gb = Gather(p, small, small_all, ag_send, ag_recv, ag_local.at[1], ga.end)
    gg = Gather(p, grad, g_all, ag_send, ag_recv, ag_local.at[2], gb.end)
    both, every = (gb, ga), (gb, ga, gg)
    sd = Scatter(p, dx_part, dx_sum, dx_bufs, rs_send, rs_recv)
    work = Worker((inbuf.at[0], inbuf.at[1]), outbuf, finbuf, load, put, fin, rs_send, rs_recv)
    order = [1, 2, 3, 0]

    def step(name, k, gathers=both):
        for g in gathers:
            getattr(g, name)(k)

    step("spread", 0)
    step("launch", 1)
    for g in every:
        g.own().start()
    step("turn", 0)
    step("arrive", 1)
    step("launch", 2)
    step("launch", 3)
    step("close", 0)
    step("turn", 1)
    step("close", 1)
    for g in every:
        g.own().wait()
    one = (gg,)
    hooks = {(t, n): [] for t in range(nz) for n in range(4)}
    hooks[0, 0] = [("arrive", 2, both)]
    hooks[0, 1] = [("turn", 2, both)]
    hooks[0, 2] = [("close", 2, both)]
    hooks[1, 0] = [("arrive", 3, both)]
    hooks[1, 1] = [("turn", 3, both)]
    hooks[1, 2] = [("close", 3, both), ("spread", 0, one)]
    hooks[2, 0] = [("turn", 0, one)]
    hooks[2, 2] = [("close", 0, one)]

    def device(r, k):
        return r * nz + p.zs[k]

    def spots(s):
        at = pin[s]
        slot = lax.broadcasted_iota(jnp.int32, (slots, length), 0)
        rows = [jnp.where(at[e : e + 1] == slot, 1.0, 0.0) for e in range(local)]
        return rows, jnp.concatenate(rows, axis=0).astype(jnp.bfloat16)

    def dispatch(k):
        def loads(r, s):
            d = device(r, k)
            pairs = (
                (x_all.at[d], xin),
                (g_all.at[d], gin),
                (place.at[d], pin),
                (small_all.at[d], sin),
                (choice_t.at[d], cin),
            )
            return [pltpu.make_async_copy(a, b.at[s], insem.at[s, n]) for n, (a, b) in enumerate(pairs)]

        def item(r, s):
            for c in loads(r, s):
                c.wait()
            masks, spot = spots(s)
            for n in range(0, width, CHUNK):
                for source, target in ((xin, xs), (gin, gs)):
                    rows = jnp.dot(spot, source[s, :, n : n + CHUNK], preferred_element_type=jnp.float32).astype(jnp.bfloat16)
                    for e in range(local):
                        at = pl.ds(pl.multiple_of(e * many + r * slots, slots), slots)
                        target[at, n : n + CHUNK] = rows[e * slots : (e + 1) * slots]
            chosen = cin[s]
            gates = sin[s].astype(jnp.float32)
            gates = gates[0:8, 0:length] + gates[8:16, 0:length]
            for e in range(local):
                weight = jnp.sum(jnp.where(chosen == first + e, gates, 0.0), axis=0, keepdims=True)
                value = jnp.sum(masks[e] * weight, axis=1, keepdims=True)
                gate[e, pl.ds(pl.multiple_of(r * slots, slots), slots)] = jnp.broadcast_to(value, (slots, 128))

        for c in loads(0, 0):
            c.start()

        def body(t, carry):
            for c in loads(2 * t + 1, 1):
                c.start()
            item(2 * t, 0)

            @pl.when(t < planes // 2 - 1)
            def _():
                for c in loads(2 * t + 2, 0):
                    c.start()

            item(2 * t + 1, 1)
            return carry

        lax.fori_loop(0, planes // 2, body, 0)

    def saves(k, e):
        at = pl.ds(pl.multiple_of(e * many, many), many)
        return [pltpu.make_async_copy(a.at[at], b.at[e, k], savesem.at[n, e]) for n, (a, b) in enumerate(((xs, xs_out), (gs, gs_out)))]

    def keeps(k, e, s):
        pairs = ((hkeep, hs_out), (gkeep, gu_out))
        return [pltpu.make_async_copy(a.at[s], b.at[e, k], keepsem.at[s, n]) for n, (a, b) in enumerate(pairs)]

    def expert(k, e, s):
        at = pl.ds(pl.multiple_of(e * many, many), many)
        rows = xs[at]
        gate_act = jnp.dot(rows, wg[e], preferred_element_type=jnp.float32)
        up_act = jnp.dot(rows, wu[e], preferred_element_type=jnp.float32)
        back = lax.dot_general(gs[at], wd[e], (((1,), (1,)), ((), ())), preferred_element_type=jnp.float32)
        weight = gate[e][:, 0:1]
        sig = jax.nn.sigmoid(gate_act)
        silu = gate_act * sig
        hidden = silu * up_act
        score[e] = jnp.broadcast_to(jnp.sum(hidden * back, axis=1, keepdims=True), (many, 128))
        grad = back * weight
        hs = (hidden * weight).astype(jnp.bfloat16)
        gu = (grad * silu).astype(jnp.bfloat16)
        gg = (grad * up_act * sig * (1.0 + gate_act * (1.0 - sig))).astype(jnp.bfloat16)
        hkeep[s] = hs
        gkeep[s] = jnp.concatenate([gg, gu], axis=1)
        for c in keeps(k, e, s):
            c.start()
        for c in saves(k, e):
            c.wait()
        for n in range(0, width, CHUNK):
            y = jnp.dot(hs, wd[e, :, n : n + CHUNK], preferred_element_type=jnp.float32)
            gs[at, n : n + CHUNK] = y.astype(jnp.bfloat16)
            form = (((1,), (1,)), ((), ()))
            dx = lax.dot_general(gg, wg[e, n : n + CHUNK], form, preferred_element_type=jnp.float32)
            dx = dx + lax.dot_general(gu, wu[e, n : n + CHUNK], form, preferred_element_type=jnp.float32)
            xs[at, n : n + CHUNK] = dx.astype(jnp.bfloat16)

    def experts(k, start, stop):
        def body(t, carry):
            for s in range(2):
                e = 2 * t + s

                @pl.when(e >= 2)
                def _():
                    for c in keeps(k, e - 2, s):
                        c.wait()

                expert(k, e, s)
            return carry

        if stop > start:
            lax.fori_loop(start // 2, stop // 2, body, 0)

    def combine(k):
        def at_offset(t, s):
            t = jnp.int32(t)
            i, j = lax.div(t, nb), lax.rem(t, nb)
            c = p.c if s else 1 - p.c
            return i, j, (xor_two(p.a, i, na) * nb + xor_two(p.b, j, nb)) * 2 + c

        def loads(t, s):
            r = at_offset(t, s)[2]
            d = device(r, k)
            return pltpu.make_async_copy(place.at[d], pin.at[s], insem.at[s, 0])

        def store_y(t, s):
            r = at_offset(t, s)[2]
            out = y_part.at[device(r, k)]
            return pltpu.make_async_copy(ybuf.at[s], out, ownsem.at[s])

        def store_dx(t, s):
            t = jnp.int32(t)
            i, j, _ = at_offset(t, s)
            if s:
                return pltpu.make_async_copy(dbuf.at[2], sd.block(i, j, k), outsem.at[0])
            n = sd.starts[0] + t * nz + k
            return sd.copy(dbuf.at[lax.rem(t, 2)], sd.r1.at[i, j, k], n, p.to(s=1))

        def item(t, s):
            r = at_offset(t, s)[2]
            loads(t, s).wait()

            @pl.when(t > 0)
            def _():
                store_y(t - 1, s).wait()
                if s:
                    store_dx(t - 1, s).wait()

            if not s:

                @pl.when(t > 1)
                def _():
                    store_dx(t - 2, s).wait_send()

            d = 2 if s else lax.rem(t, 2)
            masks, _ = spots(s)
            spot = jnp.concatenate(masks, axis=0).T.astype(jnp.bfloat16)
            for source, out in ((gs, ybuf.at[s]), (xs, dbuf.at[d])):
                for n in range(0, width, CHUNK):
                    rows = [
                        source[pl.ds(pl.multiple_of(e * many + r * slots, slots), slots), n : n + CHUNK]
                        for e in range(local)
                    ]
                    rows = jnp.concatenate(rows, axis=0)
                    total = jnp.dot(spot, rows, preferred_element_type=jnp.float32)
                    out[0:length, n : n + CHUNK] = total.astype(jnp.bfloat16)
            row = lax.broadcasted_iota(jnp.int32, (8, length), 0)
            table = jnp.zeros((8, length), jnp.float32)
            for e in range(local):
                value = score[e, pl.ds(pl.multiple_of(r * slots, slots), slots)][:, 0:1]
                line = jnp.sum(masks[e] * value, axis=0, keepdims=True)
                table = jnp.where(row == (first + e) % 8, line, table)
            table = jnp.concatenate([table, jnp.zeros((8, length), jnp.float32)], axis=0)
            table = jnp.concatenate([table, jnp.zeros((16, 256 - length), jnp.float32)], axis=1)
            dbuf[d, length : length + 16] = jnp.zeros((16, width), jnp.bfloat16)
            at = pl.ds(pl.multiple_of(first // 8 * 256, 256), 256)
            dbuf[d, length : length + 16, at] = table.astype(jnp.bfloat16)
            store_y(t, s).start()
            store_dx(t, s).start()

        loads(0, 0).start()

        def body(t, carry):
            loads(t, 1).start()
            item(t, 0)

            @pl.when(t < na * nb - 1)
            def _():
                loads(t + 1, 0).start()

            item(t, 1)
            return carry

        lax.fori_loop(0, na * nb, body, 0)
        last = na * nb - 1
        for s in range(2):
            store_y(last, s).wait()
        store_dx(last, 1).wait()
        for t in range(max(0, last - 1), last + 1):
            store_dx(t, 0).wait_send()

    def add(jobs):
        work.add(jobs)
        work.drain()

    for t, k in enumerate(order):
        for g in every if k == 0 else both:
            g.plane(k)
        dispatch(k)
        for e in range(local):
            for c in saves(k, e):
                c.start()
        for h in hooks[t, 0]:
            step(*h)
        if t == 0:
            for w in weights:
                w.wait()
        half = local // 4 * 2
        experts(k, 0, half)
        for h in hooks[t, 1]:
            step(*h)
        if t:
            add(sd.stage3(order[t - 1]))
        experts(k, half, local)
        for h in hooks[t, 2]:
            step(*h)
        for s in range(2):
            for c in keeps(k, local - 2 + s, s):
                c.wait()
        if t:
            add(sd.stage4(order[t - 1], False))
        if k == 0:
            gg.settle(k)
        combine(k)
        add(sd.stage2(k))
        for h in hooks[t, 3]:
            step(*h)
    add(sd.stage3(order[-1]))
    add(sd.stage4(order[-1], False))
    add(sd.stage4(0, True))
    work.finish()
    for g in both:
        g.finish(range(nz), range(1, nz))
    gg.finish((0,), ())


def run_experts(shape, x, small, grad, g_all, place, choice_t, wg, wu, wd, collective_id):
    na, nb, nz = shape
    local, width, hidden = wg.shape
    length = x.shape[0]
    planes = na * nb * 2
    many = planes * CAP
    tall = length + 16
    low, wide = jnp.bfloat16, jnp.float32
    any_ = pl.BlockSpec(memory_space=pl.ANY)
    sds = jax.ShapeDtypeStruct
    outs = [sds((tall, width), wide), sds(g_all.shape, low)]
    outs += [sds((local, nz, many, width), low)] * 2 + [sds((local, nz, many, n * hidden), low) for n in (1, 2)]
    outs += [sds((g_all.shape[0],) + x.shape, low), sds((g_all.shape[0],) + small.shape, low)]
    outs += [sds((na, nb, nz, tall, width), low)]
    counts, buffers = rs_layout(shape, tall)
    total = sum(counts)
    outs += [sds(b + (width,), low) for b in buffers]
    messages = 3 * ag_count(shape)
    room = tall - tall // 32 * 16
    inputs = na + nb + nz - 1
    dma = pltpu.SemaphoreType.DMA
    got = pl.pallas_call(
        functools.partial(experts_kernel, shape, local),
        out_shape=outs,
        in_specs=[any_] * 9,
        out_specs=[any_] * len(outs),
        input_output_aliases={3: 1},
        scratch_shapes=[
            pltpu.VMEM((local, width, hidden), low),
            pltpu.VMEM((local, width, hidden), low),
            pltpu.VMEM((local, hidden, width), low),
            pltpu.VMEM((local * many, width), low),
            pltpu.VMEM((local * many, width), low),
            pltpu.VMEM((2, length, width), low),
            pltpu.VMEM((2, length, width), low),
            pltpu.VMEM((2,) + place.shape[1:], jnp.int32),
            pltpu.VMEM((2,) + small.shape, low),
            pltpu.VMEM((2,) + choice_t.shape[1:], jnp.int32),
            pltpu.VMEM((2, length, width), low),
            pltpu.VMEM((3, tall, width), low),
            pltpu.VMEM((local, many, 128), wide),
            pltpu.VMEM((local, many, 128), wide),
            pltpu.VMEM((2, many, hidden), low),
            pltpu.VMEM((2, many, 2 * hidden), low),
            pltpu.VMEM((2, inputs * room, width), low),
            pltpu.VMEM((OUTS, room, width), low),
            pltpu.VMEM((room, width), wide),
            dma((3,)),
            dma((2, 5)),
            dma((2, local)),
            dma((2, 2)),
            dma((2,)),
            dma((2,)),
            dma((2, inputs)),
            dma((OUTS,)),
            dma((1,)),
            dma((messages,)),
            dma((messages,)),
            dma((3,)),
            dma((total,)),
            dma((total,)),
        ],
        compiler_params=pltpu.CompilerParams(
            collective_id=collective_id, has_side_effects=True, vmem_limit_bytes=63 << 20
        ),
    )(x, small, grad, g_all, place, choice_t, wg, wu, wd)
    return got[:6]

HEADS = 16
HEAD_DIM = 128
EXPERTS = 64
epsilon = 1e-05
masked_value = -1e30
low = jnp.bfloat16
wide = jnp.float32
ROWS_OUT = (((1,), (1,)), ((), ()))


def factor_of(values):
    return lax.rsqrt(jnp.mean(values * values, axis=-1, keepdims=True) + epsilon)


def swapped(v):
    half = v.shape[1] // 2
    return jnp.concatenate([v[:, half:], v[:, :half]], axis=1)


def front_kernel(shape, local_experts, *refs):
    na, nb, nz = shape
    tokens, allowed, cosine, sine, choice = refs[:5]
    shards = refs[5:12]
    alls = refs[12:19]
    places, choices, normed_f, normed_ft, normed_at, attended_t, gates, residual, q_raw, k_raw, q_low, k_low, v_low, probs, router_p, gains = refs[19:35]
    wq, wk, wv, wo, router, smalls, normed, attended, wsem, send, recv, local = refs[35:]
    p = Place(shape)
    length, width = tokens.shape
    greet(p)
    gs, base = [], 0
    for i in range(7):
        g = Gather(p, shards[i], alls[i], send, recv, local.at[i], base)
        base = g.end
        gs.append(g)
    weights, late = gs[:6], gs[6]

    def begin(g):
        g.begin()
        for k in range(1, nz):
            g.launch(k)

    for g in weights:
        begin(g)
    for k in range(1, nz):
        for g in weights:
            g.arrive(k)
            g.turn(k - 1)
        if k > 1:
            for g in weights:
                g.close(k - 2)
    planes = (1, 2, 3)
    for k in range(1, nz):
        late.launch(k)
    for g in weights:
        g.turn(nz - 1)
    for k in planes[:2]:
        late.arrive(k)
    for k in range(nz - 2, nz):
        for g in weights:
            g.close(k)
    copies = []
    for n, (g, target) in enumerate(zip(weights, (smalls, router, wq, wk, wv, wo))):
        g.own().wait()
        for k in range(nz):
            g.plane(k)
        c = pltpu.make_async_copy(alls[n], target, wsem.at[n])
        c.start()
        copies.append(c)

    copies[0].wait()
    devices = smalls.shape[0]

    def total(d, carry):
        gains[...] += smalls[d].astype(wide)
        return carry

    gains[...] = jnp.zeros((16, width), wide)
    lax.fori_loop(0, devices, total, 0)
    x = tokens[...].astype(wide)
    scaled = x * factor_of(x) * gains[0:1]
    normed[...] = scaled.astype(low)

    def transposed(source, target):
        def body(n, carry):
            at = pl.ds(pl.multiple_of(n * 256, 256), 256)
            target[at] = source[:, at].astype(wide).T.astype(low)
            return carry

        lax.fori_loop(0, width // 256, body, 0)

    def product(left, right, out, more=None):
        def body(n, carry):
            at = pl.ds(pl.multiple_of(n * 512, 512), 512)
            got = jnp.dot(left[...], right[:, :, at].reshape(width, 512), preferred_element_type=wide)
            if more is not None:
                got = got + more[:, at].astype(wide)
            out[:, at] = got.astype(out.dtype)
            return carry

        lax.fori_loop(0, width // 512, body, 0)

    copies[2].wait()
    product(normed, wq, q_raw)
    copies[3].wait()
    product(normed, wk, k_raw)
    copies[4].wait()
    product(normed, wv, v_low)
    for k in planes[:1]:
        late.turn(k)
    transposed(normed, normed_at)
    factor_q = factor_of(q_raw[...])
    factor_k = factor_of(k_raw[...])

    def head(h, carry):
        at = pl.ds(pl.multiple_of(h * HEAD_DIM, HEAD_DIM), HEAD_DIM)

        def turned(raw, factor, gain):
            v = raw[:, at] * factor * gain[:, at]
            return (v * cosine[...] + swapped(v) * sine[...]).astype(low)

        q = turned(q_raw, factor_q, gains.at[1:2])
        k = turned(k_raw, factor_k, gains.at[2:3])
        q_low[:, at] = q
        k_low[:, at] = k
        scores = lax.dot_general(q, k, ROWS_OUT, preferred_element_type=wide) * HEAD_DIM ** (-0.5)
        scores = jnp.where(allowed[...] > 0.0, scores, masked_value)
        e = jnp.exp(scores - jnp.max(scores, axis=-1, keepdims=True))
        e = e / jnp.sum(e, axis=-1, keepdims=True)
        probs[h] = e
        out = jnp.dot(e.astype(low), v_low[:, at], preferred_element_type=wide)
        attended[:, at] = out.astype(low)
        return carry

    lax.fori_loop(0, HEADS, head, 0)
    late.turn(planes[1])
    late.close(planes[0])
    late.arrive(planes[2])
    copies[5].wait()
    product(attended, wo, residual, tokens)
    r = residual[...]
    normed_f[...] = (r * factor_of(r) * gains[3:4]).astype(low)
    copies[1].wait()
    logits = jnp.dot(normed_f[...], router[...].reshape(width, 128), preferred_element_type=wide)
    logits = logits.T[0:EXPERTS]
    e = jnp.exp(logits - jnp.max(logits, axis=0, keepdims=True))
    chances = e / jnp.sum(e, axis=0, keepdims=True)
    router_p[...] = chances
    expert = lax.broadcasted_iota(jnp.int32, (EXPERTS, length), 0)
    rows = [
        jnp.sum(jnp.where(expert == choice[n : n + 1], chances, 0.0), axis=0, keepdims=True)
        for n in range(choice.shape[0])
    ]
    rows = jnp.concatenate(rows, axis=0)
    upper = rows.astype(low).astype(wide)
    rows = jnp.concatenate([upper, rows - upper], axis=0)
    rows = jnp.concatenate([rows, jnp.zeros((16, gates.shape[1] - length), wide)], axis=1)
    gates[...] = rows.astype(low)
    late.close(planes[1])
    late.turn(planes[2])
    first = lax.axis_index("exp") * local_experts
    order = lax.broadcasted_iota(jnp.int32, (length, length), 0)
    before = jnp.where(order < lax.broadcasted_iota(jnp.int32, (length, length), 1), 1.0, 0.0)
    before = before.astype(low)

    def slots(d, carry):
        named = smalls[d].astype(wide)[8:16, 0:length].astype(jnp.int32)
        choices[d] = named
        rows = [
            jnp.max(jnp.where(named == first + e, 1.0, 0.0), axis=0, keepdims=True)
            for e in range(local_experts)
        ]
        rows = jnp.concatenate(rows + [jnp.zeros((16 - local_experts, length), wide)], axis=0)
        ranks = jnp.dot(rows.astype(low), before, preferred_element_type=wide)
        ranks = jnp.where(rows > 0.0, ranks, -1.0).astype(jnp.int32)
        places[d] = ranks[0:local_experts]
        return carry

    lax.fori_loop(0, devices, slots, 0)
    transposed(attended, attended_t)
    transposed(normed_f, normed_ft)
    late.close(planes[2])
    for k in planes:
        late.plane(k)
    for g in weights:
        g.finish(range(nz), range(1, nz))
    late.finish(planes, range(1, nz))


def run_front(shape, tokens, allowed, cosine, sine, choice, shards, local_experts, collective_id):
    na, nb, nz = shape
    length, width = tokens.shape
    devices = na * nb * nz * 2
    any_, vmem = pl.BlockSpec(memory_space=pl.ANY), pl.BlockSpec(memory_space=pltpu.VMEM)
    sds = jax.ShapeDtypeStruct
    alls = [sds((devices,) + s.shape, low) for s in shards]
    row, tall = (length, width), (width, length)
    outs = [sds((devices, local_experts, length), jnp.int32), sds((devices, 8, length), jnp.int32)]
    outs += [sds(row, low), sds(tall, low), sds(tall, low), sds(tall, low)]
    outs += [sds((16, -length % 256 + length), low), sds(row, wide), sds(row, wide), sds(row, wide)]
    outs += [sds(row, low), sds(row, low), sds(row, low), sds((HEADS, length, length), wide)]
    outs += [sds((EXPERTS, length), wide), sds((16, width), wide)]
    count = ag_count(shape) * len(shards)
    got = pl.pallas_call(
        functools.partial(front_kernel, shape, local_experts),
        out_shape=alls + outs,
        in_specs=[vmem] * 5 + [any_] * 7,
        out_specs=[any_] * 7 + [vmem] * len(outs),
        scratch_shapes=[pltpu.VMEM(alls[n].shape, low) for n in (2, 3, 4, 5, 1, 0)]
        + [
            pltpu.VMEM(row, low),
            pltpu.VMEM(row, low),
            pltpu.SemaphoreType.DMA((6,)),
            pltpu.SemaphoreType.DMA((count,)),
            pltpu.SemaphoreType.DMA((count,)),
            pltpu.SemaphoreType.DMA((7,)),
        ],
        compiler_params=pltpu.CompilerParams(
            collective_id=collective_id, has_side_effects=True, vmem_limit_bytes=63 << 20
        ),
    )(tokens, allowed, cosine, sine, choice, *shards)
    return got[:7], got[7:]


FIRST = (((0,), (0,)), ((), ()))


def last_kernel(shape, part, *refs):
    na, nb, nz = shape
    tokens, out_grad, residual, q_raw, k_raw, q_low, k_low, v_low = refs[:8]
    normed_at, attended_t, normed_ft, router, gains, router_p, dx_in, cosine, sine = refs[8:17]
    y_part, probs, wq, wk, wv, wo, xs, gs, hs, gu = refs[17:27]
    y_sum, w_sum, input_grad, dwg, dwu, dwd, w_part = refs[27:34]
    y_bufs, w_bufs = refs[34:40], refs[40:46]
    flat, xin, gin, hin, uin, outbuf, finbuf, grads = refs[46:54]
    wsem, psem, isem, outsem, insem, savesem, load, put, fin, send, recv = refs[54:]
    p = Place(shape)
    greet(p)
    length, width = y_sum.shape
    rows = 4 * part
    tall = rows + 16
    sy = Scatter(p, y_part, y_sum, y_bufs, send, recv)
    sw = Scatter(p, w_part, w_sum, w_bufs, send, recv, sy.end)
    half = flat.shape[0] // 2
    ins = (flat.at[pl.ds(0, half)], flat.at[pl.ds(half, half)])
    work = Worker(ins, outbuf, finbuf, load, put, fin, send, recv)
    local, chunks = xs.shape[:2]
    hidden = hs.shape[3]
    order = [*reversed(range(nz))]

    def weight(source, target, n):
        return pltpu.make_async_copy(source, target, wsem.at[n])

    def back_product(left, matrix, out, kind):
        def body(n, carry):
            at = pl.ds(pl.multiple_of(n * 512, 512), 512)
            part_of = matrix[lax.div(n, 2), pl.ds(pl.multiple_of(lax.rem(n, 2) * 512, 512), 512)]
            got = lax.dot_general(left[...], part_of, ROWS_OUT, preferred_element_type=wide)
            if kind == "add":
                got = got + out[:, at]
            out[:, at] = got.astype(out.dtype)
            return carry

        lax.fori_loop(0, width // 512, body, 0)

    def norm_back(grad, unit, factor, gain):
        m = grad * gain
        return factor * (m - unit * jnp.mean(m * unit, axis=-1, keepdims=True))

    pieces = [(e, c) for e in range(local) for c in range(chunks)]

    def loads(n):
        e, c = pieces[n]
        pairs = ((xs, xin), (gs, gin), (hs, hin), (gu, uin))
        return [pltpu.make_async_copy(a.at[e, c], b.at[n % 2], insem.at[n % 2, m]) for m, (a, b) in enumerate(pairs)]

    def early(work_a, res_grad, k_grad, res_low, att_grad, dq, dk, dv, llow, pin):
        def back_ffn():
            weight(wo, xin, 0).start()
            weight(wv, gin, 1).start()
            wide_table = dx_in[length : length + 8]
            table = [wide_table[:, n * 256 : n * 256 + length] for n in range(EXPERTS // 8)]
            table = jnp.concatenate(table, axis=0)
            chances = router_p[...]
            grad = chances * (table - jnp.sum(chances * table, axis=0, keepdims=True))
            grad = jnp.concatenate([grad, jnp.zeros((128 - EXPERTS, length), wide)], axis=0)
            llow[...] = grad.T.astype(low)
            for n in range(0, width, 512):
                got = lax.dot_general(
                    llow[...], router[n : n + 512], ROWS_OUT, preferred_element_type=wide
                )
                work_a[:, n : n + 512] = got + dx_in[0:length, n : n + 512]
            factor = factor_of(residual[...])
            unit = residual[...] * factor
            grad = work_a[...]
            grads[3:4] = jnp.sum(grad * unit, axis=0, keepdims=True)
            got = out_grad[...].astype(wide) + norm_back(grad, unit, factor, gains[3:4])
            res_grad[...] = got
            res_low[...] = got.astype(low)
            weight(wo, xin, 0).wait()
            back_product(res_low, xin, att_grad, "set")
            weight(wq, xin, 0).start()

        def back_heads():
            def prob(h, s):
                return pltpu.make_async_copy(probs.at[h], pin.at[s], psem.at[s])

            prob(0, 0).start()

            def one(h, s):
                @pl.when(h + 1 < HEADS)
                def _():
                    prob(h + 1, 1 - s).start()

                prob(h, s).wait()
                at = pl.ds(pl.multiple_of(h * HEAD_DIM, HEAD_DIM), HEAD_DIM)
                grad, q, k, v = att_grad[:, at], q_low[:, at], k_low[:, at], v_low[:, at]
                chances = pin[s]
                got = lax.dot_general(chances.astype(low), grad, FIRST, preferred_element_type=wide)
                dv[:, at] = got.astype(low)
                inner = lax.dot_general(grad, v, ROWS_OUT, preferred_element_type=wide)
                inner = chances * (inner - jnp.sum(chances * inner, axis=-1, keepdims=True))
                inner = inner.astype(low)
                scale = HEAD_DIM ** (-0.5)

                def turned_back(x):
                    return x * cosine[...] - swapped(x) * sine[...]

                got = jnp.dot(inner, k, preferred_element_type=wide) * scale
                work_a[:, at] = turned_back(got)
                got = lax.dot_general(inner, q, FIRST, preferred_element_type=wide) * scale
                k_grad[:, at] = turned_back(got)

            def body(t, carry):
                one(2 * t, 0)
                one(2 * t + 1, 1)
                return carry

            lax.fori_loop(0, HEADS // 2, body, 0)

        def back_inputs():
            for raw, grad, out, n in ((q_raw, work_a, dq, 1), (k_raw, k_grad, dk, 2)):
                factor = factor_of(raw[...])
                unit = raw[...] * factor
                grads[n : n + 1] = jnp.sum(grad[...] * unit, axis=0, keepdims=True)
                out[...] = norm_back(grad[...], unit, factor, gains[n : n + 1]).astype(low)
            weight(wv, gin, 1).wait()
            back_product(dv, gin, work_a, "set")
            weight(wk, gin, 1).start()
            weight(wq, xin, 0).wait()
            back_product(dq, xin, work_a, "add")
            weight(wk, gin, 1).wait()
            back_product(dk, gin, work_a, "add")
            x = tokens[...].astype(wide)
            factor = factor_of(x)
            unit = x * factor
            grad = work_a[...]
            grads[0:1] = jnp.sum(grad * unit, axis=0, keepdims=True)
            res_grad[...] = res_grad[...] + norm_back(grad, unit, factor, gains[0:1])
            c = pltpu.make_async_copy(res_grad, input_grad, isem.at[0])
            c.start()
            c.wait()
            for d in loads(0):
                d.start()

        def products():
            def start_of(s, z):
                return (s * nz + z) * tall

            def where(t, s):
                t = jnp.int32(t)
                i, j = lax.div(t, nb), lax.rem(t, nb)
                c = p.c if s else 1 - p.c
                return i, j, (xor_two(p.a, i, na) * nb + xor_two(p.b, j, nb)) * 2 + c

            def stores(t, s):
                i, j, _ = where(t, s)
                got = []
                for k in range(nz):
                    src = flat.at[pl.ds(pl.multiple_of(start_of(s, p.zs[k]), 16), tall)]
                    if s:
                        got.append(pltpu.make_async_copy(src, sw.block(i, j, k), outsem.at[k]))
                    else:
                        n = sw.starts[0] + t * nz + k
                        got.append(sw.copy(src, sw.r1.at[i, j, k], n, p.to(s=1)))
                return got

            def finish(t, s):
                for c in stores(t, s):
                    if s:
                        c.wait()
                    else:
                        c.wait_send()

            pairs = ((normed_at, dq), (normed_at, dk), (normed_at, dv), (attended_t, res_low))
            groups = part // 16

            def body(t, carry):
                for s in range(2):

                    @pl.when(t > 0)
                    def _():
                        finish(t - 1, s)

                    r = where(t, s)[2]
                    at = pl.ds(pl.multiple_of(r * nz * part, nz * part), nz * part)
                    for m, (left, right) in enumerate(pairs):
                        for n in range(0, width, 512):
                            got = jnp.dot(left[at], right[:, n : n + 512], preferred_element_type=wide)
                            got = got.astype(low)
                            for z in range(nz):
                                to = start_of(s, z) + m * part
                                flat[to : to + part, n : n + 512] = got[z * part : (z + 1) * part]
                    got = jnp.dot(normed_ft[at], llow[...], preferred_element_type=wide).astype(low)
                    for z in range(nz):
                        to = start_of(s, z) + rows
                        lanes = pl.ds(pl.multiple_of((r * nz + z) * part // 128 * 128, 128), 128)
                        gain = jnp.concatenate([grads[:, lanes], jnp.zeros((8, 128), wide)], axis=0)
                        flat[to : to + 16] = jnp.zeros((16, width), low)
                        for n in range(groups):
                            piece = got[z * part + n * 16 : z * part + (n + 1) * 16]
                            flat[to : to + 16, n * 128 : (n + 1) * 128] = piece
                        flat[to : to + 16, groups * 128 : (groups + 1) * 128] = gain.astype(low)
                    for c in stores(t, s):
                        c.start()
                return carry

            lax.fori_loop(0, na * nb, body, 0)
            for s in range(2):
                finish(na * nb - 1, s)

        steps_of = (back_ffn, back_heads, back_inputs, products)
        for kind, what in plan[:cut]:
            if kind == "add":
                add(what)
            else:
                steps_of[what]()

    def late(og, ou, od, accg, accd):
        def saves(e):
            s = e % og.shape[0]
            pairs = ((og, dwg), (ou, dwu), (od, dwd))
            return [pltpu.make_async_copy(a.at[s], b.at[e], savesem.at[s, m]) for m, (a, b) in enumerate(pairs)]

        def piece(n):
            e, c = pieces[n]
            s, o = n % 2, e % og.shape[0]
            if n + 1 < len(pieces):
                for d in loads(n + 1):
                    d.start()
            for d in loads(n):
                d.wait()
            if c == 0 and e >= og.shape[0]:
                for d in saves(e - og.shape[0]):
                    d.wait()
            form = (((0,), (0,)), ((), ()))

            def columns(t, carry):
                at = pl.ds(pl.multiple_of(t * 512, 512), 512)
                g = lax.dot_general(xin[s, :, at], uin[s], form, preferred_element_type=jnp.float32)
                d = lax.dot_general(hin[s], gin[s, :, at], form, preferred_element_type=jnp.float32)
                if c:
                    g = g + accg[at]
                    d = d + accd[:, at]
                if c + 1 < chunks:
                    accg[at] = g
                    accd[:, at] = d
                else:
                    og[o, at] = g[:, :hidden].astype(jnp.bfloat16)
                    ou[o, at] = g[:, hidden:].astype(jnp.bfloat16)
                    od[o, :, at] = d.astype(jnp.bfloat16)
                return carry

            lax.fori_loop(0, width // 512, columns, 0)
            if c + 1 == chunks:
                for d in saves(e):
                    d.start()

        for kind, what in plan[cut:]:
            if kind == "add":
                add(what)
            else:
                piece(what)
        for e in range(max(0, local - og.shape[0]), local):
            for d in saves(e):
                d.wait()

    def add(jobs):
        work.add(jobs)
        work.drain()

    grads[...] = jnp.zeros((8, width), wide)
    for k in order:
        sy.start(k)
    steps = [(s, k) for s in (sy, sw) for k in order]
    slow = 4
    plan, done, count, cut = [], 0, len(steps), 0
    for t in range(count + 2):
        if t < count:
            s, k = steps[t]
            plan.append(("add", s.stage2(k)))
        if t < slow:
            plan.append(("first", t))
            cut = len(plan)
        else:
            until = len(pieces) * (t - slow + 1) // (count - slow) if t < count else len(pieces)
            while done < until:
                plan.append(("piece", done))
                done += 1
        if 1 <= t <= count:
            s, k = steps[t - 1]
            plan.append(("add", s.stage3(k)))
        if 2 <= t:
            s, k = steps[t - 2]
            plan.append(("add", s.stage4(k, False)))
        if t == nz + 2:
            plan.append(("add", sy.stage4(0, True)))
    plan.append(("add", sw.stage4(0, True)))
    row, vmem = (length, width), pltpu.VMEM
    pl.run_scoped(
        early,
        *[vmem(row, wide)] * 3,
        *[vmem(row, low)] * 5,
        vmem((length, 128), low),
        vmem((2,) + probs.shape[1:], wide),
    )
    several = chunks > 1
    slots = 1 if several else 2
    pl.run_scoped(
        late,
        vmem((slots, width, hidden), low),
        vmem((slots, width, hidden), low),
        vmem((slots, hidden, width), low),
        vmem((width if several else 8, 2 * hidden), wide),
        vmem((hidden if several else 8, width), wide),
    )
    work.finish()
    for k in order:
        sy.finish(k)


def run_last(shape, part, vmem_in, any_in, collective_id):
    na, nb, nz = shape
    length, width = vmem_in[0].shape
    y_part, probs, wq, wk, wv, wo, xs, gs, hs, gu = any_in
    tall = 4 * part + 16
    local, hidden = xs.shape[0], hs.shape[3]
    total_slots = xs.shape[1] * xs.shape[2]
    deep = width // 2
    xs, gs, hs, gu = (a.reshape(local, total_slots // deep, deep, a.shape[3]) for a in (xs, gs, hs, gu))
    wq, wk, wv, wo = (a.reshape(2, deep, width) for a in (wq, wk, wv, wo))
    any_, vmem = pl.BlockSpec(memory_space=pl.ANY), pl.BlockSpec(memory_space=pltpu.VMEM)
    sds = jax.ShapeDtypeStruct
    outs = [sds((length, width), wide), sds((tall, width), wide), sds((length, width), wide)]
    outs += [sds((local, width, hidden), low)] * 2 + [sds((local, hidden, width), low)]
    outs += [sds((na, nb, nz, tall, width), low)]
    y_counts, y_buffers = rs_layout(shape, length)
    w_counts, w_buffers = rs_layout(shape, tall)
    total = sum(y_counts) + sum(w_counts)
    outs += [sds(b + (width,), low) for b in y_buffers + w_buffers]
    room = max(tall - tall // 32 * 16, length - length // 32 * 16)
    inputs = na + nb + nz - 1
    dma = pltpu.SemaphoreType.DMA
    got = pl.pallas_call(
        functools.partial(last_kernel, shape, part),
        out_shape=outs,
        in_specs=[vmem] * len(vmem_in) + [any_] * len(any_in),
        out_specs=[any_] * len(outs),
        scratch_shapes=[
            pltpu.VMEM((2 * max(nz * tall, inputs * room), width), low),
            pltpu.VMEM((2, deep, width), low),
            pltpu.VMEM((2, deep, width), low),
            pltpu.VMEM((2, deep, hidden), low),
            pltpu.VMEM((2, deep, 2 * hidden), low),
            pltpu.VMEM((OUTS, room, width), low),
            pltpu.VMEM((room, width), wide),
            pltpu.VMEM((8, width), wide),
            dma((2,)),
            dma((2,)),
            dma((1,)),
            dma((nz,)),
            dma((2, 4)),
            dma((2, 3)),
            dma((2, inputs)),
            dma((OUTS,)),
            dma((1,)),
            dma((total,)),
            dma((total,)),
        ],
        compiler_params=pltpu.CompilerParams(
            collective_id=collective_id, has_side_effects=True, vmem_limit_bytes=63 << 20
        ),
    )(*vmem_in, y_part, probs, wq, wk, wv, wo, xs, gs, hs, gu)
    return got[:6]


def widen_kernel(*refs):
    half = len(refs) // 2
    for source, target in zip(refs[:half], refs[half:]):
        target[...] = source[...].astype(wide)


def widen(arrays):
    local = arrays[0].shape[0]
    specs = [
        pl.BlockSpec((1, a.shape[1] // 2, a.shape[2]), lambda e, n: (e, n, 0)) for a in arrays
    ]
    return pl.pallas_call(
        widen_kernel,
        grid=(local, 2),
        out_shape=[jax.ShapeDtypeStruct(a.shape, wide) for a in arrays],
        in_specs=specs,
        out_specs=specs,
        compiler_params=pltpu.CompilerParams(vmem_limit_bytes=32 << 20),
    )(*arrays)

TOP = 8

base_freq = 10000.0


def rotary(length, head_width):
    positions = jnp.arange(length, dtype=jnp.float32)
    freqs = base_freq ** (-jnp.arange(head_width // 2, dtype=jnp.float32) * 2.0 / head_width)
    angles = positions[:, None] * freqs[None, :]
    return (jnp.cos(angles), jnp.sin(angles))


def on_device(
    shape,
    tokens,
    segment_ids,
    expert_choice,
    w_query,
    w_key,
    w_value,
    w_output,
    w_router,
    attn_gain,
    query_gain,
    key_gain,
    ffn_gain,
    w_gate,
    w_up,
    w_down,
    out_grad,
):
    length, width = tokens.shape
    part = w_query.shape[0]
    devices = width // part

    place = (lax.axis_index("exp") * lax.axis_size("hid") + lax.axis_index("hid")) * part
    small = jnp.stack([attn_gain, query_gain, key_gain, ffn_gain])
    small = lax.dynamic_update_slice(jnp.zeros((16, width), low), small, (0, place))
    listing = expert_choice.T
    small = lax.dynamic_update_slice(small, listing.astype(low), (8, 0))
    router = jnp.pad(w_router, ((0, 0), (0, 128 - EXPERTS)))
    positions = jnp.arange(length)
    segment_row = segment_ids[0]
    allowed = (positions[:, None] >= positions[None, :]) & (
        segment_row[:, None] == segment_row[None, :]
    )
    cosine, sine = rotary(length, HEAD_DIM)
    shards = [small, router, w_query, w_key, w_value, w_output, out_grad]
    alls, saved = run_front(
        shape,
        tokens,
        allowed.astype(wide),
        jnp.concatenate([cosine, cosine], axis=1),
        jnp.concatenate([-sine, sine], axis=1),
        listing,
        shards,
        w_gate.shape[0],
        1,
    )
    _, router_all, query_all, key_all, value_all, output_all, g_all = alls
    places, choices, normed_ffn, normed_ft, normed_at, attended_t, gates = saved[:7]
    residual, query_raw, key_raw, query_low, key_low, value_low, attn_probs, router_pt, gains = saved[7:]
    total_counts = jnp.sum(
        (choices.reshape(devices, -1)[:, None, :] == jnp.arange(EXPERTS)[:, None]).astype(jnp.int32),
        axis=2,
    )
    dx_sum, y_part, xs, gs, hs, gu = run_experts(
        shape,
        normed_ffn,
        gates,
        out_grad,
        g_all,
        places,
        choices,
        w_gate,
        w_up,
        w_down,
        2,
    )
    vmem_in = [
        tokens,
        out_grad,
        residual,
        query_raw,
        key_raw,
        query_low,
        key_low,
        value_low,
        normed_at,
        attended_t,
        normed_ft,
        router_all.reshape(width, -1),
        gains,
        router_pt,
        dx_sum,
        jnp.concatenate([cosine, cosine], axis=1),
        jnp.concatenate([-sine, sine], axis=1),
    ]
    any_in = [y_part, attn_probs, query_all, key_all, value_all, output_all, xs, gs, hs, gu]
    mixture, sums, input_grad, grad_wgate, grad_wup, grad_wdown = run_last(
        shape, part, vmem_in, any_in, 3
    )
    result = (residual + mixture).astype(low)
    small = sums[4 * part :]
    sums = sums[: 4 * part].reshape(4, part, width)
    lanes = part // 16 * 128
    sum_router = small[:, :lanes].reshape(16, -1, 128)[:, :, :EXPERTS].transpose(1, 0, 2)
    sum_router = sum_router.reshape(part, EXPERTS)
    sum_gains = lax.dynamic_slice(small, (0, lanes + place % 128), (4, part))
    return (
        result,
        input_grad,
        sums[0],
        sums[1],
        sums[2],
        sums[3],
        sum_router,
        sum_gains[0],
        sum_gains[1],
        sum_gains[2],
        sum_gains[3],
        *widen([grad_wgate, grad_wup, grad_wdown]),
        total_counts,
    )


def solution(mesh):
    rows, both = P(("exp", "hid"), None), P(("exp", "hid"))
    shape = grid_of(mesh.shape["exp"], mesh.shape["hid"])
    experts = (P("exp", None, "hid"), P("exp", None, "hid"), P("exp", "hid", None))
    return jax.shard_map(
        functools.partial(on_device, shape),
        mesh=mesh,
        in_specs=(rows,) * 8 + (both,) * 4 + experts + (rows,),
        out_specs=(rows,) * 7 + (both,) * 4 + experts + (P(),),
        check_vma=False,
    )
```

```python
import functools
import math

import jax
import jax.numpy as jnp
from jax import lax
from jax.experimental import pallas as pl
from jax.experimental.pallas import tpu as pltpu
from jax.sharding import PartitionSpec as P

MESH = pl.DeviceIdType.MESH


def grid_of(exp, hid):
    plane = exp // 2
    na = 1 << (int(math.log2(plane)) // 2)
    return na, plane // na, hid


class Place:
    def __init__(self, shape):
        na, nb, nz = self.na, self.nb, self.nz = shape
        e = lax.axis_index("exp")
        self.z = lax.axis_index("hid")
        self.c = lax.rem(e, 2)
        self.b = lax.rem(lax.div(e, 2), nb)
        self.a = lax.div(e, 2 * nb)
        self.zs = [xor(self.z, k) for k in range(nz)]
        aa = [xor(self.a, i) for i in range(na)]
        bb = [xor(self.b, j) for j in range(nb)]
        cc = [self.c, 1 - self.c]
        self.exp = [[[(x * nb + y) * 2 + w for w in cc] for y in bb] for x in aa]
        self.lines = [[[[w * nz + z for z in self.zs] for w in v] for v in u] for u in self.exp]

    def to(self, i=0, j=0, k=0, s=0):
        return (self.exp[i][j][s], self.zs[k])

    def line(self, i=0, j=0, k=0, s=0):
        return self.lines[i][j][s][k]


def xor(value, k):
    out = value
    for bit in (1, 2, 4):
        if k & bit:
            out = out + bit - 2 * bit * lax.rem(lax.div(value, bit), 2)
    return out


def xor_two(value, other, size):
    out, bit = 0, 1
    while bit < size:
        out = out + lax.rem(lax.div(value, bit) + lax.div(other, bit), 2) * bit
        bit *= 2
    return out


def greet(p):
    barrier = pltpu.get_barrier_semaphore()
    others = [p.to(k=k) for k in range(1, p.nz)] + [p.to(i=i) for i in range(1, p.na)]
    others += [p.to(j=j) for j in range(1, p.nb)] + [p.to(s=1)]
    for other in others:
        pl.semaphore_signal(barrier, inc=1, device_id=other, device_id_type=MESH)
    pl.semaphore_wait(barrier, len(others))


def ag_count(shape):
    na, nb, nz = shape
    return (nz - 1) + nz * (na - 1) + nz * (nb - 1) + nz * na * (nb - 1) + nz * nb * (na - 1) + na * nb * nz


class Gather:
    def __init__(self, p, x, o, send, recv, local, base=0):
        self.p, self.x, self.o, self.send, self.recv, self.local = p, x, o, send, recv, local
        self.settled = set()
        rows = x.shape[0]
        cut = rows // 32 * 16 if rows >= 32 else rows
        self.halves = ((0, cut), (cut, rows - cut))
        na, nb, nz = p.na, p.nb, p.nz
        whole = rows > cut
        self.a1, self.b2 = range(1, na), range(1, nb)
        self.b1, self.a2 = (range(1, nb), range(1, na)) if whole else ((), ())
        i = base
        self.iz = i; i += nz - 1
        self.i1a = i; i += nz * (na - 1)
        self.i1b = i; i += nz * (nb - 1)
        self.i2b = i; i += nz * na * (nb - 1)
        self.i2a = i; i += nz * nb * (na - 1)
        self.isib = i; i += na * nb * nz
        self.end = i

    def copy(self, src, dst, i, target):
        return pltpu.make_async_remote_copy(src_ref=src, dst_ref=dst, send_sem=self.send.at[i], recv_sem=self.recv.at[i], device_id=target, device_id_type=MESH)

    def part(self, d, h):
        s, n = self.halves[h]
        return self.o.at[d, pl.ds(s, n)]

    def src(self, d, h, own):
        s, n = self.halves[h]
        return self.x.at[pl.ds(s, n)] if own else self.o.at[d, pl.ds(s, n)]

    def m_z(self, k):
        p = self.p
        return self.copy(self.x, self.o.at[p.line()], self.iz + k - 1, p.to(k=k))

    def r_z(self, k):
        p = self.p
        o = self.o.at[p.line(k=k)]
        return self.copy(o, o, self.iz + k - 1, p.to(k=k))

    def m_1(self, axis, k, j):
        p = self.p
        n, base, h, t = (p.na, self.i1a, 0, p.to(i=j)) if axis == "a" else (p.nb, self.i1b, 1, p.to(j=j))
        d = p.line(k=k)
        return self.copy(self.src(d, h, k == 0), self.part(d, h), base + k * (n - 1) + j - 1, t)

    def r_1(self, axis, k, j):
        p = self.p
        if axis == "a":
            n, base, h, t, d = p.na, self.i1a, 0, p.to(i=j), p.line(i=j, k=k)
        else:
            n, base, h, t, d = p.nb, self.i1b, 1, p.to(j=j), p.line(j=j, k=k)
        return self.copy(self.part(d, h), self.part(d, h), base + k * (n - 1) + j - 1, t)

    def m_2(self, axis, k, i, j):
        p = self.p
        if axis == "a":
            n, m, base, h, t, d = p.na, p.nb, self.i2a, 1, p.to(i=j), p.line(j=i, k=k)
        else:
            n, m, base, h, t, d = p.nb, p.na, self.i2b, 0, p.to(j=j), p.line(i=i, k=k)
        return self.copy(self.src(d, h, k == 0 and i == 0), self.part(d, h), base + (k * m + i) * (n - 1) + j - 1, t)

    def r_2(self, axis, k, i, j):
        p = self.p
        if axis == "a":
            n, m, base, h, t, d = p.na, p.nb, self.i2a, 1, p.to(i=j), p.line(i=j, j=i, k=k)
        else:
            n, m, base, h, t, d = p.nb, p.na, self.i2b, 0, p.to(j=j), p.line(i=i, j=j, k=k)
        return self.copy(self.part(d, h), self.part(d, h), base + (k * m + i) * (n - 1) + j - 1, t)

    def m_s(self, k, i, j):
        p = self.p
        d = p.line(i=i, j=j, k=k)
        own = k == 0 and i == 0 and j == 0
        return self.copy(self.x if own else self.o.at[d], self.o.at[d], self.isib + (k * p.na + i) * p.nb + j, p.to(s=1))

    def r_s(self, k, i, j):
        p = self.p
        d = p.line(i=i, j=j, k=k, s=1)
        return self.copy(self.o.at[d], self.o.at[d], self.isib + (k * p.na + i) * p.nb + j, p.to(s=1))

    def own(self):
        return pltpu.make_async_copy(self.x, self.o.at[self.p.line()], self.local)

    def begin(self):
        self.own().start()
        self.spread(0)

    def launch(self, k):
        self.m_z(k).start()

    def spread(self, k):
        p = self.p
        for j in self.a1:
            self.m_1("a", k, j).start()
        for j in self.b1:
            self.m_1("b", k, j).start()
        for j in self.b2:
            self.m_2("b", k, 0, j).start()
        for j in self.a2:
            self.m_2("a", k, 0, j).start()
        self.m_s(k, 0, 0).start()

    def turn(self, k):
        p = self.p
        for i in self.a1:
            self.r_1("a", k, i).wait_recv()
            for j in self.b2:
                self.m_2("b", k, i, j).start()
        for i in self.b1:
            self.r_1("b", k, i).wait_recv()
            for j in self.a2:
                self.m_2("a", k, i, j).start()

    def close(self, k):
        p = self.p
        for i in range(p.na):
            for j in self.b2:
                self.r_2("b", k, i, j).wait_recv()
        for i in range(p.nb):
            for j in self.a2:
                self.r_2("a", k, i, j).wait_recv()
        for i in range(p.na):
            for j in range(p.nb):
                if i or j:
                    self.m_s(k, i, j).start()

    def receive(self, k):
        self.r_z(k).wait_recv()

    def arrive(self, k):
        self.receive(k)
        self.spread(k)

    def plane(self, k):
        for i in range(self.p.na):
            for j in range(self.p.nb):
                self.r_s(k, i, j).wait_recv()

    def settle(self, k):
        p = self.p
        self.settled.add(k)
        for i in range(p.na):
            for j in range(p.nb):
                self.m_s(k, i, j).wait_send()
        for j in self.a1:
            self.m_1("a", k, j).wait_send()
        for j in self.b1:
            self.m_1("b", k, j).wait_send()
        for j in self.a2:
            for i in range(p.nb):
                self.m_2("a", k, i, j).wait_send()
        for j in self.b2:
            for i in range(p.na):
                self.m_2("b", k, i, j).wait_send()

    def finish(self, planes, far):
        for k in planes:
            if k not in self.settled:
                self.settle(k)
        for k in far:
            self.m_z(k).wait_send()

OUTS = 4


def rs_layout(shape, rows):
    na, nb, nz = shape
    cut = rows // 32 * 16
    s0, s1 = cut, rows - cut
    counts = [na * nb * nz, (nb - 1) * na * nz, (na - 1) * nb * nz, (na - 1) * nz, (nb - 1) * nz, 2 * (nz - 1)]
    buffers = [
        (na, nb, nz, rows),
        (nb - 1, na, nz, s0),
        (na - 1, nb, nz, s1),
        (na - 1, nz, s0),
        (nb - 1, nz, s1),
        (nz - 1, rows),
    ]
    return counts, buffers


class Scatter:
    def __init__(self, p, v, out, buffers, send, recv, base=0, rows=None):
        self.p, self.v, self.out, self.send, self.recv = p, v, out, send, recv
        self.r1, self.r2b, self.r2a, self.r3a, self.r3b, self.r4 = buffers
        rows = out.shape[0] if rows is None else rows
        cut = rows // 32 * 16
        self.rows = rows
        self.halves = ((0, cut), (cut, rows - cut))
        counts, _ = rs_layout((p.na, p.nb, p.nz), rows)
        self.starts = []
        for n in counts:
            self.starts.append(base)
            base += n
        self.end = base
        self.waited = set()

    def copy(self, src, dst, i, target):
        return pltpu.make_async_remote_copy(src_ref=src, dst_ref=dst, send_sem=self.send.at[i], recv_sem=self.recv.at[i], device_id=target, device_id_type=MESH)

    def block(self, i, j, k, s=0):
        p = self.p
        if len(self.v.shape) == 5:
            return self.v.at[i, j, k]
        return self.v.at[p.line(i, j, k, s), pl.ds(0, self.rows)]

    def half(self, ref, h):
        s, n = self.halves[h]
        return ref.at[pl.ds(s, n)]

    def sibling(self, i, j, k):
        p = self.p
        n = self.starts[0] + (i * p.nb + j) * p.nz + k
        return self.copy(self.block(i, j, k, 1), self.r1.at[i, j, k], n, p.to(s=1))

    def arrived(self, key, ref, i):
        if key in self.waited:
            return None
        self.waited.add(key)
        p = self.p
        return self.copy(ref, ref, i, p.to(s=1))

    def base_inputs(self, i, j, k, h):
        p = self.p
        n = self.starts[0] + (i * p.nb + j) * p.nz + k
        r = self.r1.at[i, j, k]
        return [(self.half(self.block(i, j, k), h), None), (self.half(r, h), self.arrived((1, i, j, k), r, n))]

    def two(self, h, far, near, k):
        p = self.p
        if h == 0:
            r, n = self.r2b.at[far - 1, near, k], self.starts[1] + ((far - 1) * p.na + near) * p.nz + k
        else:
            r, n = self.r2a.at[far - 1, near, k], self.starts[2] + ((far - 1) * p.nb + near) * p.nz + k
        return r, n

    def three(self, h, far, k):
        p = self.p
        if h == 0:
            return self.r3a.at[far - 1, k], self.starts[3] + (far - 1) * p.nz + k
        return self.r3b.at[far - 1, k], self.starts[4] + (far - 1) * p.nz + k

    def four(self, h, k):
        return self.half(self.r4.at[k - 1], h), self.starts[5] + 2 * (k - 1) + h

    def stage2(self, k):
        p, jobs = self.p, []
        for far, near in [(f, n) for n in range(max(p.na, p.nb)) for f in range(1, max(p.na, p.nb))]:
            if far < p.nb and near < p.na:
                r, n = self.two(0, far, near, k)
                own = self.half(self.r1.at[near, far, k], 0)
                jobs.append((self.base_inputs(near, far, k, 0), (own, r, n, p.to(j=far))))
            if far < p.na and near < p.nb:
                r, n = self.two(1, far, near, k)
                own = self.half(self.r1.at[far, near, k], 1)
                jobs.append((self.base_inputs(far, near, k, 1), (own, r, n, p.to(i=far))))
        return jobs

    def with_two(self, h, near, k):
        p = self.p
        i, j = (near, 0) if h == 0 else (0, near)
        got = self.base_inputs(i, j, k, h)
        for far in range(1, p.nb if h == 0 else p.na):
            r, n = self.two(h, far, near, k)
            got.append((r, self.arrived((2, h, far, near, k), r, n)))
        return got

    def stage3(self, k):
        p, jobs = self.p, []
        for near in range(1, max(p.na, p.nb)):
            if near < p.na:
                r, n = self.three(0, near, k)
                own = self.half(self.r1.at[near, 0, k], 0)
                jobs.append((self.with_two(0, near, k), (own, r, n, p.to(i=near))))
            if near < p.nb:
                r, n = self.three(1, near, k)
                own = self.half(self.r1.at[0, near, k], 1)
                jobs.append((self.with_two(1, near, k), (own, r, n, p.to(j=near))))
        return jobs

    def with_three(self, h, k):
        p = self.p
        got = self.with_two(h, 0, k)
        for far in range(1, p.na if h == 0 else p.nb):
            r, n = self.three(h, far, k)
            got.append((r, self.arrived((3, h, far, k), r, n)))
        return got

    def stage4(self, k, last):
        p, jobs = self.p, []
        if last != (k == 0):
            return jobs
        for h in range(2):
            got = self.with_three(h, k)
            if k:
                r, n = self.four(h, k)
                own = self.half(self.r1.at[0, 0, k], h)
                jobs.append((got, (own, r, n, p.to(k=k))))
            else:
                for far in range(1, p.nz):
                    r, n = self.four(h, far)
                    got.append((r, self.arrived((4, h, far), r, n)))
                jobs.append((got, self.half(self.out, h)))
        return jobs

    def start(self, k):
        p = self.p
        for i in reversed(range(p.na)):
            for j in reversed(range(p.nb)):
                self.sibling(i, j, k).start()

    def finish(self, k):
        p = self.p
        for i in range(p.na):
            for j in range(p.nb):
                self.sibling(i, j, k).wait_send()


class Worker:
    def __init__(self, ins, outbuf, finbuf, load, put, fin, send, recv):
        self.ins, self.outbuf, self.finbuf = ins, outbuf, finbuf
        self.load, self.put, self.fin, self.send, self.recv = load, put, fin, send, recv
        self.room = outbuf.shape[1]
        self.jobs, self.loaded, self.ran = [], 0, 0
        self.puts, self.n_out = [], 0
        self.sends = []

    def add(self, jobs):
        self.jobs.extend(jobs)

    def place(self, j, n, rows):
        return self.ins[j % 2].at[pl.ds(n * self.room, rows)]

    def loading(self, j, n):
        ref, _ = self.jobs[j][0][n]
        return pltpu.make_async_copy(ref, self.place(j, n, ref.shape[0]), self.load.at[j % 2, n])

    def fetch(self, j):
        inputs, _ = self.jobs[j]
        for n, (ref, arrived) in enumerate(inputs):
            if arrived is not None:
                if n > 1:
                    self.forward(0)
                arrived.wait_recv()
            self.loading(j, n).start()
        self.loaded = j + 1

    def forward(self, left):
        while len(self.puts) > left:
            put, out = self.puts.pop(0)
            put.wait()
            self.sending(out).start()
            self.sends.append(out)

    def sending(self, out):
        own, r, n, where = out
        return pltpu.make_async_remote_copy(
            src_ref=own,
            dst_ref=r,
            send_sem=self.send.at[n],
            recv_sem=self.recv.at[n],
            device_id=where,
            device_id_type=MESH,
        )

    def run(self, j):
        inputs, out = self.jobs[j]
        rows = inputs[0][0].shape[0]
        for n in range(len(inputs)):
            self.loading(j, n).wait()
        final = not isinstance(out, tuple)
        if final:
            target = self.finbuf
        else:
            self.forward(OUTS - 1)
            s = self.n_out % OUTS
            self.n_out += 1
            target = self.outbuf.at[s]
        source, count, room = self.ins[j % 2], len(inputs), self.room

        def body(t, carry):
            acc = source[pl.ds(pl.multiple_of(t * 16, 16), 16)].astype(jnp.float32)
            for n in range(1, count):
                at = pl.ds(pl.multiple_of(n * room + t * 16, 16), 16)
                acc = acc + source[at].astype(jnp.float32)
            target[pl.ds(pl.multiple_of(t * 16, 16), 16)] = acc.astype(target.dtype)
            return carry

        lax.fori_loop(0, rows // 16, body, 0)
        if final:
            c = pltpu.make_async_copy(target.at[pl.ds(0, rows)], out, self.fin.at[0])
            c.start()
            c.wait()
        else:
            c = pltpu.make_async_copy(target.at[pl.ds(0, rows)], out[0], self.put.at[s])
            c.start()
            self.puts.append((c, out))
            self.forward(1)

    def drain(self):
        for j in range(self.ran, len(self.jobs)):
            if self.loaded <= j:
                self.fetch(j)
            if j + 1 < len(self.jobs):
                self.fetch(j + 1)
            self.run(j)
            self.ran = j + 1
        self.forward(0)

    def finish(self):
        for out in self.sends:
            self.sending(out).wait_send()

CHUNK = 512
CAP = 32


def experts_kernel(shape, local, *refs):
    na, nb, nz = shape
    x, small, grad, _, place, choice_t, wg_hbm, wu_hbm, wd_hbm = refs[:9]
    dx_sum, y_part, xs_out, gs_out, hs_out, gu_out = refs[9:15]
    x_all, small_all, dx_part = refs[15:18]
    dx_bufs = refs[18:24]
    (wg, wu, wd, xs, gs, xin, gin, pin, sin, cin, ybuf, dbuf, gate, score, hkeep, gkeep, inbuf, outbuf, finbuf) = refs[24:43]
    (wsem, insem, savesem, keepsem, ownsem, outsem, load, put, fin, ag_send, ag_recv, ag_local, rs_send, rs_recv) = refs[43:]
    g_all = y_part
    p = Place(shape)
    length, width = x.shape
    planes = na * nb * 2
    slots = CAP
    many = planes * slots
    first = lax.axis_index("exp") * local
    greet(p)
    weights = [pltpu.make_async_copy(a, b, wsem.at[n]) for n, (a, b) in enumerate(((wg_hbm, wg), (wu_hbm, wu), (wd_hbm, wd)))]
    for w in weights:
        w.start()
    ga = Gather(p, x, x_all, ag_send, ag_recv, ag_local.at[0])
    gb = Gather(p, small, small_all, ag_send, ag_recv, ag_local.at[1], ga.end)
    gg = Gather(p, grad, g_all, ag_send, ag_recv, ag_local.at[2], gb.end)
    both, every = (gb, ga), (gb, ga, gg)
    sd = Scatter(p, dx_part, dx_sum, dx_bufs, rs_send, rs_recv)
    work = Worker((inbuf.at[0], inbuf.at[1]), outbuf, finbuf, load, put, fin, rs_send, rs_recv)
    order = [1, 2, 3, 0]

    def step(name, k, gathers=both):
        for g in gathers:
            getattr(g, name)(k)

    step("spread", 0)
    step("launch", 1)
    for g in every:
        g.own().start()
    step("turn", 0)
    step("arrive", 1)
    step("launch", 2)
    step("launch", 3)
    step("close", 0)
    step("turn", 1)
    step("close", 1)
    for g in every:
        g.own().wait()
    one = (gg,)
    hooks = {(t, n): [] for t in range(nz) for n in range(4)}
    hooks[0, 0] = [("arrive", 2, both)]
    hooks[0, 1] = [("turn", 2, both)]
    hooks[0, 2] = [("close", 2, both)]
    hooks[1, 0] = [("arrive", 3, both)]
    hooks[1, 1] = [("turn", 3, both)]
    hooks[1, 2] = [("close", 3, both), ("spread", 0, one)]
    hooks[2, 0] = [("turn", 0, one)]
    hooks[2, 2] = [("close", 0, one)]

    def device(r, k):
        return r * nz + p.zs[k]

    def spots(s):
        at = pin[s]
        slot = lax.broadcasted_iota(jnp.int32, (slots, length), 0)
        rows = [jnp.where(at[e : e + 1] == slot, 1.0, 0.0) for e in range(local)]
        return rows, jnp.concatenate(rows, axis=0).astype(jnp.bfloat16)

    def dispatch(k):
        def loads(r, s):
            d = device(r, k)
            pairs = (
                (x_all.at[d], xin),
                (g_all.at[d], gin),
                (place.at[d], pin),
                (small_all.at[d], sin),
                (choice_t.at[d], cin),
            )
            return [pltpu.make_async_copy(a, b.at[s], insem.at[s, n]) for n, (a, b) in enumerate(pairs)]

        def item(r, s):
            for c in loads(r, s):
                c.wait()
            masks, spot = spots(s)
            for n in range(0, width, CHUNK):
                for source, target in ((xin, xs), (gin, gs)):
                    rows = jnp.dot(spot, source[s, :, n : n + CHUNK], preferred_element_type=jnp.float32).astype(jnp.bfloat16)
                    for e in range(local):
                        at = pl.ds(pl.multiple_of(e * many + r * slots, slots), slots)
                        target[at, n : n + CHUNK] = rows[e * slots : (e + 1) * slots]
            chosen = cin[s]
            gates = sin[s].astype(jnp.float32)
            gates = gates[0:8, 0:length] + gates[8:16, 0:length]
            for e in range(local):
                weight = jnp.sum(jnp.where(chosen == first + e, gates, 0.0), axis=0, keepdims=True)
                value = jnp.sum(masks[e] * weight, axis=1, keepdims=True)
                gate[e, pl.ds(pl.multiple_of(r * slots, slots), slots)] = jnp.broadcast_to(value, (slots, 128))

        for c in loads(0, 0):
            c.start()

        def body(t, carry):
            for c in loads(2 * t + 1, 1):
                c.start()
            item(2 * t, 0)

            @pl.when(t < planes // 2 - 1)
            def _():
                for c in loads(2 * t + 2, 0):
                    c.start()

            item(2 * t + 1, 1)
            return carry

        lax.fori_loop(0, planes // 2, body, 0)

    def saves(k, e):
        at = pl.ds(pl.multiple_of(e * many, many), many)
        return [pltpu.make_async_copy(a.at[at], b.at[e, k], savesem.at[n, e]) for n, (a, b) in enumerate(((xs, xs_out), (gs, gs_out)))]

    def keeps(k, e, s):
        pairs = ((hkeep, hs_out), (gkeep, gu_out))
        return [pltpu.make_async_copy(a.at[s], b.at[e, k], keepsem.at[s, n]) for n, (a, b) in enumerate(pairs)]

    def expert(k, e, s):
        at = pl.ds(pl.multiple_of(e * many, many), many)
        rows = xs[at]
        gate_act = jnp.dot(rows, wg[e], preferred_element_type=jnp.float32)
        up_act = jnp.dot(rows, wu[e], preferred_element_type=jnp.float32)
        back = lax.dot_general(gs[at], wd[e], (((1,), (1,)), ((), ())), preferred_element_type=jnp.float32)
        weight = gate[e][:, 0:1]
        sig = jax.nn.sigmoid(gate_act)
        silu = gate_act * sig
        hidden = silu * up_act
        score[e] = jnp.broadcast_to(jnp.sum(hidden * back, axis=1, keepdims=True), (many, 128))
        grad = back * weight
        hs = (hidden * weight).astype(jnp.bfloat16)
        gu = (grad * silu).astype(jnp.bfloat16)
        gg = (grad * up_act * sig * (1.0 + gate_act * (1.0 - sig))).astype(jnp.bfloat16)
        hkeep[s] = hs
        gkeep[s] = jnp.concatenate([gg, gu], axis=1)
        for c in keeps(k, e, s):
            c.start()
        for c in saves(k, e):
            c.wait()
        for n in range(0, width, CHUNK):
            y = jnp.dot(hs, wd[e, :, n : n + CHUNK], preferred_element_type=jnp.float32)
            gs[at, n : n + CHUNK] = y.astype(jnp.bfloat16)
            form = (((1,), (1,)), ((), ()))
            dx = lax.dot_general(gg, wg[e, n : n + CHUNK], form, preferred_element_type=jnp.float32)
            dx = dx + lax.dot_general(gu, wu[e, n : n + CHUNK], form, preferred_element_type=jnp.float32)
            xs[at, n : n + CHUNK] = dx.astype(jnp.bfloat16)

    def experts(k, start, stop):
        def body(t, carry):
            for s in range(2):
                e = 2 * t + s

                @pl.when(e >= 2)
                def _():
                    for c in keeps(k, e - 2, s):
                        c.wait()

                expert(k, e, s)
            return carry

        if stop > start:
            lax.fori_loop(start // 2, stop // 2, body, 0)

    def combine(k):
        def at_offset(t, s):
            t = jnp.int32(t)
            i, j = lax.div(t, nb), lax.rem(t, nb)
            c = p.c if s else 1 - p.c
            return i, j, (xor_two(p.a, i, na) * nb + xor_two(p.b, j, nb)) * 2 + c

        def loads(t, s):
            r = at_offset(t, s)[2]
            d = device(r, k)
            return pltpu.make_async_copy(place.at[d], pin.at[s], insem.at[s, 0])

        def store_y(t, s):
            r = at_offset(t, s)[2]
            out = y_part.at[device(r, k)]
            return pltpu.make_async_copy(ybuf.at[s], out, ownsem.at[s])

        def store_dx(t, s):
            t = jnp.int32(t)
            i, j, _ = at_offset(t, s)
            if s:
                return pltpu.make_async_copy(dbuf.at[2], sd.block(i, j, k), outsem.at[0])
            n = sd.starts[0] + t * nz + k
            return sd.copy(dbuf.at[lax.rem(t, 2)], sd.r1.at[i, j, k], n, p.to(s=1))

        def item(t, s):
            r = at_offset(t, s)[2]
            loads(t, s).wait()

            @pl.when(t > 0)
            def _():
                store_y(t - 1, s).wait()
                if s:
                    store_dx(t - 1, s).wait()

            if not s:

                @pl.when(t > 1)
                def _():
                    store_dx(t - 2, s).wait_send()

            d = 2 if s else lax.rem(t, 2)
            masks, _ = spots(s)
            spot = jnp.concatenate(masks, axis=0).T.astype(jnp.bfloat16)
            for source, out in ((gs, ybuf.at[s]), (xs, dbuf.at[d])):
                for n in range(0, width, CHUNK):
                    rows = [
                        source[pl.ds(pl.multiple_of(e * many + r * slots, slots), slots), n : n + CHUNK]
                        for e in range(local)
                    ]
                    rows = jnp.concatenate(rows, axis=0)
                    total = jnp.dot(spot, rows, preferred_element_type=jnp.float32)
                    out[0:length, n : n + CHUNK] = total.astype(jnp.bfloat16)
            row = lax.broadcasted_iota(jnp.int32, (8, length), 0)
            table = jnp.zeros((8, length), jnp.float32)
            for e in range(local):
                value = score[e, pl.ds(pl.multiple_of(r * slots, slots), slots)][:, 0:1]
                line = jnp.sum(masks[e] * value, axis=0, keepdims=True)
                table = jnp.where(row == (first + e) % 8, line, table)
            table = jnp.concatenate([table, jnp.zeros((8, length), jnp.float32)], axis=0)
            table = jnp.concatenate([table, jnp.zeros((16, 256 - length), jnp.float32)], axis=1)
            dbuf[d, length : length + 16] = jnp.zeros((16, width), jnp.bfloat16)
            at = pl.ds(pl.multiple_of(first // 8 * 256, 256), 256)
            dbuf[d, length : length + 16, at] = table.astype(jnp.bfloat16)
            store_y(t, s).start()
            store_dx(t, s).start()

        loads(0, 0).start()

        def body(t, carry):
            loads(t, 1).start()
            item(t, 0)

            @pl.when(t < na * nb - 1)
            def _():
                loads(t + 1, 0).start()

            item(t, 1)
            return carry

        lax.fori_loop(0, na * nb, body, 0)
        last = na * nb - 1
        for s in range(2):
            store_y(last, s).wait()
        store_dx(last, 1).wait()
        for t in range(max(0, last - 1), last + 1):
            store_dx(t, 0).wait_send()

    def add(jobs):
        work.add(jobs)
        work.drain()

    for t, k in enumerate(order):
        for g in every if k == 0 else both:
            g.plane(k)
        dispatch(k)
        for e in range(local):
            for c in saves(k, e):
                c.start()
        for h in hooks[t, 0]:
            step(*h)
        if t == 0:
            for w in weights:
                w.wait()
        half = local // 4 * 2
        experts(k, 0, half)
        for h in hooks[t, 1]:
            step(*h)
        if t:
            add(sd.stage3(order[t - 1]))
        experts(k, half, local)
        for h in hooks[t, 2]:
            step(*h)
        for s in range(2):
            for c in keeps(k, local - 2 + s, s):
                c.wait()
        jobs = sd.stage4(order[t - 1], False) if t else []
        if k == 0:
            gg.settle(k)
            add(jobs)
            jobs = []
        combine(k)
        add(jobs + sd.stage2(k))
        for h in hooks[t, 3]:
            step(*h)
    add(sd.stage3(order[-1]))
    add(sd.stage4(order[-1], False))
    add(sd.stage4(0, True))
    work.finish()
    for g in both:
        g.finish(range(nz), range(1, nz))
    gg.finish((0,), ())


def run_experts(shape, x, small, grad, g_all, place, choice_t, wg, wu, wd, collective_id):
    na, nb, nz = shape
    local, width, hidden = wg.shape
    length = x.shape[0]
    planes = na * nb * 2
    many = planes * CAP
    tall = length + 16
    low, wide = jnp.bfloat16, jnp.float32
    any_ = pl.BlockSpec(memory_space=pl.ANY)
    sds = jax.ShapeDtypeStruct
    outs = [sds((tall, width), wide), sds(g_all.shape, low)]
    outs += [sds((local, nz, many, width), low)] * 2 + [sds((local, nz, many, n * hidden), low) for n in (1, 2)]
    outs += [sds((g_all.shape[0],) + x.shape, low), sds((g_all.shape[0],) + small.shape, low)]
    outs += [sds((na, nb, nz, tall, width), low)]
    counts, buffers = rs_layout(shape, tall)
    total = sum(counts)
    outs += [sds(b + (width,), low) for b in buffers]
    messages = 3 * ag_count(shape)
    room = tall - tall // 32 * 16
    inputs = na + nb + nz - 1
    dma = pltpu.SemaphoreType.DMA
    got = pl.pallas_call(
        functools.partial(experts_kernel, shape, local),
        out_shape=outs,
        in_specs=[any_] * 9,
        out_specs=[any_] * len(outs),
        input_output_aliases={3: 1},
        scratch_shapes=[
            pltpu.VMEM((local, width, hidden), low),
            pltpu.VMEM((local, width, hidden), low),
            pltpu.VMEM((local, hidden, width), low),
            pltpu.VMEM((local * many, width), low),
            pltpu.VMEM((local * many, width), low),
            pltpu.VMEM((2, length, width), low),
            pltpu.VMEM((2, length, width), low),
            pltpu.VMEM((2,) + place.shape[1:], jnp.int32),
            pltpu.VMEM((2,) + small.shape, low),
            pltpu.VMEM((2,) + choice_t.shape[1:], jnp.int32),
            pltpu.VMEM((2, length, width), low),
            pltpu.VMEM((3, tall, width), low),
            pltpu.VMEM((local, many, 128), wide),
            pltpu.VMEM((local, many, 128), wide),
            pltpu.VMEM((2, many, hidden), low),
            pltpu.VMEM((2, many, 2 * hidden), low),
            pltpu.VMEM((2, inputs * room, width), low),
            pltpu.VMEM((OUTS, room, width), low),
            pltpu.VMEM((room, width), wide),
            dma((3,)),
            dma((2, 5)),
            dma((2, local)),
            dma((2, 2)),
            dma((2,)),
            dma((2,)),
            dma((2, inputs)),
            dma((OUTS,)),
            dma((1,)),
            dma((messages,)),
            dma((messages,)),
            dma((3,)),
            dma((total,)),
            dma((total,)),
        ],
        compiler_params=pltpu.CompilerParams(
            collective_id=collective_id, has_side_effects=True, vmem_limit_bytes=63 << 20
        ),
    )(x, small, grad, g_all, place, choice_t, wg, wu, wd)
    return got[:6]

HEADS = 16
HEAD_DIM = 128
EXPERTS = 64
epsilon = 1e-05
masked_value = -1e30
low = jnp.bfloat16
wide = jnp.float32
ROWS_OUT = (((1,), (1,)), ((), ()))


def factor_of(values):
    return lax.rsqrt(jnp.mean(values * values, axis=-1, keepdims=True) + epsilon)


def swapped(v):
    half = v.shape[1] // 2
    return jnp.concatenate([v[:, half:], v[:, :half]], axis=1)


def front_kernel(shape, local_experts, *refs):
    na, nb, nz = shape
    tokens, allowed, cosine, sine, choice = refs[:5]
    shards = refs[5:12]
    alls = refs[12:19]
    places, choices, normed_f, normed_ft, normed_at, attended_t, gates, residual, q_raw, k_raw, q_low, k_low, v_low, probs, router_p, gains = refs[19:35]
    wq, wk, wv, wo, router, smalls, normed, attended, wsem, send, recv, local = refs[35:]
    p = Place(shape)
    length, width = tokens.shape
    greet(p)
    gs, base = [], 0
    for i in range(7):
        g = Gather(p, shards[i], alls[i], send, recv, local.at[i], base)
        base = g.end
        gs.append(g)
    weights, late = gs[:6], gs[6]

    def begin(g):
        g.begin()
        for k in range(1, nz):
            g.launch(k)

    for g in weights:
        begin(g)
    for k in range(1, nz):
        for g in weights:
            g.arrive(k)
            g.turn(k - 1)
        if k > 1:
            for g in weights:
                g.close(k - 2)
    planes = (1, 2, 3)
    for k in range(1, nz):
        late.launch(k)
    for g in weights:
        g.turn(nz - 1)
    for k in planes[:2]:
        late.arrive(k)
    for k in range(nz - 2, nz):
        for g in weights:
            g.close(k)
    copies = []
    for n, (g, target) in enumerate(zip(weights, (smalls, router, wq, wk, wv, wo))):
        g.own().wait()
        for k in range(nz):
            g.plane(k)
        c = pltpu.make_async_copy(alls[n], target, wsem.at[n])
        c.start()
        copies.append(c)

    copies[0].wait()
    devices = smalls.shape[0]

    def total(d, carry):
        gains[...] += smalls[d].astype(wide)
        return carry

    gains[...] = jnp.zeros((16, width), wide)
    lax.fori_loop(0, devices, total, 0)
    x = tokens[...].astype(wide)
    scaled = x * factor_of(x) * gains[0:1]
    normed[...] = scaled.astype(low)

    def transposed(source, target):
        def body(n, carry):
            at = pl.ds(pl.multiple_of(n * 256, 256), 256)
            target[at] = source[:, at].astype(wide).T.astype(low)
            return carry

        lax.fori_loop(0, width // 256, body, 0)

    def product(left, right, out, more=None):
        def body(n, carry):
            at = pl.ds(pl.multiple_of(n * 512, 512), 512)
            got = jnp.dot(left[...], right[:, :, at].reshape(width, 512), preferred_element_type=wide)
            if more is not None:
                got = got + more[:, at].astype(wide)
            out[:, at] = got.astype(out.dtype)
            return carry

        lax.fori_loop(0, width // 512, body, 0)

    copies[2].wait()
    product(normed, wq, q_raw)
    copies[3].wait()
    product(normed, wk, k_raw)
    copies[4].wait()
    product(normed, wv, v_low)
    for k in planes[:1]:
        late.turn(k)
    transposed(normed, normed_at)
    factor_q = factor_of(q_raw[...])
    factor_k = factor_of(k_raw[...])

    def head(h, carry):
        at = pl.ds(pl.multiple_of(h * HEAD_DIM, HEAD_DIM), HEAD_DIM)

        def turned(raw, factor, gain):
            v = raw[:, at] * factor * gain[:, at]
            return (v * cosine[...] + swapped(v) * sine[...]).astype(low)

        q = turned(q_raw, factor_q, gains.at[1:2])
        k = turned(k_raw, factor_k, gains.at[2:3])
        q_low[:, at] = q
        k_low[:, at] = k
        scores = lax.dot_general(q, k, ROWS_OUT, preferred_element_type=wide) * HEAD_DIM ** (-0.5)
        scores = jnp.where(allowed[...] > 0.0, scores, masked_value)
        e = jnp.exp(scores - jnp.max(scores, axis=-1, keepdims=True))
        e = e / jnp.sum(e, axis=-1, keepdims=True)
        probs[h] = e
        out = jnp.dot(e.astype(low), v_low[:, at], preferred_element_type=wide)
        attended[:, at] = out.astype(low)
        return carry

    lax.fori_loop(0, HEADS, head, 0)
    late.turn(planes[1])
    late.close(planes[0])
    late.arrive(planes[2])
    copies[5].wait()
    product(attended, wo, residual, tokens)
    r = residual[...]
    normed_f[...] = (r * factor_of(r) * gains[3:4]).astype(low)
    copies[1].wait()
    logits = jnp.dot(normed_f[...], router[...].reshape(width, 128), preferred_element_type=wide)
    logits = logits.T[0:EXPERTS]
    e = jnp.exp(logits - jnp.max(logits, axis=0, keepdims=True))
    chances = e / jnp.sum(e, axis=0, keepdims=True)
    router_p[...] = chances
    expert = lax.broadcasted_iota(jnp.int32, (EXPERTS, length), 0)
    rows = [
        jnp.sum(jnp.where(expert == choice[n : n + 1], chances, 0.0), axis=0, keepdims=True)
        for n in range(choice.shape[0])
    ]
    rows = jnp.concatenate(rows, axis=0)
    upper = rows.astype(low).astype(wide)
    rows = jnp.concatenate([upper, rows - upper], axis=0)
    rows = jnp.concatenate([rows, jnp.zeros((16, gates.shape[1] - length), wide)], axis=1)
    gates[...] = rows.astype(low)
    late.close(planes[1])
    late.turn(planes[2])
    first = lax.axis_index("exp") * local_experts
    order = lax.broadcasted_iota(jnp.int32, (length, length), 0)
    before = jnp.where(order < lax.broadcasted_iota(jnp.int32, (length, length), 1), 1.0, 0.0)
    before = before.astype(low)

    def slots(d, carry):
        named = smalls[d].astype(wide)[8:16, 0:length].astype(jnp.int32)
        choices[d] = named
        rows = [
            jnp.max(jnp.where(named == first + e, 1.0, 0.0), axis=0, keepdims=True)
            for e in range(local_experts)
        ]
        rows = jnp.concatenate(rows + [jnp.zeros((16 - local_experts, length), wide)], axis=0)
        ranks = jnp.dot(rows.astype(low), before, preferred_element_type=wide)
        ranks = jnp.where(rows > 0.0, ranks, -1.0).astype(jnp.int32)
        places[d] = ranks[0:local_experts]
        return carry

    lax.fori_loop(0, devices, slots, 0)
    transposed(attended, attended_t)
    transposed(normed_f, normed_ft)
    late.close(planes[2])
    for k in planes:
        late.plane(k)
    for g in weights:
        g.finish(range(nz), range(1, nz))
    late.finish(planes, range(1, nz))


def run_front(shape, tokens, allowed, cosine, sine, choice, shards, local_experts, collective_id):
    na, nb, nz = shape
    length, width = tokens.shape
    devices = na * nb * nz * 2
    any_, vmem = pl.BlockSpec(memory_space=pl.ANY), pl.BlockSpec(memory_space=pltpu.VMEM)
    sds = jax.ShapeDtypeStruct
    alls = [sds((devices,) + s.shape, low) for s in shards]
    row, tall = (length, width), (width, length)
    outs = [sds((devices, local_experts, length), jnp.int32), sds((devices, 8, length), jnp.int32)]
    outs += [sds(row, low), sds(tall, low), sds(tall, low), sds(tall, low)]
    outs += [sds((16, -length % 256 + length), low), sds(row, wide), sds(row, wide), sds(row, wide)]
    outs += [sds(row, low), sds(row, low), sds(row, low), sds((HEADS, length, length), wide)]
    outs += [sds((EXPERTS, length), wide), sds((16, width), wide)]
    count = ag_count(shape) * len(shards)
    got = pl.pallas_call(
        functools.partial(front_kernel, shape, local_experts),
        out_shape=alls + outs,
        in_specs=[vmem] * 5 + [any_] * 7,
        out_specs=[any_] * 7 + [vmem] * len(outs),
        scratch_shapes=[pltpu.VMEM(alls[n].shape, low) for n in (2, 3, 4, 5, 1, 0)]
        + [
            pltpu.VMEM(row, low),
            pltpu.VMEM(row, low),
            pltpu.SemaphoreType.DMA((6,)),
            pltpu.SemaphoreType.DMA((count,)),
            pltpu.SemaphoreType.DMA((count,)),
            pltpu.SemaphoreType.DMA((7,)),
        ],
        compiler_params=pltpu.CompilerParams(
            collective_id=collective_id, has_side_effects=True, vmem_limit_bytes=63 << 20
        ),
    )(tokens, allowed, cosine, sine, choice, *shards)
    return got[:7], got[7:]


FIRST = (((0,), (0,)), ((), ()))


def last_kernel(shape, part, *refs):
    na, nb, nz = shape
    tokens, out_grad, residual, q_raw, k_raw, q_low, k_low, v_low = refs[:8]
    normed_at, attended_t, normed_ft, router, gains, router_p, dx_in, cosine, sine = refs[8:17]
    y_part, probs, wq, wk, wv, wo, xs, gs, hs, gu = refs[17:27]
    y_sum, w_sum, input_grad, dwg, dwu, dwd, w_part = refs[27:34]
    y_bufs, w_bufs = refs[34:40], refs[40:46]
    flat, xin, gin, hin, uin, outbuf, finbuf, grads = refs[46:54]
    wsem, psem, isem, outsem, insem, savesem, load, put, fin, send, recv = refs[54:]
    p = Place(shape)
    greet(p)
    length, width = y_sum.shape
    rows = 4 * part
    tall = rows + 16
    sy = Scatter(p, y_part, y_sum, y_bufs, send, recv)
    sw = Scatter(p, w_part, w_sum, w_bufs, send, recv, sy.end)
    half = flat.shape[0] // 2
    ins = (flat.at[pl.ds(0, half)], flat.at[pl.ds(half, half)])
    work = Worker(ins, outbuf, finbuf, load, put, fin, send, recv)
    local, chunks = xs.shape[:2]
    hidden = hs.shape[3]
    order = [*reversed(range(nz))]

    def weight(source, target, n):
        return pltpu.make_async_copy(source, target, wsem.at[n])

    def back_product(left, matrix, out, kind):
        def body(n, carry):
            at = pl.ds(pl.multiple_of(n * 512, 512), 512)
            part_of = matrix[lax.div(n, 2), pl.ds(pl.multiple_of(lax.rem(n, 2) * 512, 512), 512)]
            got = lax.dot_general(left[...], part_of, ROWS_OUT, preferred_element_type=wide)
            if kind == "add":
                got = got + out[:, at]
            out[:, at] = got.astype(out.dtype)
            return carry

        lax.fori_loop(0, width // 512, body, 0)

    def norm_back(grad, unit, factor, gain):
        m = grad * gain
        return factor * (m - unit * jnp.mean(m * unit, axis=-1, keepdims=True))

    pieces = [(e, c) for e in range(local) for c in range(chunks)]

    def loads(n):
        e, c = pieces[n]
        pairs = ((xs, xin), (gs, gin), (hs, hin), (gu, uin))
        return [pltpu.make_async_copy(a.at[e, c], b.at[n % 2], insem.at[n % 2, m]) for m, (a, b) in enumerate(pairs)]

    def early(work_a, res_grad, k_grad, res_low, att_grad, dq, dk, dv, llow, pin):
        def back_ffn():
            weight(wo, xin, 0).start()
            weight(wv, gin, 1).start()
            wide_table = dx_in[length : length + 8]
            table = [wide_table[:, n * 256 : n * 256 + length] for n in range(EXPERTS // 8)]
            table = jnp.concatenate(table, axis=0)
            chances = router_p[...]
            grad = chances * (table - jnp.sum(chances * table, axis=0, keepdims=True))
            grad = jnp.concatenate([grad, jnp.zeros((128 - EXPERTS, length), wide)], axis=0)
            llow[...] = grad.T.astype(low)
            for n in range(0, width, 512):
                got = lax.dot_general(
                    llow[...], router[n : n + 512], ROWS_OUT, preferred_element_type=wide
                )
                work_a[:, n : n + 512] = got + dx_in[0:length, n : n + 512]
            factor = factor_of(residual[...])
            unit = residual[...] * factor
            grad = work_a[...]
            grads[3:4] = jnp.sum(grad * unit, axis=0, keepdims=True)
            got = out_grad[...].astype(wide) + norm_back(grad, unit, factor, gains[3:4])
            res_grad[...] = got
            res_low[...] = got.astype(low)
            weight(wo, xin, 0).wait()
            back_product(res_low, xin, att_grad, "set")
            weight(wq, xin, 0).start()

        def back_heads():
            def prob(h, s):
                return pltpu.make_async_copy(probs.at[h], pin.at[s], psem.at[s])

            prob(0, 0).start()

            def one(h, s):
                @pl.when(h + 1 < HEADS)
                def _():
                    prob(h + 1, 1 - s).start()

                prob(h, s).wait()
                at = pl.ds(pl.multiple_of(h * HEAD_DIM, HEAD_DIM), HEAD_DIM)
                grad, q, k, v = att_grad[:, at], q_low[:, at], k_low[:, at], v_low[:, at]
                chances = pin[s]
                got = lax.dot_general(chances.astype(low), grad, FIRST, preferred_element_type=wide)
                dv[:, at] = got.astype(low)
                inner = lax.dot_general(grad, v, ROWS_OUT, preferred_element_type=wide)
                inner = chances * (inner - jnp.sum(chances * inner, axis=-1, keepdims=True))
                inner = inner.astype(low)
                scale = HEAD_DIM ** (-0.5)

                def turned_back(x):
                    return x * cosine[...] - swapped(x) * sine[...]

                got = jnp.dot(inner, k, preferred_element_type=wide) * scale
                work_a[:, at] = turned_back(got)
                got = lax.dot_general(inner, q, FIRST, preferred_element_type=wide) * scale
                k_grad[:, at] = turned_back(got)

            def body(t, carry):
                one(2 * t, 0)
                one(2 * t + 1, 1)
                return carry

            lax.fori_loop(0, HEADS // 2, body, 0)

        def back_inputs():
            for raw, grad, out, n in ((q_raw, work_a, dq, 1), (k_raw, k_grad, dk, 2)):
                factor = factor_of(raw[...])
                unit = raw[...] * factor
                grads[n : n + 1] = jnp.sum(grad[...] * unit, axis=0, keepdims=True)
                out[...] = norm_back(grad[...], unit, factor, gains[n : n + 1]).astype(low)
            weight(wv, gin, 1).wait()
            back_product(dv, gin, work_a, "set")
            weight(wk, gin, 1).start()
            weight(wq, xin, 0).wait()
            back_product(dq, xin, work_a, "add")
            weight(wk, gin, 1).wait()
            back_product(dk, gin, work_a, "add")
            x = tokens[...].astype(wide)
            factor = factor_of(x)
            unit = x * factor
            grad = work_a[...]
            grads[0:1] = jnp.sum(grad * unit, axis=0, keepdims=True)
            res_grad[...] = res_grad[...] + norm_back(grad, unit, factor, gains[0:1])
            c = pltpu.make_async_copy(res_grad, input_grad, isem.at[0])
            c.start()
            c.wait()
            for d in loads(0):
                d.start()

        def products():
            def start_of(s, z):
                return (s * nz + z) * tall

            def where(t, s):
                t = jnp.int32(t)
                i, j = lax.div(t, nb), lax.rem(t, nb)
                c = p.c if s else 1 - p.c
                return i, j, (xor_two(p.a, i, na) * nb + xor_two(p.b, j, nb)) * 2 + c

            def stores(t, s):
                i, j, _ = where(t, s)
                got = []
                for k in range(nz):
                    src = flat.at[pl.ds(pl.multiple_of(start_of(s, p.zs[k]), 16), tall)]
                    if s:
                        got.append(pltpu.make_async_copy(src, sw.block(i, j, k), outsem.at[k]))
                    else:
                        n = sw.starts[0] + t * nz + k
                        got.append(sw.copy(src, sw.r1.at[i, j, k], n, p.to(s=1)))
                return got

            def finish(t, s):
                for c in stores(t, s):
                    if s:
                        c.wait()
                    else:
                        c.wait_send()

            pairs = ((normed_at, dq), (normed_at, dk), (normed_at, dv), (attended_t, res_low))
            groups = part // 16

            def body(t, carry):
                for s in range(2):

                    @pl.when(t > 0)
                    def _():
                        finish(t - 1, s)

                    r = where(t, s)[2]
                    at = pl.ds(pl.multiple_of(r * nz * part, nz * part), nz * part)
                    for m, (left, right) in enumerate(pairs):
                        for n in range(0, width, 512):
                            got = jnp.dot(left[at], right[:, n : n + 512], preferred_element_type=wide)
                            got = got.astype(low)
                            for z in range(nz):
                                to = start_of(s, z) + m * part
                                flat[to : to + part, n : n + 512] = got[z * part : (z + 1) * part]
                    got = jnp.dot(normed_ft[at], llow[...], preferred_element_type=wide).astype(low)
                    for z in range(nz):
                        to = start_of(s, z) + rows
                        lanes = pl.ds(pl.multiple_of((r * nz + z) * part // 128 * 128, 128), 128)
                        gain = jnp.concatenate([grads[:, lanes], jnp.zeros((8, 128), wide)], axis=0)
                        flat[to : to + 16] = jnp.zeros((16, width), low)
                        for n in range(groups):
                            piece = got[z * part + n * 16 : z * part + (n + 1) * 16]
                            flat[to : to + 16, n * 128 : (n + 1) * 128] = piece
                        flat[to : to + 16, groups * 128 : (groups + 1) * 128] = gain.astype(low)
                    for c in stores(t, s):
                        c.start()
                return carry

            lax.fori_loop(0, na * nb, body, 0)
            for s in range(2):
                finish(na * nb - 1, s)

        steps_of = (back_ffn, back_heads, back_inputs, products)
        for kind, what in plan[:cut]:
            if kind == "add":
                add(what)
            else:
                steps_of[what]()

    def late(og, ou, od, accg, accd):
        def saves(e):
            s = e % og.shape[0]
            pairs = ((og, dwg), (ou, dwu), (od, dwd))
            return [pltpu.make_async_copy(a.at[s], b.at[e], savesem.at[s, m]) for m, (a, b) in enumerate(pairs)]

        def piece(n):
            e, c = pieces[n]
            s, o = n % 2, e % og.shape[0]
            if n + 1 < len(pieces):
                for d in loads(n + 1):
                    d.start()
            for d in loads(n):
                d.wait()
            if c == 0 and e >= og.shape[0]:
                for d in saves(e - og.shape[0]):
                    d.wait()
            form = (((0,), (0,)), ((), ()))

            def columns(t, carry):
                at = pl.ds(pl.multiple_of(t * 512, 512), 512)
                g = lax.dot_general(xin[s, :, at], uin[s], form, preferred_element_type=jnp.float32)
                d = lax.dot_general(hin[s], gin[s, :, at], form, preferred_element_type=jnp.float32)
                if c:
                    g = g + accg[at]
                    d = d + accd[:, at]
                if c + 1 < chunks:
                    accg[at] = g
                    accd[:, at] = d
                else:
                    og[o, at] = g[:, :hidden].astype(jnp.bfloat16)
                    ou[o, at] = g[:, hidden:].astype(jnp.bfloat16)
                    od[o, :, at] = d.astype(jnp.bfloat16)
                return carry

            lax.fori_loop(0, width // 512, columns, 0)
            if c + 1 == chunks:
                for d in saves(e):
                    d.start()

        for kind, what in plan[cut:]:
            if kind == "add":
                add(what)
            else:
                piece(what)
        for e in range(max(0, local - og.shape[0]), local):
            for d in saves(e):
                d.wait()

    def add(jobs):
        work.add(jobs)
        work.drain()

    grads[...] = jnp.zeros((8, width), wide)
    for k in order:
        sy.start(k)
    steps = [(s, k) for s in (sy, sw) for k in order]
    slow = 4
    plan, done, count, cut = [], 0, len(steps), 0
    for t in range(count + 2):
        if t < count:
            s, k = steps[t]
            plan.append(("add", s.stage2(k)))
        if t < slow:
            plan.append(("first", t))
            cut = len(plan)
        else:
            until = len(pieces) * (t - slow + 1) // (count - slow + 1) if t < count else len(pieces)
            while done < until:
                plan.append(("piece", done))
                done += 1
        jobs = []
        if t >= 2:
            s, k = steps[t - 2]
            jobs = s.stage4(k, False)
        if 1 <= t <= count:
            s, k = steps[t - 1]
            jobs = jobs + s.stage3(k)
        plan.append(("add", jobs))
        if t == nz + 2:
            plan.append(("add", sy.stage4(0, True)))
    plan.append(("add", sw.stage4(0, True)))
    row, vmem = (length, width), pltpu.VMEM
    pl.run_scoped(
        early,
        *[vmem(row, wide)] * 3,
        *[vmem(row, low)] * 5,
        vmem((length, 128), low),
        vmem((2,) + probs.shape[1:], wide),
    )
    several = chunks > 1
    slots = 1 if several else 2
    pl.run_scoped(
        late,
        vmem((slots, width, hidden), low),
        vmem((slots, width, hidden), low),
        vmem((slots, hidden, width), low),
        vmem((width if several else 8, 2 * hidden), wide),
        vmem((hidden if several else 8, width), wide),
    )
    work.finish()
    for k in order:
        sy.finish(k)


def run_last(shape, part, vmem_in, any_in, collective_id):
    na, nb, nz = shape
    length, width = vmem_in[0].shape
    y_part, probs, wq, wk, wv, wo, xs, gs, hs, gu = any_in
    tall = 4 * part + 16
    local, hidden = xs.shape[0], hs.shape[3]
    total_slots = xs.shape[1] * xs.shape[2]
    deep = width // 2
    xs, gs, hs, gu = (a.reshape(local, total_slots // deep, deep, a.shape[3]) for a in (xs, gs, hs, gu))
    wq, wk, wv, wo = (a.reshape(2, deep, width) for a in (wq, wk, wv, wo))
    any_, vmem = pl.BlockSpec(memory_space=pl.ANY), pl.BlockSpec(memory_space=pltpu.VMEM)
    sds = jax.ShapeDtypeStruct
    outs = [sds((length, width), wide), sds((tall, width), wide), sds((length, width), wide)]
    outs += [sds((local, width, hidden), low)] * 2 + [sds((local, hidden, width), low)]
    outs += [sds((na, nb, nz, tall, width), low)]
    y_counts, y_buffers = rs_layout(shape, length)
    w_counts, w_buffers = rs_layout(shape, tall)
    total = sum(y_counts) + sum(w_counts)
    outs += [sds(b + (width,), low) for b in y_buffers + w_buffers]
    room = max(tall - tall // 32 * 16, length - length // 32 * 16)
    inputs = na + nb + nz - 1
    dma = pltpu.SemaphoreType.DMA
    got = pl.pallas_call(
        functools.partial(last_kernel, shape, part),
        out_shape=outs,
        in_specs=[vmem] * len(vmem_in) + [any_] * len(any_in),
        out_specs=[any_] * len(outs),
        scratch_shapes=[
            pltpu.VMEM((2 * max(nz * tall, inputs * room), width), low),
            pltpu.VMEM((2, deep, width), low),
            pltpu.VMEM((2, deep, width), low),
            pltpu.VMEM((2, deep, hidden), low),
            pltpu.VMEM((2, deep, 2 * hidden), low),
            pltpu.VMEM((OUTS, room, width), low),
            pltpu.VMEM((room, width), wide),
            pltpu.VMEM((8, width), wide),
            dma((2,)),
            dma((2,)),
            dma((1,)),
            dma((nz,)),
            dma((2, 4)),
            dma((2, 3)),
            dma((2, inputs)),
            dma((OUTS,)),
            dma((1,)),
            dma((total,)),
            dma((total,)),
        ],
        compiler_params=pltpu.CompilerParams(
            collective_id=collective_id, has_side_effects=True, vmem_limit_bytes=63 << 20
        ),
    )(*vmem_in, y_part, probs, wq, wk, wv, wo, xs, gs, hs, gu)
    return got[:6]


def widen_kernel(*refs):
    half = len(refs) // 2
    for source, target in zip(refs[:half], refs[half:]):
        target[...] = source[...].astype(wide)


def widen(arrays):
    local = arrays[0].shape[0]
    specs = [
        pl.BlockSpec((1, a.shape[1] // 2, a.shape[2]), lambda e, n: (e, n, 0)) for a in arrays
    ]
    return pl.pallas_call(
        widen_kernel,
        grid=(local, 2),
        out_shape=[jax.ShapeDtypeStruct(a.shape, wide) for a in arrays],
        in_specs=specs,
        out_specs=specs,
        compiler_params=pltpu.CompilerParams(vmem_limit_bytes=32 << 20),
    )(*arrays)

TOP = 8

base_freq = 10000.0


def rotary(length, head_width):
    positions = jnp.arange(length, dtype=jnp.float32)
    freqs = base_freq ** (-jnp.arange(head_width // 2, dtype=jnp.float32) * 2.0 / head_width)
    angles = positions[:, None] * freqs[None, :]
    return (jnp.cos(angles), jnp.sin(angles))


def on_device(
    shape,
    tokens,
    segment_ids,
    expert_choice,
    w_query,
    w_key,
    w_value,
    w_output,
    w_router,
    attn_gain,
    query_gain,
    key_gain,
    ffn_gain,
    w_gate,
    w_up,
    w_down,
    out_grad,
):
    length, width = tokens.shape
    part = w_query.shape[0]
    devices = width // part

    place = (lax.axis_index("exp") * lax.axis_size("hid") + lax.axis_index("hid")) * part
    small = jnp.stack([attn_gain, query_gain, key_gain, ffn_gain])
    small = lax.dynamic_update_slice(jnp.zeros((16, width), low), small, (0, place))
    listing = expert_choice.T
    small = lax.dynamic_update_slice(small, listing.astype(low), (8, 0))
    router = jnp.pad(w_router, ((0, 0), (0, 128 - EXPERTS)))
    positions = jnp.arange(length)
    segment_row = segment_ids[0]
    allowed = (positions[:, None] >= positions[None, :]) & (
        segment_row[:, None] == segment_row[None, :]
    )
    cosine, sine = rotary(length, HEAD_DIM)
    shards = [small, router, w_query, w_key, w_value, w_output, out_grad]
    alls, saved = run_front(
        shape,
        tokens,
        allowed.astype(wide),
        jnp.concatenate([cosine, cosine], axis=1),
        jnp.concatenate([-sine, sine], axis=1),
        listing,
        shards,
        w_gate.shape[0],
        1,
    )
    _, router_all, query_all, key_all, value_all, output_all, g_all = alls
    places, choices, normed_ffn, normed_ft, normed_at, attended_t, gates = saved[:7]
    residual, query_raw, key_raw, query_low, key_low, value_low, attn_probs, router_pt, gains = saved[7:]
    total_counts = jnp.sum(
        (choices.reshape(devices, -1)[:, None, :] == jnp.arange(EXPERTS)[:, None]).astype(jnp.int32),
        axis=2,
    )
    dx_sum, y_part, xs, gs, hs, gu = run_experts(
        shape,
        normed_ffn,
        gates,
        out_grad,
        g_all,
        places,
        choices,
        w_gate,
        w_up,
        w_down,
        2,
    )
    vmem_in = [
        tokens,
        out_grad,
        residual,
        query_raw,
        key_raw,
        query_low,
        key_low,
        value_low,
        normed_at,
        attended_t,
        normed_ft,
        router_all.reshape(width, -1),
        gains,
        router_pt,
        dx_sum,
        jnp.concatenate([cosine, cosine], axis=1),
        jnp.concatenate([-sine, sine], axis=1),
    ]
    any_in = [y_part, attn_probs, query_all, key_all, value_all, output_all, xs, gs, hs, gu]
    mixture, sums, input_grad, grad_wgate, grad_wup, grad_wdown = run_last(
        shape, part, vmem_in, any_in, 3
    )
    result = (residual + mixture).astype(low)
    small = sums[4 * part :]
    sums = sums[: 4 * part].reshape(4, part, width)
    lanes = part // 16 * 128
    sum_router = small[:, :lanes].reshape(16, -1, 128)[:, :, :EXPERTS].transpose(1, 0, 2)
    sum_router = sum_router.reshape(part, EXPERTS)
    sum_gains = lax.dynamic_slice(small, (0, lanes + place % 128), (4, part))
    return (
        result,
        input_grad,
        sums[0],
        sums[1],
        sums[2],
        sums[3],
        sum_router,
        sum_gains[0],
        sum_gains[1],
        sum_gains[2],
        sum_gains[3],
        *widen([grad_wgate, grad_wup, grad_wdown]),
        total_counts,
    )


def solution(mesh):
    rows, both = P(("exp", "hid"), None), P(("exp", "hid"))
    shape = grid_of(mesh.shape["exp"], mesh.shape["hid"])
    experts = (P("exp", None, "hid"), P("exp", None, "hid"), P("exp", "hid", None))
    return jax.shard_map(
        functools.partial(on_device, shape),
        mesh=mesh,
        in_specs=(rows,) * 8 + (both,) * 4 + experts + (rows,),
        out_specs=(rows,) * 7 + (both,) * 4 + experts + (P(),),
        check_vma=False,
    )
```
